32 devices in a mesh: ia: 4 (over y, x), ja: 2 (over core), ka: 4 (over z).
Axes of the slice: x: 2, y: 2, z: 4, core: 2. Of those that a mesh axis runs over, the one named last changes fastest.
Arguments:
- observed: bfloat16 [4, 2, 20, 128, 32, 128], P('ia', 'ja', 'ka'), may hold values from -6 to 6
- weights: bfloat16 [4, 2, 20, 128, 32, 128], P('ia', 'ja', 'ka'), may hold values from 0 to 4, as said below
- coords: int32 [4, 2, 20, 3], P('ia', 'ja', 'ka'), may hold values from 0 to 31, as said below
- counts: int32 [4, 2, 4], P('ia', 'ja', 'ka'), may hold values from 0 to 5, as said below
- factor_rows: bfloat16 [64, 4096], P(None, ('ia', 'ja', 'ka')), may hold values from -0.75 to 0.75
- factor_cols: bfloat16 [64, 1024], P(None, ('ja', 'ka')), may hold values from -0.75 to 0.75
- factor_depth: bfloat16 [64, 512], replicated, may hold values from -0.75 to 0.75
- core_tensor: bfloat16 [64, 64, 64], replicated, may hold values from -6 to 6
Outputs:
- rows_gradient: float32 [64, 4096], P(None, ('ia', 'ja', 'ka'))
- cols_gradient: float32 [64, 1024], P(None, ('ja', 'ka'))
- depth_gradient: float32 [64, 512], P(None, 'ka')
- core_gradient: float32 [64, 64, 64], replicated
The draws below stay inside these ranges and needn't reach their ends.
Inputs may be any that keep to these rules, and one draw needn't show every extreme that they name: counts[a, b, c] is the number of live slots of the device at index a of ia, b of ja, c of ka; the busiest devices hold 5. coords[a, b, c * 5 + s] = (p, q, t) with a * 8 <= p < (a + 1) * 8, b * 4 <= q < (b + 1) * 4, c * 4 <= t < (c + 1) * 4; the 5 slots of one device name distinct blocks. `weights`: zero at unobserved entries, positive at observed ones.
All inputs are finite; a program needn't handle non-finite values.
Results may differ from the reference program's by a relative error of at most 0.0012.
Values may be sent and summed in bfloat16 or wider, within the bound.
No kernel may reach another device: no remote copies, remote signals or barrier semaphores. Data moves between devices by JAX's collectives and lax.ppermute only.
A program may use at most 64 MiB of HBM per device.

```python
import math
import jax
import jax.numpy as jnp
from jax import lax

R = 64
BI = 128
BJ = 128
BK = 32
IB_DEV = 8
JB_DEV = 4
KB_DEV = 4
CAP = 5
I = 4096
J = 1024
K = 512
N_IA = 4
N_JA = 2
N_KA = 4


def draw_weights(key, part):
    full_shape = (N_IA, N_JA, N_KA * CAP, BI, BK, BJ)
    seen_key, level_key = jax.random.split(jax.random.fold_in(key, 7))
    seen_mask = jax.random.bernoulli(seen_key, 0.5, full_shape)
    level_value = jnp.exp(jax.random.uniform(level_key, full_shape, jnp.float32, math.log(0.25), math.log(4.0)))
    return jnp.where(seen_mask, level_value, 0.0).astype(jnp.bfloat16)


def draw_counts(key, part):
    base_key, rare_key, pick_key = jax.random.split(jax.random.fold_in(key, 11), 3)
    full_shape = (N_IA, N_JA, N_KA)
    device_total = N_IA * N_JA * N_KA
    base_count = jax.random.randint(base_key, full_shape, 0, CAP // 2 + 1)
    rare_full = jax.random.randint(rare_key, full_shape, 0, 16) == 0
    chosen = jax.random.randint(pick_key, (), 0, device_total)
    flat_number = jnp.arange(device_total, dtype=jnp.int32).reshape(full_shape)
    full_slots = jnp.logical_or(rare_full, flat_number == chosen)
    return jnp.where(full_slots, CAP, base_count).astype(jnp.int32)


def draw_coords(key, part):
    device_total = N_IA * N_JA * N_KA
    combos = IB_DEV * JB_DEV * KB_DEV
    device_keys = jax.random.split(jax.random.fold_in(key, 23), device_total)
    shuffled = jax.vmap(lambda device_key: jax.random.permutation(device_key, combos))(device_keys)[:, :CAP]
    flat_number = jnp.arange(device_total, dtype=jnp.int32)
    shift_amount = jnp.where(flat_number == device_total - 1, combos - 1 - shuffled[:, 0], 0)
    shift_amount = jnp.where(flat_number == 0, combos - shuffled[:, 0], shift_amount)
    picked = (shuffled + shift_amount[:, None]) % combos
    row_block = picked // (JB_DEV * KB_DEV)
    col_block = picked // KB_DEV % JB_DEV
    depth_block = picked % KB_DEV
    row_owner = flat_number // (N_JA * N_KA)
    col_owner = flat_number // N_KA % N_JA
    depth_owner = flat_number % N_KA
    global_coords = jnp.stack([row_block + row_owner[:, None] * IB_DEV, col_block + col_owner[:, None] * JB_DEV, depth_block + depth_owner[:, None] * KB_DEV], axis=-1)
    return global_coords.reshape(N_IA, N_JA, N_KA * CAP, 3).astype(jnp.int32)


def levels(stream_key, extent, shards, least, high):
    gain, own = 1.0, jax.random.fold_in(stream_key, 6)
    for axis_at, blocks in shards:
        heights = jnp.exp(jax.random.uniform(jax.random.fold_in(own, axis_at), (blocks,), jnp.float32, least / len(shards), high / len(shards)))
        gain = gain * jnp.repeat(heights, extent[axis_at] // blocks).reshape([-1 if axis == axis_at else 1 for axis in range(len(extent))])
    return gain


def normal_values(own_key, extent, scale, reach, cuts=(), kind=jnp.bfloat16):
    factor_of = levels(own_key, extent, cuts, -0.22, 0.18) if cuts else 1.0
    array = jax.random.normal(own_key, extent, jnp.float32) * scale * factor_of
    return jnp.minimum(jnp.maximum(array, -reach), reach).astype(kind)


def setup_inputs(seed: int = 0) -> dict:
    keys = jax.random.split(jax.random.key(seed), 9)
    observed = normal_values(keys[0], (N_IA, N_JA, N_KA * CAP, BI, BK, BJ), 1.0, 6.0, ((0, 4), (1, 2), (2, 4)))
    weights = draw_weights(jax.random.fold_in(keys[8], 71), 0)
    coords = draw_coords(jax.random.fold_in(keys[8], 71), 0)
    counts = draw_counts(jax.random.fold_in(keys[8], 71), 0)
    factor_rows = normal_values(keys[4], (R, I), R ** -0.5, 0.75, ((1, 32),))
    factor_cols = normal_values(keys[5], (R, J), R ** -0.5, 0.75, ((1, 8),))
    factor_depth = normal_values(keys[6], (R, K), R ** -0.5, 0.75)
    core_tensor = normal_values(keys[7], (R, R, R), 1.0, 6.0)
    return {"observed": observed, "weights": weights, "coords": coords, "counts": counts, "factor_rows": factor_rows, "factor_cols": factor_cols, "factor_depth": factor_depth, "core_tensor": core_tensor}


resid_scale = 1.0 / 64.0


def block_terms(observed_block, weight_block, row_factor, col_factor, depth_factor, core_tensor):
    rank_width, block_rows = row_factor.shape
    block_cols = col_factor.shape[1]
    slab_depth = depth_factor.shape[1]
    core_flat = core_tensor.reshape(rank_width * rank_width, rank_width)
    first_cube = jnp.dot(core_flat, depth_factor, preferred_element_type=jnp.float32).astype(jnp.bfloat16)
    first_cube = first_cube.reshape(rank_width, rank_width, slab_depth)
    second_cube = jnp.einsum("rsk,sj->rkj", first_cube.astype(jnp.float32), col_factor.astype(jnp.float32)).astype(jnp.bfloat16)
    second_flat = second_cube.reshape(rank_width, slab_depth * block_cols)
    model_block = jnp.dot(row_factor.T, second_flat, preferred_element_type=jnp.float32)
    weight_flat = weight_block.reshape(block_rows, slab_depth * block_cols).astype(jnp.float32)
    data_flat = observed_block.reshape(block_rows, slab_depth * block_cols).astype(jnp.float32)
    residual = (weight_flat * (model_block - data_flat) * resid_scale).astype(jnp.bfloat16)
    row_term = jnp.dot(second_flat, residual.T, preferred_element_type=jnp.float32)
    first_back = jnp.dot(row_factor, residual, preferred_element_type=jnp.float32).astype(jnp.bfloat16)
    back_cube = first_back.reshape(rank_width, slab_depth, block_cols)
    col_term = jnp.einsum("rsk,rkj->sj", first_cube.astype(jnp.float32), back_cube.astype(jnp.float32))
    second_back = jnp.einsum("sj,rkj->rsk", col_factor.astype(jnp.float32), back_cube.astype(jnp.float32)).astype(jnp.bfloat16)
    back_flat = second_back.reshape(rank_width * rank_width, slab_depth)
    depth_term = jnp.dot(core_flat.T, back_flat, preferred_element_type=jnp.float32)
    core_term = jnp.dot(back_flat, depth_factor.T, preferred_element_type=jnp.float32).reshape(rank_width, rank_width, rank_width)
    return row_term, col_term, depth_term, core_term


def add_columns(table, piece, start_col):
    width = piece.shape[1]
    return lax.dynamic_update_slice_in_dim(table, lax.dynamic_slice_in_dim(table, start_col, width, 1) + piece, start_col, 1)


def reference(observed, weights, coords, counts, factor_rows, factor_cols, factor_depth, core_tensor):
    rank_width = core_tensor.shape[0]
    slot_total = N_IA * N_JA * N_KA * CAP
    data_all = observed.reshape(slot_total, BI, BK, BJ)
    weight_all = weights.reshape(slot_total, BI, BK, BJ)
    coord_all = coords.reshape(slot_total, 3)
    slot_local = jnp.arange(CAP, dtype=jnp.int32)
    live_slot = (slot_local[None, None, None, :] < counts[:, :, :, None]).reshape(slot_total)
    start_sums = (
        jnp.zeros((rank_width, I), jnp.float32),
        jnp.zeros((rank_width, J), jnp.float32),
        jnp.zeros((rank_width, K), jnp.float32),
        jnp.zeros((rank_width, rank_width, rank_width), jnp.float32),
    )

    def accumulate(running, slot_index):
        def add_block(current):
            rows_sum, cols_sum, depth_sum, core_sum = current
            position = coord_all[slot_index]
            row_start = (position[0] * BI).astype(jnp.int32)
            col_start = (position[1] * BJ).astype(jnp.int32)
            depth_start = (position[2] * BK).astype(jnp.int32)
            row_factor = lax.dynamic_slice_in_dim(factor_rows, row_start, BI, 1)
            col_factor = lax.dynamic_slice_in_dim(factor_cols, col_start, BJ, 1)
            depth_factor = lax.dynamic_slice_in_dim(factor_depth, depth_start, BK, 1)
            block_sums = block_terms(data_all[slot_index], weight_all[slot_index], row_factor, col_factor, depth_factor, core_tensor)
            rows_sum = add_columns(rows_sum, block_sums[0], row_start)
            cols_sum = add_columns(cols_sum, block_sums[1], col_start)
            depth_sum = add_columns(depth_sum, block_sums[2], depth_start)
            return (rows_sum, cols_sum, depth_sum, core_sum + block_sums[3])

        def keep_block(current):
            return current

        return lax.cond(live_slot[slot_index], add_block, keep_block, running), None

    finished, _ = lax.scan(accumulate, start_sums, jnp.arange(slot_total, dtype=jnp.int32))
    return (finished[0], finished[1], finished[2], finished[3])
```

```python
import functools

import jax
import jax.numpy as jnp
from jax import lax
from jax.experimental import pallas as pl
from jax.experimental.pallas import tpu as pltpu
from jax.sharding import PartitionSpec as P

resid_scale = 1.0 / 64.0
f32 = jnp.float32
bf16 = jnp.bfloat16


def dot(a, b, contract=((1,), (0,))):
    return lax.dot_general(a, b, (contract, ((), ())), preferred_element_type=f32)


def prepare_kernel(
    scalars, observed, weights, factor_depth, core, data_out, weight_out, cube_out, cube_turned_out, spread, cube_wide
):
    slot = pl.program_id(0)
    rank = core.shape[0]
    _, rows, slab, cols = observed.shape
    depth_blocks = cube_out.shape[0]
    half = slab // 2

    @pl.when(slot == 0)
    def _():
        width = depth_blocks * slab
        start = pl.multiple_of(scalars[1] * width, width)
        depth = factor_depth[:, pl.ds(start, width)].astype(f32).T
        order = [
            depth[t * slab + h * half : t * slab + (h + 1) * half] for h in range(2) for t in range(depth_blocks)
        ]
        depth = jnp.concatenate(order, axis=0).astype(bf16)
        count = depth_blocks * half

        def one_rank(r1, carry):
            piece = dot(depth, core[r1], ((1,), (1,)))
            wide = jnp.concatenate([piece[:count], piece[count:]], axis=1)
            cube_wide[pl.ds(r1, count, stride=rank), :] = wide
            return carry

        lax.fori_loop(0, rank, one_rank, 0, unroll=8)
        for t in range(depth_blocks):
            block = cube_wide[t * half * rank : (t + 1) * half * rank, :]
            cube_out[t] = block.astype(bf16)
            cube_turned_out[t] = block.T.astype(bf16)

    @pl.when(slot < scalars[0])
    def _():
        for source, target in ((observed, data_out), (weights, weight_out)):
            for i in range(0, rows, 16):
                spread[i * slab : (i + 16) * slab, :] = (
                    source[0, i : i + 16].astype(f32).reshape(16 * slab, cols)
                )
            for k in range(slab):
                target[0, k] = spread[pl.ds(k, rows, stride=slab), :].astype(bf16)


def prepare(scalars, observed, weights, factor_depth, core, depth_blocks):
    slots, rows, slab, cols = observed.shape
    rank = core.shape[0]
    half = slab // 2

    def live(slot, scalars):
        return (jnp.minimum(slot, jnp.maximum(scalars[0] - 1, 0)), 0, 0, 0)

    def whole(ndim):
        return lambda slot, scalars: (0,) * ndim

    turned = (slots, slab, rows, cols)
    cube = (depth_blocks, half * rank, 2 * rank)
    cube_turned = (depth_blocks, 2 * rank, half * rank)
    return pl.pallas_call(
        prepare_kernel,
        out_shape=(
            jax.ShapeDtypeStruct(turned, bf16),
            jax.ShapeDtypeStruct(turned, bf16),
            jax.ShapeDtypeStruct(cube, bf16),
            jax.ShapeDtypeStruct(cube_turned, bf16),
        ),
        grid_spec=pltpu.PrefetchScalarGridSpec(
            num_scalar_prefetch=1,
            grid=(slots,),
            in_specs=[
                pl.BlockSpec((1, rows, slab, cols), live),
                pl.BlockSpec((1, rows, slab, cols), live),
                pl.BlockSpec(factor_depth.shape, whole(2)),
                pl.BlockSpec(core.shape, whole(3)),
            ],
            out_specs=[
                pl.BlockSpec((1, slab, rows, cols), live),
                pl.BlockSpec((1, slab, rows, cols), live),
                pl.BlockSpec(cube, whole(3)),
                pl.BlockSpec(cube_turned, whole(3)),
            ],
            scratch_shapes=[
                pltpu.VMEM((rows * slab, cols), f32),
                pltpu.VMEM((depth_blocks * half * rank, 2 * rank), f32),
            ],
        ),
        compiler_params=pltpu.CompilerParams(vmem_limit_bytes=48 * 2**20),
        cost_estimate=pl.CostEstimate(flops=10**8, bytes_accessed=16 * 2**20, transcendentals=0),
        name="prepare",
    )(scalars, observed, weights, factor_depth, core)


COUNT, KA, ROW_BASE, COL_BASE, ROW_MASK, COL_MASK, CORE_MASK, COORDS = range(8)


def terms_kernel(
    row_chunks,
    scalars,
    data,
    weight,
    cube,
    cube_turned,
    row_table,
    col_table,
    factor_depth,
    core,
    core_out,
    rows_out,
    cols_out,
    depth_out,
    wide_col,
    forward,
    backward,
    by_rank,
    second_all,
    depth_all,
    depth_turned,
    depth_sum,
):
    slot = pl.program_id(0)
    slots = pl.num_programs(0)
    _, slab, rows, cols = data.shape
    rank = core.shape[0]
    half = slab // 2
    pairs = rank // 2
    depth_blocks = cube.shape[0]

    @pl.when(slot == 0)
    def _():
        second_all[...] = jnp.zeros_like(second_all)
        depth_all[...] = jnp.zeros_like(depth_all)
        depth_sum[...] = jnp.zeros_like(depth_sum)
        rows_out[...] = jnp.zeros_like(rows_out)
        cols_out[...] = jnp.zeros_like(cols_out)
        wide_col[...] = jnp.zeros_like(wide_col)
        width = depth_blocks * slab
        start = pl.multiple_of(scalars[KA] * width, width)
        depth_turned[...] = factor_depth[:, pl.ds(start, width)].astype(f32).T

    @pl.when(slot < scalars[COUNT])
    def _():
        row_at = (scalars[COORDS + 3 * slot] - scalars[ROW_BASE]) ^ scalars[ROW_MASK]
        col_at = (scalars[COORDS + 3 * slot + 1] - scalars[COL_BASE]) ^ scalars[COL_MASK]
        depth_at = scalars[COORDS + 3 * slot + 2] - scalars[KA] * depth_blocks
        row_factor = row_table[row_at]
        row_turned = row_factor.astype(f32).T.astype(bf16)
        col_factor = col_table[col_at]
        wide_col[:rank, :cols] = col_factor
        wide_col[rank:, cols:] = col_factor
        own_depth = depth_turned[pl.ds(pl.multiple_of(depth_at * slab, slab), slab), :]
        depth_all[pl.ds(pl.multiple_of(slot * slab, slab), slab), :] = own_depth.astype(bf16)

        step = 4

        def some_pairs(at, row_sum):
            first = at * step
            for extra in range(step):
                kp = first + extra
                lines = pl.ds(pl.multiple_of(kp * rank, rank), rank)
                second = dot(cube[depth_at, lines, :], wide_col[...]).astype(bf16)
                model = dot(row_turned, second)
                parts = []
                for h in range(2):
                    seen = data[0, h * half + kp].astype(f32)
                    scale = weight[0, h * half + kp].astype(f32)
                    gap = model[:, h * cols : (h + 1) * cols] - seen
                    parts.append((scale * gap * resid_scale).astype(bf16))
                residual = jnp.concatenate(parts, axis=1)
                row_sum = row_sum + dot(second, residual, ((1,), (1,)))
                back = dot(row_factor, residual).astype(bf16)
                backward[lines, :] = back
                back = back.astype(f32)
                for h in range(2):
                    by_rank[pl.ds(h * half + kp, rank, stride=slab), :] = back[:, h * cols : (h + 1) * cols]
            return row_sum

        row_sum = lax.fori_loop(0, half // step, some_pairs, jnp.zeros((rank, rows), f32))
        rows_out[row_at] += row_sum
        wide = dot(cube_turned[depth_at], backward[...])
        cols_out[col_at] += wide[:rank, :cols] + wide[rank:, cols:]
        count = pairs * slab
        for part in range(4):
            lo, size = part * count // 4, count // 4
            ranked = jnp.concatenate(
                [by_rank[lo : lo + size, :].astype(bf16), by_rank[count + lo : count + lo + size, :].astype(bf16)],
                axis=1,
            )
            second_back = dot(ranked, wide_col[...], ((1,), (1,))).astype(bf16)
            second_all[pl.ds(part * pairs // 4, pairs // 4), pl.ds(pl.multiple_of(slot * slab, slab), slab), :] = (
                second_back.reshape(pairs // 4, slab, 2 * rank)
            )

    @pl.when(slot == slots - 1)
    def _():
        def one_chunk(at, total):
            pair = at ^ scalars[CORE_MASK]
            second = second_all[pair]
            both = jnp.concatenate([core[pair], core[pairs + pair]], axis=0)
            total = total + dot(second, both)
            piece = dot(second, depth_all[...], ((0,), (0,)))
            core_out[at] = jnp.concatenate([piece[:rank], piece[rank:]], axis=1)
            return total

        total = lax.fori_loop(0, pairs, one_chunk, jnp.zeros((second_all.shape[1], rank), f32), unroll=2)
        for s in range(second_all.shape[1] // slab):

            @pl.when(s < scalars[COUNT])
            def _():
                at = scalars[COORDS + 3 * s + 2] - scalars[KA] * depth_blocks
                lines = pl.ds(pl.multiple_of(at * slab, slab), slab)
                depth_sum[lines, :] += total[s * slab : (s + 1) * slab]

        depth_out[...] = depth_sum[...].T


def terms(scalars, data, weight, cube, cube_turned, row_table, col_table, factor_depth, core):
    slots, slab, rows, cols = data.shape
    rank = core.shape[0]
    half = slab // 2
    depth_blocks = cube.shape[0]

    def live(slot, scalars):
        return (jnp.minimum(slot, jnp.maximum(scalars[COUNT] - 1, 0)), 0, 0, 0)

    def whole(array):
        return pl.BlockSpec(array.shape, lambda slot, scalars: (0,) * len(array.shape))

    outs = (
        jax.ShapeDtypeStruct((rank // 2, rank, 2 * rank), f32),
        jax.ShapeDtypeStruct((row_table.shape[0], rank, rows), f32),
        jax.ShapeDtypeStruct((col_table.shape[0], rank, cols), f32),
        jax.ShapeDtypeStruct((rank, depth_blocks * slab), f32),
    )
    return pl.pallas_call(
        functools.partial(terms_kernel, row_table.shape[0]),
        out_shape=outs,
        grid_spec=pltpu.PrefetchScalarGridSpec(
            num_scalar_prefetch=1,
            grid=(slots,),
            in_specs=[
                pl.BlockSpec((1, slab, rows, cols), live),
                pl.BlockSpec((1, slab, rows, cols), live),
                whole(cube),
                whole(cube_turned),
                whole(row_table),
                whole(col_table),
                whole(factor_depth),
                whole(core),
            ],
            out_specs=[whole(out) for out in outs],
            scratch_shapes=[
                pltpu.VMEM((2 * rank, 2 * cols), bf16),
                pltpu.VMEM((8, 128), bf16),
                pltpu.VMEM((half * rank, 2 * cols), bf16),
                pltpu.VMEM((rank * slab, cols), f32),
                pltpu.VMEM((rank // 2, slots * slab, 2 * rank), bf16),
                pltpu.VMEM((slots * slab, rank), bf16),
                pltpu.VMEM((depth_blocks * slab, rank), f32),
                pltpu.VMEM((depth_blocks * slab, rank), f32),
            ],
        ),
        compiler_params=pltpu.CompilerParams(vmem_limit_bytes=48 * 2**20),
        cost_estimate=pl.CostEstimate(flops=10**9, bytes_accessed=16 * 2**20, transcendentals=0),
        name="terms",
    )(scalars, data, weight, cube, cube_turned, row_table, col_table, factor_depth, core)


def unpack_kernel(scalars, own, other, out):
    rank = out.shape[1]
    mine = pl.program_id(0)
    high = pl.program_id(1)
    count = out.shape[0]
    low = scalars[0] & (count - 1)

    for source, which in ((own, 0), (other, 1)):
        for h in range(2):

            @pl.when(jnp.logical_and(mine == which, high == h))
            def _():
                def one(at, carry):
                    out[at ^ low] = source[at][:, h * rank : (h + 1) * rank]
                    return carry

                lax.fori_loop(0, count, one, 0, unroll=4)


def unpack(mask, own, other):
    count, rank, _ = own.shape
    parts = 2

    def place(mine, high, scalars):
        return (high * parts + ((scalars[0] // count) ^ mine), 0, 0)

    def all_of(mine, high, scalars):
        return (0, 0, 0)

    return pl.pallas_call(
        unpack_kernel,
        out_shape=jax.ShapeDtypeStruct((rank, rank, rank), f32),
        grid_spec=pltpu.PrefetchScalarGridSpec(
            num_scalar_prefetch=1,
            grid=(parts, 2),
            in_specs=[pl.BlockSpec(own.shape, all_of), pl.BlockSpec(other.shape, all_of)],
            out_specs=pl.BlockSpec((count, rank, rank), place),
        ),
        compiler_params=pltpu.CompilerParams(vmem_limit_bytes=32 * 2**20),
        name="unpack",
    )(mask, own, other)


def power_of_two(n):
    return n & (n - 1) == 0


def swap(value, axis, size, mask):
    return lax.ppermute(value, axis, [(at, at ^ mask) for at in range(size)])


def on_device(sizes, observed, weights, coords, counts, factor_rows, factor_cols, factor_depth, core_tensor):
    n_ia, n_ja, n_ka = sizes["ia"], sizes["ja"], sizes["ka"]
    devices = n_ia * n_ja * n_ka
    rank = core_tensor.shape[0]
    _, _, slots, rows, slab, cols = observed.shape
    data = observed.reshape(observed.shape[2:])
    weight = weights.reshape(weights.shape[2:])
    own_coords = coords.reshape(slots * 3)
    own_count = counts.reshape(())
    row_chunks = factor_rows.shape[1] * n_ja * n_ka // rows
    col_chunks = factor_cols.shape[1] * n_ka // cols
    depth_blocks = factor_depth.shape[1] // n_ka // slab
    ia, ja, ka = lax.axis_index("ia"), lax.axis_index("ja"), lax.axis_index("ka")
    by_swaps = (
        n_ja == 2
        and power_of_two(n_ia)
        and power_of_two(n_ka)
        and rank // 2 == devices
        and factor_rows.shape[1] == rows
        and factor_cols.shape[1] == cols
    )

    data, weight, cube, cube_turned = prepare(
        jnp.stack([own_count, ka]).astype(jnp.int32), data, weight, factor_depth, core_tensor, depth_blocks
    )

    if by_swaps:
        both = jnp.stack([factor_rows, factor_cols])
        from_ka = [both] + [swap(both, "ka", n_ka, mask) for mask in range(1, n_ka)]
        own_rows = jnp.stack([piece[0] for piece in from_ka])
        row_table = jnp.concatenate([own_rows, swap(own_rows, "ja", n_ja, 1)])
        col_table = jnp.stack([piece[1] for piece in from_ka])
        masks = [ja * n_ka + ka, ka, (ja * n_ia + ia) * n_ka + ka]
    else:
        row_table = lax.all_gather(factor_rows, ("ja", "ka"), axis=1, tiled=True)
        row_table = row_table.reshape(rank, row_chunks, rows).transpose(1, 0, 2)
        col_table = lax.all_gather(factor_cols, "ka", axis=1, tiled=True)
        col_table = col_table.reshape(rank, col_chunks, cols).transpose(1, 0, 2)
        masks = [0, 0, 0]

    scalars = jnp.stack([own_count, ka, ia * row_chunks, ja * col_chunks, *masks]).astype(jnp.int32)
    core_sum, rows_sum, cols_sum, depth_sum = terms(
        jnp.concatenate([scalars, own_coords]),
        data,
        weight,
        cube,
        cube_turned,
        row_table,
        col_table,
        factor_depth,
        core_tensor,
    )

    if not by_swaps:
        rows_whole = rows_sum.transpose(1, 0, 2).reshape(rank, row_chunks * rows)
        cols_whole = cols_sum.transpose(1, 0, 2).reshape(rank, col_chunks * cols)
        core_whole = core_sum.reshape(rank // 2, rank, 2, rank).transpose(2, 0, 1, 3).reshape(rank, rank, rank)
        return (
            lax.psum_scatter(rows_whole, ("ja", "ka"), scatter_dimension=1, tiled=True),
            lax.psum_scatter(lax.psum(cols_whole, "ia"), "ka", scatter_dimension=1, tiled=True),
            lax.psum(depth_sum, ("ia", "ja")),
            lax.psum(core_whole, ("ia", "ja", "ka")),
        )

    half = devices // 2
    keep = jnp.concatenate([core_sum[:half], rows_sum[:n_ka], depth_sum[None]])
    send = jnp.concatenate([core_sum[half:], rows_sum[n_ka:], depth_sum[None]])
    total = keep + swap(send, "ja", n_ja, 1)
    core_half, rows_half, depth_half = total[:half], total[half : half + n_ka], total[half + n_ka :]
    core_quarter = core_half[:n_ka]
    depth_total = depth_half[0]
    for mask in range(1, n_ia):
        piece = jnp.concatenate([core_half[mask * n_ka : (mask + 1) * n_ka], depth_half])
        got = swap(piece, "ia", n_ia, mask)
        core_quarter = core_quarter + got[:n_ka]
        depth_total = depth_total + got[n_ka]
    own = jnp.stack([core_quarter[0], rows_half[0], cols_sum[0]])
    for mask in range(1, n_ka):
        own = own + swap(jnp.stack([core_quarter[mask], rows_half[mask], cols_sum[mask]]), "ka", n_ka, mask)
    core_own, rows_total, cols_own = own[0], own[1], own[2]
    pieces = [core_own] + [swap(core_own, "ka", n_ka, mask) for mask in range(1, n_ka)]
    pack = jnp.stack(pieces + [cols_own])
    cols_total = cols_own
    gathered = [pack[:n_ka]]
    for mask in range(1, n_ia):
        got = swap(pack, "ia", n_ia, mask)
        gathered.append(got[:n_ka])
        cols_total = cols_total + got[n_ka]
    mine = jnp.concatenate(gathered)
    other = swap(mine, "ja", n_ja, 1)
    core_total = unpack(jnp.stack([masks[2]]).astype(jnp.int32), mine, other)
    return (rows_total, cols_total, depth_total, core_total)


def solution(mesh):
    in_specs = (
        P("ia", "ja", "ka", None, None, None),
        P("ia", "ja", "ka", None, None, None),
        P("ia", "ja", "ka", None),
        P("ia", "ja", "ka"),
        P(None, ("ia", "ja", "ka")),
        P(None, ("ja", "ka")),
        P(),
        P(),
    )
    out_specs = (P(None, ("ia", "ja", "ka")), P(None, ("ja", "ka")), P(None, "ka"), P())
    return jax.shard_map(
        functools.partial(on_device, dict(mesh.shape)),
        mesh=mesh,
        in_specs=in_specs,
        out_specs=out_specs,
        check_vma=False,
    )
```

```python
import functools

import jax
import jax.numpy as jnp
from jax import lax
from jax.experimental import pallas as pl
from jax.experimental.pallas import tpu as pltpu
from jax.sharding import PartitionSpec as P

resid_scale = 1.0 / 64.0
f32 = jnp.float32
bf16 = jnp.bfloat16


def dot(a, b, contract=((1,), (0,))):
    return lax.dot_general(a, b, (contract, ((), ())), preferred_element_type=f32)


def cube_kernel(depth_blocks, slab, factor_depth, core, cube_out, cube_turned_out, cube_wide):
    rank = core.shape[0]
    half = slab // 2
    width = depth_blocks * slab
    start = pl.multiple_of(lax.axis_index("ka") * width, width)
    depth = factor_depth[:, pl.ds(start, width)].astype(f32).T
    order = [depth[t * slab + h * half : t * slab + (h + 1) * half] for h in range(2) for t in range(depth_blocks)]
    depth = jnp.concatenate(order, axis=0).astype(bf16)
    count = depth_blocks * half

    def one_rank(r1, carry):
        piece = dot(depth, core[r1], ((1,), (1,)))
        wide = jnp.concatenate([piece[:count], piece[count:]], axis=1)
        cube_wide[pl.ds(r1, count, stride=rank + 1), :] = wide
        return carry

    lax.fori_loop(0, rank, one_rank, 0, unroll=16)
    for t in range(depth_blocks):
        for kp in range(half):
            at = (t * half + kp) * (rank + 1)
            block = cube_wide[at : at + rank, :]
            cube_out[t, kp * rank : (kp + 1) * rank, :] = block.astype(bf16)
        cube_turned_out[t] = cube_out[t].astype(f32).T.astype(bf16)


def first_cubes(factor_depth, core, depth_blocks, slab):
    rank = core.shape[0]
    half = slab // 2
    return pl.pallas_call(
        functools.partial(cube_kernel, depth_blocks, slab),
        out_shape=(
            jax.ShapeDtypeStruct((depth_blocks, half * rank, 2 * rank), bf16),
            jax.ShapeDtypeStruct((depth_blocks, 2 * rank, half * rank), bf16),
        ),
        in_specs=[pl.BlockSpec(memory_space=pltpu.VMEM)] * 2,
        out_specs=[pl.BlockSpec(memory_space=pltpu.VMEM)] * 2,
        scratch_shapes=[pltpu.VMEM((depth_blocks * half * (rank + 1), 2 * rank), f32)],
        compiler_params=pltpu.CompilerParams(vmem_limit_bytes=24 * 2**20),
        cost_estimate=pl.CostEstimate(flops=10**9, bytes_accessed=4 * 2**20, transcendentals=0),
        name="first_cubes",
    )(factor_depth, core)


def masks_of(relative, sizes):
    ia, ja, ka = lax.axis_index("ia"), lax.axis_index("ja"), lax.axis_index("ka")
    if not relative:
        return 0, 0, 0
    return ja * sizes["ka"] + ka, ka, (ja * sizes["ia"] + ia) * sizes["ka"] + ka


def terms_kernel(
    relative,
    sizes,
    counts,
    coords,
    data,
    weight,
    cube,
    cube_turned,
    row_table,
    col_table,
    factor_depth,
    core,
    core_out,
    rows_out,
    cols_out,
    depth_out,
    wide_col,
    backward,
    by_rank,
    second_all,
    depth_all,
    depth_turned,
    depth_sum,
    spread_data,
    spread_weight,
):
    slot = pl.program_id(0)
    slots = pl.num_programs(0)
    _, rows, slab, cols = data.shape
    rank = core.shape[0]
    half = slab // 2
    pairs = rank // 2
    depth_blocks = cube.shape[0]
    count = counts[0, 0, 0]
    row_mask, col_mask, core_mask = masks_of(relative, sizes)
    row_base = lax.axis_index("ia") * row_table.shape[0]
    col_base = lax.axis_index("ja") * col_table.shape[0]
    depth_base = lax.axis_index("ka") * depth_blocks

    @pl.when(slot == 0)
    def _():
        second_all[...] = jnp.zeros_like(second_all)
        depth_all[...] = jnp.zeros_like(depth_all)
        depth_sum[...] = jnp.zeros_like(depth_sum)
        rows_out[...] = jnp.zeros_like(rows_out)
        cols_out[...] = jnp.zeros_like(cols_out)
        wide_col[...] = jnp.zeros_like(wide_col)
        width = depth_blocks * slab
        start = pl.multiple_of(lax.axis_index("ka") * width, width)
        depth_turned[...] = factor_depth[:, pl.ds(start, width)].astype(f32).T

    @pl.when(slot < count)
    def _():
        row_at = (coords[0, 0, slot, 0] - row_base) ^ row_mask
        col_at = (coords[0, 0, slot, 1] - col_base) ^ col_mask
        depth_at = coords[0, 0, slot, 2] - depth_base
        row_factor = row_table[row_at]
        row_turned = row_factor.astype(f32).T.astype(bf16)
        col_factor = col_table[col_at]
        wide_col[:rank, :cols] = col_factor
        wide_col[rank:, cols:] = col_factor
        own_depth = depth_turned[pl.ds(pl.multiple_of(depth_at * slab, slab), slab), :]
        depth_all[pl.ds(pl.multiple_of(slot * slab, slab), slab), :] = own_depth.astype(bf16)

        step = 4
        groups = half // step
        wide_factor = wide_col[...]
        for source, target in ((data, spread_data), (weight, spread_weight)):
            for i in range(rows):
                target[i * (slab + 1) : i * (slab + 1) + slab, :] = source[0, i].astype(f32)

        def second_of(g):
            lines = cube[depth_at, g * step * rank : (g + 1) * step * rank, :]
            block = dot(lines, wide_factor).astype(bf16)
            return jnp.concatenate([block[kp * rank : (kp + 1) * rank] for kp in range(step)], axis=1)

        def residual_of(g, model):
            parts = []
            for kp in range(step):
                for h in range(2):
                    lines = pl.ds(h * half + g * step + kp, rows, stride=slab + 1)
                    seen, scale = spread_data[lines, :], spread_weight[lines, :]
                    at = (kp * 2 + h) * cols
                    gap = model[:, at : at + cols] - seen
                    parts.append((scale * gap * resid_scale).astype(bf16))
            return jnp.concatenate(parts, axis=1)

        def keep_back(g, back):
            back = back.astype(bf16)
            for kp in range(step):
                pair = back[:, kp * 2 * cols : (kp + 1) * 2 * cols]
                at = (g * step + kp) * rank
                backward[at : at + rank, :] = pair
                wider = pair.astype(f32)
                for h in range(2):
                    lines = pl.ds(h * half + g * step + kp, rank, stride=slab + 1)
                    by_rank[lines, :] = wider[:, h * cols : (h + 1) * cols]

        row_sum = jnp.zeros((rank, rows), f32)
        seconds = [second_of(g) for g in range(groups)]
        models = [None] * groups
        models[0] = dot(row_turned, seconds[0])
        for g in range(groups):
            if g + 1 < groups:
                models[g + 1] = dot(row_turned, seconds[g + 1])
            residual = residual_of(g, models[g])
            keep_back(g, dot(row_factor, residual))
            row_sum = row_sum + dot(seconds[g], residual, ((1,), (1,)))
        rows_out[row_at] += row_sum
        wide = dot(cube_turned[depth_at], backward[...])
        cols_out[col_at] += wide[:rank, :cols] + wide[rank:, cols:]
        lines = pl.ds(pl.multiple_of(slot * slab, slab), slab)
        for first in range(0, pairs, 8):
            ranked = []
            for pair in range(first, first + 8):
                spots = [at * (slab + 1) for at in (pair, pairs + pair)]
                ranked.append(jnp.concatenate([by_rank[at : at + slab, :].astype(bf16) for at in spots], axis=1))
            ranked = jnp.concatenate(ranked, axis=0)
            second_back = dot(ranked, wide_col[...], ((1,), (1,))).astype(bf16)
            second_all[first : first + 8, lines, :] = second_back.reshape(8, slab, 2 * rank)

    @pl.when(slot == slots - 1)
    def _():
        def one_chunk(at, total):
            pair = at ^ core_mask
            second = second_all[pair]
            both = jnp.concatenate([core[pair], core[pairs + pair]], axis=0)
            total = total + dot(second, both)
            piece = dot(second, depth_all[...], ((0,), (0,)))
            core_out[at] = jnp.concatenate([piece[:rank], piece[rank:]], axis=1)
            return total

        total = lax.fori_loop(0, pairs, one_chunk, jnp.zeros((second_all.shape[1], rank), f32), unroll=16)
        for s in range(second_all.shape[1] // slab):

            @pl.when(s < count)
            def _():
                at = coords[0, 0, s, 2] - depth_base
                lines = pl.ds(pl.multiple_of(at * slab, slab), slab)
                depth_sum[lines, :] += total[s * slab : (s + 1) * slab]

        depth_out[...] = depth_sum[...].T


def terms(relative, sizes, counts, coords, data, weight, cube, cube_turned, row_table, col_table, factor_depth, core):
    slots, rows, slab, cols = data.shape
    rank = core.shape[0]
    half = slab // 2
    depth_blocks = cube.shape[0]

    def live(slot, counts, coords):
        return (jnp.minimum(slot, jnp.maximum(counts[0, 0, 0] - 1, 0)), 0, 0, 0)

    def whole(array):
        return pl.BlockSpec(array.shape, lambda slot, counts, coords: (0,) * len(array.shape))

    outs = (
        jax.ShapeDtypeStruct((rank // 2, rank, 2 * rank), f32),
        jax.ShapeDtypeStruct((row_table.shape[0], rank, rows), f32),
        jax.ShapeDtypeStruct((col_table.shape[0], rank, cols), f32),
        jax.ShapeDtypeStruct((rank, depth_blocks * slab), f32),
    )
    return pl.pallas_call(
        functools.partial(terms_kernel, relative, sizes),
        out_shape=outs,
        grid_spec=pltpu.PrefetchScalarGridSpec(
            num_scalar_prefetch=2,
            grid=(slots,),
            in_specs=[
                pl.BlockSpec((1, rows, slab, cols), live),
                pl.BlockSpec((1, rows, slab, cols), live),
                whole(cube),
                whole(cube_turned),
                whole(row_table),
                whole(col_table),
                whole(factor_depth),
                whole(core),
            ],
            out_specs=[whole(out) for out in outs],
            scratch_shapes=[
                pltpu.VMEM((2 * rank, 2 * cols), bf16),
                pltpu.VMEM((half * rank, 2 * cols), bf16),
                pltpu.VMEM((rank * (slab + 1), cols), f32),
                pltpu.VMEM((rank // 2, slots * slab, 2 * rank), bf16),
                pltpu.VMEM((slots * slab, rank), bf16),
                pltpu.VMEM((depth_blocks * slab, rank), f32),
                pltpu.VMEM((depth_blocks * slab, rank), f32),
                pltpu.VMEM((rows * (slab + 1), cols), f32),
                pltpu.VMEM((rows * (slab + 1), cols), f32),
            ],
        ),
        compiler_params=pltpu.CompilerParams(vmem_limit_bytes=48 * 2**20),
        cost_estimate=pl.CostEstimate(flops=10**9, bytes_accessed=16 * 2**20, transcendentals=0),
        name="terms",
    )(counts, coords, data, weight, cube, cube_turned, row_table, col_table, factor_depth, core)


def unpack_kernel(scalars, own, other, out):
    rank = out.shape[1]
    mine = pl.program_id(0)
    high = pl.program_id(1)
    count = out.shape[0]
    low = scalars[0] & (count - 1)

    for source, which in ((own, 0), (other, 1)):
        for h in range(2):

            @pl.when(jnp.logical_and(mine == which, high == h))
            def _():
                def one(at, carry):
                    out[at ^ low] = source[at][:, h * rank : (h + 1) * rank]
                    return carry

                lax.fori_loop(0, count, one, 0, unroll=4)


def unpack(mask, own, other):
    count, rank, _ = own.shape
    parts = 2

    def place(mine, high, scalars):
        return (high * parts + ((scalars[0] // count) ^ mine), 0, 0)

    def all_of(mine, high, scalars):
        return (0, 0, 0)

    return pl.pallas_call(
        unpack_kernel,
        out_shape=jax.ShapeDtypeStruct((rank, rank, rank), f32),
        grid_spec=pltpu.PrefetchScalarGridSpec(
            num_scalar_prefetch=1,
            grid=(parts, 2),
            in_specs=[pl.BlockSpec(own.shape, all_of), pl.BlockSpec(other.shape, all_of)],
            out_specs=pl.BlockSpec((count, rank, rank), place),
        ),
        compiler_params=pltpu.CompilerParams(vmem_limit_bytes=32 * 2**20),
        name="unpack",
    )(mask, own, other)


def power_of_two(n):
    return n & (n - 1) == 0


def swap(value, axis, size, mask):
    return lax.ppermute(value, axis, [(at, at ^ mask) for at in range(size)])


def on_device(sizes, observed, weights, coords, counts, factor_rows, factor_cols, factor_depth, core_tensor):
    n_ia, n_ja, n_ka = sizes["ia"], sizes["ja"], sizes["ka"]
    devices = n_ia * n_ja * n_ka
    rank = core_tensor.shape[0]
    _, _, slots, rows, slab, cols = observed.shape
    data = observed.reshape(observed.shape[2:])
    weight = weights.reshape(weights.shape[2:])
    row_chunks = factor_rows.shape[1] * n_ja * n_ka // rows
    col_chunks = factor_cols.shape[1] * n_ka // cols
    depth_blocks = factor_depth.shape[1] // n_ka // slab
    ia, ja, ka = lax.axis_index("ia"), lax.axis_index("ja"), lax.axis_index("ka")
    by_swaps = (
        n_ja == 2
        and power_of_two(n_ia)
        and power_of_two(n_ka)
        and rank // 2 == devices
        and factor_rows.shape[1] == rows
        and factor_cols.shape[1] == cols
    )

    cube, cube_turned = first_cubes(factor_depth, core_tensor, depth_blocks, slab)

    if by_swaps:
        both = jnp.stack([factor_rows, factor_cols])
        from_ka = [both] + [swap(both, "ka", n_ka, mask) for mask in range(1, n_ka)]
        own_rows = jnp.stack([piece[0] for piece in from_ka])
        row_table = jnp.concatenate([own_rows, swap(own_rows, "ja", n_ja, 1)])
        col_table = jnp.stack([piece[1] for piece in from_ka])
    else:
        row_table = lax.all_gather(factor_rows, ("ja", "ka"), axis=1, tiled=True)
        row_table = row_table.reshape(rank, row_chunks, rows).transpose(1, 0, 2)
        col_table = lax.all_gather(factor_cols, "ka", axis=1, tiled=True)
        col_table = col_table.reshape(rank, col_chunks, cols).transpose(1, 0, 2)

    core_sum, rows_sum, cols_sum, depth_sum = terms(
        by_swaps,
        sizes,
        counts,
        coords,
        data,
        weight,
        cube,
        cube_turned,
        row_table,
        col_table,
        factor_depth,
        core_tensor,
    )

    if not by_swaps:
        rows_whole = rows_sum.transpose(1, 0, 2).reshape(rank, row_chunks * rows)
        cols_whole = cols_sum.transpose(1, 0, 2).reshape(rank, col_chunks * cols)
        core_whole = core_sum.reshape(rank // 2, rank, 2, rank).transpose(2, 0, 1, 3).reshape(rank, rank, rank)
        return (
            lax.psum_scatter(rows_whole, ("ja", "ka"), scatter_dimension=1, tiled=True),
            lax.psum_scatter(lax.psum(cols_whole, "ia"), "ka", scatter_dimension=1, tiled=True),
            lax.psum(depth_sum, ("ia", "ja")),
            lax.psum(core_whole, ("ia", "ja", "ka")),
        )

    half = devices // 2
    keep = jnp.concatenate([core_sum[:half], rows_sum[:n_ka], depth_sum[None]])
    send = jnp.concatenate([core_sum[half:], rows_sum[n_ka:], depth_sum[None]])
    total = keep + swap(send, "ja", n_ja, 1)
    core_half, rows_half, depth_half = total[:half], total[half : half + n_ka], total[half + n_ka :]
    core_quarter = core_half[:n_ka]
    depth_total = depth_half[0]
    for mask in range(1, n_ia):
        piece = jnp.concatenate([core_half[mask * n_ka : (mask + 1) * n_ka], depth_half])
        got = swap(piece, "ia", n_ia, mask)
        core_quarter = core_quarter + got[:n_ka]
        depth_total = depth_total + got[n_ka]
    own = jnp.stack([core_quarter[0], rows_half[0], cols_sum[0]])
    for mask in range(1, n_ka):
        own = own + swap(jnp.stack([core_quarter[mask], rows_half[mask], cols_sum[mask]]), "ka", n_ka, mask)
    core_own, rows_total, cols_own = own[0], own[1], own[2]
    pieces = [core_own] + [swap(core_own, "ka", n_ka, mask) for mask in range(1, n_ka)]
    pack = jnp.stack(pieces + [cols_own])
    cols_total = cols_own
    gathered = [pack[:n_ka]]
    for mask in range(1, n_ia):
        got = swap(pack, "ia", n_ia, mask)
        gathered.append(got[:n_ka])
        cols_total = cols_total + got[n_ka]
    mine = jnp.concatenate(gathered)
    other = swap(mine, "ja", n_ja, 1)
    mask = (ja * n_ia + ia) * n_ka + ka
    core_total = unpack(jnp.stack([mask]).astype(jnp.int32), mine, other)
    return (rows_total, cols_total, depth_total, core_total)


def solution(mesh):
    in_specs = (
        P("ia", "ja", "ka", None, None, None),
        P("ia", "ja", "ka", None, None, None),
        P("ia", "ja", "ka", None),
        P("ia", "ja", "ka"),
        P(None, ("ia", "ja", "ka")),
        P(None, ("ja", "ka")),
        P(),
        P(),
    )
    out_specs = (P(None, ("ia", "ja", "ka")), P(None, ("ja", "ka")), P(None, "ka"), P())
    return jax.shard_map(
        functools.partial(on_device, dict(mesh.shape)),
        mesh=mesh,
        in_specs=in_specs,
        out_specs=out_specs,
        check_vma=False,
    )
```

```python
import functools

import jax
import jax.numpy as jnp
from jax import lax
from jax.experimental import pallas as pl
from jax.experimental.pallas import tpu as pltpu
from jax.sharding import PartitionSpec as P

resid_scale = 1.0 / 64.0
f32 = jnp.float32
bf16 = jnp.bfloat16
wire = jnp.float16


def dot(a, b, contract=((1,), (0,))):
    return lax.dot_general(a, b, (contract, ((), ())), preferred_element_type=f32)


def cube_kernel(depth_blocks, slab, factor_depth, core, cube_out, cube_turned_out, cube_wide):
    rank = core.shape[0]
    half = slab // 2
    width = depth_blocks * slab
    start = pl.multiple_of(lax.axis_index("ka") * width, width)
    depth = factor_depth[:, pl.ds(start, width)].astype(f32).T
    order = [depth[t * slab + h * half : t * slab + (h + 1) * half] for h in range(2) for t in range(depth_blocks)]
    depth = jnp.concatenate(order, axis=0).astype(bf16)
    count = depth_blocks * half

    def one_rank(r1, carry):
        piece = dot(depth, core[r1], ((1,), (1,)))
        wide = jnp.concatenate([piece[:count], piece[count:]], axis=1)
        cube_wide[pl.ds(r1, count, stride=rank + 1), :] = wide
        return carry

    lax.fori_loop(0, rank, one_rank, 0, unroll=16)
    for t in range(depth_blocks):
        for kp in range(half):
            at = (t * half + kp) * (rank + 1)
            block = cube_wide[at : at + rank, :]
            cube_out[t, kp * rank : (kp + 1) * rank, :] = block.astype(bf16)
        cube_turned_out[t] = cube_out[t].astype(f32).T.astype(bf16)


def first_cubes(factor_depth, core, depth_blocks, slab):
    rank = core.shape[0]
    half = slab // 2
    return pl.pallas_call(
        functools.partial(cube_kernel, depth_blocks, slab),
        out_shape=(
            jax.ShapeDtypeStruct((depth_blocks, half * rank, 2 * rank), bf16),
            jax.ShapeDtypeStruct((depth_blocks, 2 * rank, half * rank), bf16),
        ),
        in_specs=[pl.BlockSpec(memory_space=pltpu.VMEM)] * 2,
        out_specs=[pl.BlockSpec(memory_space=pltpu.VMEM)] * 2,
        scratch_shapes=[pltpu.VMEM((depth_blocks * half * (rank + 1), 2 * rank), f32)],
        compiler_params=pltpu.CompilerParams(vmem_limit_bytes=24 * 2**20),
        cost_estimate=pl.CostEstimate(flops=10**9, bytes_accessed=4 * 2**20, transcendentals=0),
        name="first_cubes",
    )(factor_depth, core)


def masks_of(relative, sizes):
    ia, ja, ka = lax.axis_index("ia"), lax.axis_index("ja"), lax.axis_index("ka")
    if not relative:
        return 0, 0, 0
    return ja * sizes["ka"] + ka, ka, (ja * sizes["ia"] + ia) * sizes["ka"] + ka


def terms_kernel(
    relative,
    sizes,
    counts,
    coords,
    data,
    weight,
    cube,
    cube_turned,
    row_table,
    col_table,
    factor_depth,
    core,
    core_out,
    rows_out,
    cols_out,
    depth_out,
    wide_col,
    backward,
    by_rank,
    second_all,
    depth_all,
    depth_turned,
    depth_sum,
    spread_data,
    spread_weight,
):
    slot = pl.program_id(0)
    slots = pl.num_programs(0)
    _, rows, slab, cols = data.shape
    rank = core.shape[0]
    half = slab // 2
    pairs = rank // 2
    depth_blocks = cube.shape[0]
    count = counts[0, 0, 0]
    row_mask, col_mask, core_mask = masks_of(relative, sizes)
    row_base = lax.axis_index("ia") * row_table.shape[0]
    col_base = lax.axis_index("ja") * col_table.shape[0]
    depth_base = lax.axis_index("ka") * depth_blocks

    @pl.when(slot == 0)
    def _():
        second_all[...] = jnp.zeros_like(second_all)
        depth_all[...] = jnp.zeros_like(depth_all)
        depth_sum[...] = jnp.zeros_like(depth_sum)
        rows_out[...] = jnp.zeros_like(rows_out)
        cols_out[...] = jnp.zeros_like(cols_out)
        wide_col[...] = jnp.zeros_like(wide_col)
        width = depth_blocks * slab
        start = pl.multiple_of(lax.axis_index("ka") * width, width)
        depth_turned[...] = factor_depth[:, pl.ds(start, width)].astype(f32).T

    @pl.when(slot < count)
    def _():
        row_at = (coords[0, 0, slot, 0] - row_base) ^ row_mask
        col_at = (coords[0, 0, slot, 1] - col_base) ^ col_mask
        depth_at = coords[0, 0, slot, 2] - depth_base
        row_factor = row_table[row_at]
        row_turned = row_factor.astype(f32).T.astype(bf16)
        col_factor = col_table[col_at]
        wide_col[:rank, :cols] = col_factor
        wide_col[rank:, cols:] = col_factor
        own_depth = depth_turned[pl.ds(pl.multiple_of(depth_at * slab, slab), slab), :]
        depth_all[pl.ds(pl.multiple_of(slot * slab, slab), slab), :] = own_depth.astype(bf16)

        step = 4
        groups = half // step
        wide_factor = wide_col[...]
        for source, target in ((data, spread_data), (weight, spread_weight)):
            for i in range(rows):
                target[i * (slab + 1) : i * (slab + 1) + slab, :] = source[0, i].astype(f32)

        def second_of(g):
            lines = cube[depth_at, g * step * rank : (g + 1) * step * rank, :]
            block = dot(lines, wide_factor).astype(bf16)
            return jnp.concatenate([block[kp * rank : (kp + 1) * rank] for kp in range(step)], axis=1)

        def residual_of(g, model):
            parts = []
            for kp in range(step):
                for h in range(2):
                    lines = pl.ds(h * half + g * step + kp, rows, stride=slab + 1)
                    seen, scale = spread_data[lines, :], spread_weight[lines, :]
                    at = (kp * 2 + h) * cols
                    gap = model[:, at : at + cols] - seen
                    parts.append((scale * gap * resid_scale).astype(bf16))
            return jnp.concatenate(parts, axis=1)

        def keep_back(g, back):
            back = back.astype(bf16)
            for kp in range(step):
                pair = back[:, kp * 2 * cols : (kp + 1) * 2 * cols]
                at = (g * step + kp) * rank
                backward[at : at + rank, :] = pair
                wider = pair.astype(f32)
                for h in range(2):
                    lines = pl.ds(h * half + g * step + kp, rank, stride=slab + 1)
                    by_rank[lines, :] = wider[:, h * cols : (h + 1) * cols]

        row_sum = jnp.zeros((rank, rows), f32)
        seconds = [second_of(g) for g in range(groups)]
        models = [None] * groups
        models[0] = dot(row_turned, seconds[0])
        for g in range(groups):
            if g + 1 < groups:
                models[g + 1] = dot(row_turned, seconds[g + 1])
            residual = residual_of(g, models[g])
            keep_back(g, dot(row_factor, residual))
            row_sum = row_sum + dot(seconds[g], residual, ((1,), (1,)))
        rows_out[row_at] += row_sum
        wide = dot(cube_turned[depth_at], backward[...])
        cols_out[col_at] += wide[:rank, :cols] + wide[rank:, cols:]
        lines = pl.ds(pl.multiple_of(slot * slab, slab), slab)
        for first in range(0, pairs, 8):
            ranked = []
            for pair in range(first, first + 8):
                spots = [at * (slab + 1) for at in (pair, pairs + pair)]
                ranked.append(jnp.concatenate([by_rank[at : at + slab, :].astype(bf16) for at in spots], axis=1))
            ranked = jnp.concatenate(ranked, axis=0)
            second_back = dot(ranked, wide_col[...], ((1,), (1,))).astype(bf16)
            second_all[first : first + 8, lines, :] = second_back.reshape(8, slab, 2 * rank)

    @pl.when(slot == slots - 1)
    def _():
        def one_chunk(at, total):
            pair = at ^ core_mask
            second = second_all[pair]
            both = jnp.concatenate([core[pair], core[pairs + pair]], axis=0)
            total = total + dot(second, both)
            piece = dot(second, depth_all[...], ((0,), (0,)))
            core_out[at] = jnp.concatenate([piece[:rank], piece[rank:]], axis=1)
            return total

        total = lax.fori_loop(0, pairs, one_chunk, jnp.zeros((second_all.shape[1], rank), f32), unroll=16)
        for s in range(second_all.shape[1] // slab):

            @pl.when(s < count)
            def _():
                at = coords[0, 0, s, 2] - depth_base
                lines = pl.ds(pl.multiple_of(at * slab, slab), slab)
                depth_sum[lines, :] += total[s * slab : (s + 1) * slab]

        depth_out[...] = depth_sum[...].T


def terms(relative, sizes, counts, coords, data, weight, cube, cube_turned, row_table, col_table, factor_depth, core):
    slots, rows, slab, cols = data.shape
    rank = core.shape[0]
    half = slab // 2
    depth_blocks = cube.shape[0]

    def live(slot, counts, coords):
        return (jnp.minimum(slot, jnp.maximum(counts[0, 0, 0] - 1, 0)), 0, 0, 0)

    def whole(array):
        return pl.BlockSpec(array.shape, lambda slot, counts, coords: (0,) * len(array.shape))

    outs = (
        jax.ShapeDtypeStruct((rank // 2, rank, 2 * rank), f32),
        jax.ShapeDtypeStruct((row_table.shape[0], rank, rows), f32),
        jax.ShapeDtypeStruct((col_table.shape[0], rank, cols), f32),
        jax.ShapeDtypeStruct((rank, depth_blocks * slab), f32),
    )
    return pl.pallas_call(
        functools.partial(terms_kernel, relative, sizes),
        out_shape=outs,
        grid_spec=pltpu.PrefetchScalarGridSpec(
            num_scalar_prefetch=2,
            grid=(slots,),
            in_specs=[
                pl.BlockSpec((1, rows, slab, cols), live),
                pl.BlockSpec((1, rows, slab, cols), live),
                whole(cube),
                whole(cube_turned),
                whole(row_table),
                whole(col_table),
                whole(factor_depth),
                whole(core),
            ],
            out_specs=[whole(out) for out in outs],
            scratch_shapes=[
                pltpu.VMEM((2 * rank, 2 * cols), bf16),
                pltpu.VMEM((half * rank, 2 * cols), bf16),
                pltpu.VMEM((rank * (slab + 1), cols), f32),
                pltpu.VMEM((rank // 2, slots * slab, 2 * rank), bf16),
                pltpu.VMEM((slots * slab, rank), bf16),
                pltpu.VMEM((depth_blocks * slab, rank), f32),
                pltpu.VMEM((depth_blocks * slab, rank), f32),
                pltpu.VMEM((rows * (slab + 1), cols), f32),
                pltpu.VMEM((rows * (slab + 1), cols), f32),
            ],
        ),
        compiler_params=pltpu.CompilerParams(vmem_limit_bytes=48 * 2**20),
        cost_estimate=pl.CostEstimate(flops=10**9, bytes_accessed=16 * 2**20, transcendentals=0),
        name="terms",
    )(counts, coords, data, weight, cube, cube_turned, row_table, col_table, factor_depth, core)


mark_rows = 16
top_exponent = 14.0


def vmem_call(kernel, out_shape, *operands, name):
    return pl.pallas_call(
        kernel,
        out_shape=out_shape,
        in_specs=[pl.BlockSpec(memory_space=pltpu.VMEM)] * len(operands),
        out_specs=jax.tree.map(lambda _: pl.BlockSpec(memory_space=pltpu.VMEM), out_shape),
        compiler_params=pltpu.CompilerParams(vmem_limit_bytes=24 * 2**20),
        name=name,
    )(*operands)


def power_of(exponent):
    whole = jnp.abs(exponent).astype(jnp.int32)
    value = jnp.ones_like(exponent)
    for bit in range(7):
        factor = jnp.where(exponent < 0, f32(2.0 ** -(2**bit)), f32(2.0 ** (2**bit)))
        value = value * jnp.where((whole >> bit) & 1 == 1, factor, f32(1.0))
    return value


def exponent_of(value):
    lanes = value.shape[-1]
    largest = jnp.max(jnp.max(jnp.abs(value.reshape(-1, 8, lanes)), axis=0), axis=0, keepdims=True)
    largest = jnp.max(largest, axis=1, keepdims=True)
    largest = jnp.broadcast_to(jnp.maximum(largest, f32(1e-30)), (8, lanes))
    return jnp.ceil(jnp.log(largest) * f32(1.4426950408889634)) - f32(top_exponent)


def rounded(value):
    stretched = value * f32(8193.0)
    return stretched - (stretched - value)


def scaled(value):
    exponent = exponent_of(value)
    return rounded(value * power_of(-exponent)[:1]), exponent


def fill_message(out, *parts):
    at = 0
    marks = []
    for part in parts:
        lanes = part.shape[-1]
        flat, exponent = scaled(part.reshape(-1, lanes))
        out[at : at + flat.shape[0], :] = flat
        at += flat.shape[0]
        marks.append(jnp.concatenate([exponent] * (mark_rows // 8), axis=0))
    for mark in marks:
        out[at : at + mark_rows, :] = mark
        at += mark_rows


def message_part(message, start, rows, part, parts):
    mark = message.shape[0] - (parts - part) * mark_rows
    return message[start : start + rows, :] * power_of(message[mark : mark + 8, :])[:1]


def tree_sum(values):
    values = list(values)
    while len(values) > 1:
        values = [values[at] + values[at + 1] for at in range(0, len(values), 2)]
    return values[0]


def after_cores_kernel(n_ia, n_ka, keep, got, cols_sum, own_core, own_depth, *outs):
    messages, columns = outs[: n_ia - 1], outs[n_ia - 1 :]
    half = n_ia * n_ka
    depth = keep[half + n_ka] + got[half + n_ka]
    flat, exponent = scaled(depth)
    own_depth[...] = flat * power_of(exponent)[:1]
    own_core[...] = keep[:n_ka] + got[:n_ka]
    for mask in range(1, n_ia):
        lines = slice(mask * n_ka, (mask + 1) * n_ka)
        fill_message(messages[mask - 1], keep[lines] + got[lines], depth)
    for mask in range(n_ka):
        columns[mask][0] = keep[half + mask] + got[half + mask]
        columns[mask][1] = cols_sum[mask]


def after_cores(n_ia, n_ka, keep, got, cols_sum):
    _, rank, lanes = keep.shape
    message = jax.ShapeDtypeStruct(((n_ka + 1) * rank + 2 * mark_rows, lanes), f32)
    outs = [jax.ShapeDtypeStruct((n_ka, rank, lanes), f32), jax.ShapeDtypeStruct((rank, lanes), f32)]
    outs += [message] * (n_ia - 1) + [jax.ShapeDtypeStruct((2, rank, lanes), f32)] * n_ka
    outs = vmem_call(
        functools.partial(after_cores_kernel, n_ia, n_ka), tuple(outs), keep, got, cols_sum, name="after_cores"
    )
    return outs[0], outs[1], outs[2 : 1 + n_ia], outs[1 + n_ia :]


def after_rows_kernel(own_core, own_depth, *refs):
    *messages, out, depth_out = refs
    count, rank, lanes = own_core.shape
    core = own_core[...].reshape(count * rank, lanes)
    depths = [own_depth[...]]
    for message in messages:
        core = core + message_part(message, 0, count * rank, 0, 2)
        depths.append(message_part(message, count * rank, rank, 1, 2))
    depth_out[...] = tree_sum(depths)
    fill_message(out, core)


def after_rows(own_core, own_depth, messages):
    count, rank, lanes = own_core.shape
    outs = (
        jax.ShapeDtypeStruct((count * rank + mark_rows, lanes), f32),
        jax.ShapeDtypeStruct((rank, lanes), f32),
    )
    return vmem_call(after_rows_kernel, outs, own_core, own_depth, *messages, name="after_rows")


def after_depths_kernel(n_ka, *refs):
    messages, columns, out, rows_out = refs[:n_ka], refs[n_ka : 2 * n_ka], refs[-2], refs[-1]
    _, rank, lanes = columns[0].shape
    cores = []
    for mask, message in enumerate(messages):
        part = message_part(message, 0, n_ka * rank, 0, 1)
        cores.append(jnp.concatenate([part[(at ^ mask) * rank : ((at ^ mask) + 1) * rank] for at in range(n_ka)]))
    core = tree_sum(cores)
    rows_out[...] = tree_sum(column[0] for column in columns)
    fill_message(out, core, tree_sum(column[1] for column in columns))


def after_depths(messages, columns):
    n_ka = len(messages)
    _, rank, lanes = columns[0].shape
    outs = (
        jax.ShapeDtypeStruct(((n_ka + 1) * rank + 2 * mark_rows, lanes), f32),
        jax.ShapeDtypeStruct((rank, lanes), f32),
    )
    return vmem_call(
        functools.partial(after_depths_kernel, n_ka), outs, *messages, *columns, name="after_depths"
    )


def unpack_kernel(sizes, rank, *refs):
    n_ia, n_ka = sizes["ia"], sizes["ka"]
    messages = refs[: 2 * n_ia]
    core_out, cols_out, whole, sems = refs[2 * n_ia :]
    pairs = rank // 2
    own = masks_of(True, sizes)[2]
    copies = []
    for at in range(2 * n_ia):
        first = pl.multiple_of(((own // n_ka) ^ at) * n_ka, n_ka)
        for mask in range(n_ka):
            piece = message_part(messages[at], mask * rank, rank, 0, 2)
            pair = first + (lax.rem(own, n_ka) ^ mask)
            whole[pair] = piece[:, :rank]
            whole[pairs + pair] = piece[:, rank:]
        for h in range(2):
            lines = pl.ds(h * pairs + first, n_ka)
            copies.append(pltpu.make_async_copy(whole.at[lines], core_out.at[lines], sems.at[2 * at + h]))
            copies[-1].start()
    cols_out[...] = tree_sum(message_part(message, n_ka * rank, rank, 1, 2) for message in messages[:n_ia])
    for copy in copies:
        copy.wait()


def unpack(sizes, rank, messages):
    lanes = messages[0].shape[1]
    return pl.pallas_call(
        functools.partial(unpack_kernel, sizes, rank),
        out_shape=(jax.ShapeDtypeStruct((rank, rank, rank), f32), jax.ShapeDtypeStruct((rank, lanes), f32)),
        in_specs=[pl.BlockSpec(memory_space=pltpu.VMEM)] * len(messages),
        out_specs=(pl.BlockSpec(memory_space=pl.ANY), pl.BlockSpec(memory_space=pltpu.VMEM)),
        scratch_shapes=[pltpu.VMEM((rank, rank, rank), f32), pltpu.SemaphoreType.DMA((2 * len(messages),))],
        compiler_params=pltpu.CompilerParams(vmem_limit_bytes=24 * 2**20),
        name="unpack",
    )(*messages)


def power_of_two(n):
    return n & (n - 1) == 0


def swap(value, axis, size, mask):
    return lax.ppermute(value, axis, [(at, at ^ mask) for at in range(size)])


def on_device(sizes, observed, weights, coords, counts, factor_rows, factor_cols, factor_depth, core_tensor):
    n_ia, n_ja, n_ka = sizes["ia"], sizes["ja"], sizes["ka"]
    devices = n_ia * n_ja * n_ka
    rank = core_tensor.shape[0]
    _, _, slots, rows, slab, cols = observed.shape
    data = observed.reshape(observed.shape[2:])
    weight = weights.reshape(weights.shape[2:])
    row_chunks = factor_rows.shape[1] * n_ja * n_ka // rows
    col_chunks = factor_cols.shape[1] * n_ka // cols
    depth_blocks = factor_depth.shape[1] // n_ka // slab
    ia, ja, ka = lax.axis_index("ia"), lax.axis_index("ja"), lax.axis_index("ka")
    by_swaps = (
        n_ja == 2
        and power_of_two(n_ia)
        and power_of_two(n_ka)
        and rank // 2 == devices
        and factor_rows.shape[1] == rows
        and factor_cols.shape[1] == cols
    )

    cube, cube_turned = first_cubes(factor_depth, core_tensor, depth_blocks, slab)

    if by_swaps:
        both = jnp.stack([factor_rows, factor_cols])
        from_ka = [both] + [swap(both, "ka", n_ka, mask) for mask in range(1, n_ka)]
        own_rows = jnp.stack([piece[0] for piece in from_ka])
        row_table = jnp.concatenate([own_rows, swap(own_rows, "ja", n_ja, 1)])
        col_table = jnp.stack([piece[1] for piece in from_ka])
    else:
        row_table = lax.all_gather(factor_rows, ("ja", "ka"), axis=1, tiled=True)
        row_table = row_table.reshape(rank, row_chunks, rows).transpose(1, 0, 2)
        col_table = lax.all_gather(factor_cols, "ka", axis=1, tiled=True)
        col_table = col_table.reshape(rank, col_chunks, cols).transpose(1, 0, 2)

    core_sum, rows_sum, cols_sum, depth_sum = terms(
        by_swaps,
        sizes,
        counts,
        coords,
        data,
        weight,
        cube,
        cube_turned,
        row_table,
        col_table,
        factor_depth,
        core_tensor,
    )

    if not by_swaps:
        rows_whole = rows_sum.transpose(1, 0, 2).reshape(rank, row_chunks * rows)
        cols_whole = cols_sum.transpose(1, 0, 2).reshape(rank, col_chunks * cols)
        core_whole = core_sum.reshape(rank // 2, rank, 2, rank).transpose(2, 0, 1, 3).reshape(rank, rank, rank)
        return (
            lax.psum_scatter(rows_whole, ("ja", "ka"), scatter_dimension=1, tiled=True),
            lax.psum_scatter(lax.psum(cols_whole, "ia"), "ka", scatter_dimension=1, tiled=True),
            lax.psum(depth_sum, ("ia", "ja")),
            lax.psum(core_whole, ("ia", "ja", "ka")),
        )

    half = devices // 2
    keep = jnp.concatenate([core_sum[:half], rows_sum[:n_ka], depth_sum[None]])
    send = jnp.concatenate([core_sum[half:], rows_sum[n_ka:], depth_sum[None]])
    got = swap(send, "ja", n_ja, 1)
    own_core, own_depth, messages, columns = after_cores(n_ia, n_ka, keep, got, cols_sum)
    messages = [swap(message.astype(wire), "ia", n_ia, at + 1).astype(f32) for at, message in enumerate(messages)]
    columns = [columns[0]] + [swap(columns[mask], "ka", n_ka, mask) for mask in range(1, n_ka)]
    message, depth_total = after_rows(own_core, own_depth, messages)
    sent = message.astype(wire)
    messages = [message] + [swap(sent, "ka", n_ka, mask).astype(f32) for mask in range(1, n_ka)]
    message, rows_total = after_depths(messages, columns)
    sent = message.astype(wire)
    sent = [sent] + [swap(sent, "ia", n_ia, mask) for mask in range(1, n_ia)]
    sent = sent + [swap(each, "ja", n_ja, 1) for each in sent]
    core_total, cols_total = unpack(sizes, rank, [each.astype(f32) for each in sent])
    return (rows_total, cols_total, depth_total, core_total)


def solution(mesh):
    in_specs = (
        P("ia", "ja", "ka", None, None, None),
        P("ia", "ja", "ka", None, None, None),
        P("ia", "ja", "ka", None),
        P("ia", "ja", "ka"),
        P(None, ("ia", "ja", "ka")),
        P(None, ("ja", "ka")),
        P(),
        P(),
    )
    out_specs = (P(None, ("ia", "ja", "ka")), P(None, ("ja", "ka")), P(None, "ka"), P())
    return jax.shard_map(
        functools.partial(on_device, dict(mesh.shape)),
        mesh=mesh,
        in_specs=in_specs,
        out_specs=out_specs,
        check_vma=False,
    )
```

```python
import functools

import jax
import jax.numpy as jnp
from jax import lax
from jax.experimental import pallas as pl
from jax.experimental.pallas import tpu as pltpu
from jax.sharding import PartitionSpec as P

resid_scale = 1.0 / 64.0
f32 = jnp.float32
bf16 = jnp.bfloat16
wire = jnp.float16


def dot(a, b, contract=((1,), (0,))):
    return lax.dot_general(a, b, (contract, ((), ())), preferred_element_type=f32)


def cube_kernel(
    depth_blocks,
    slab,
    after,
    factor_depth,
    core,
    cube_out,
    cube_turned_out,
    core_out,
    depth_out,
    depth_here,
    core_here,
    cube_wide,
    sems,
):
    rank = core.shape[0]
    half = slab // 2
    pairs = rank // 2
    width = depth_blocks * slab
    start = pl.multiple_of(lax.axis_index("ka") * width, width)
    core_copy = pltpu.make_async_copy(core, core_here, sems.at[0])
    core_copy.start()
    depth_copy = pltpu.make_async_copy(factor_depth.at[:, pl.ds(start, width)], depth_here, sems.at[1])
    depth_copy.start()
    depth_copy.wait()
    depth = depth_here[...].astype(f32).T
    depth_out[...] = depth.astype(bf16)
    order = [depth[t * slab + h * half : t * slab + (h + 1) * half] for h in range(2) for t in range(depth_blocks)]
    depth = jnp.concatenate(order, axis=0).astype(bf16)
    count = depth_blocks * half
    core_copy.wait()

    def one_rank(r1, carry):
        piece = dot(depth, core_here[r1], ((1,), (1,)))
        wide = jnp.concatenate([piece[:count], piece[count:]], axis=1)
        cube_wide[pl.ds(r1, count, stride=rank + 1), :] = wide
        return carry

    lax.fori_loop(0, rank, one_rank, 0, unroll=16)
    for pair in range(pairs):
        core_out[pair] = jnp.concatenate([core_here[pair], core_here[pairs + pair]], axis=0)
    for t in range(depth_blocks):
        for kp in range(half):
            at = (t * half + kp) * (rank + 1)
            block = cube_wide[at : at + rank, :]
            cube_out[t, kp * rank : (kp + 1) * rank, :] = block.astype(bf16)
        cube_turned_out[t] = cube_out[t].astype(f32).T.astype(bf16)


def first_cubes(after, factor_depth, core, depth_blocks, slab):
    rank = core.shape[0]
    half = slab // 2
    width = depth_blocks * slab
    return pl.pallas_call(
        functools.partial(cube_kernel, depth_blocks, slab),
        out_shape=(
            jax.ShapeDtypeStruct((depth_blocks, half * rank, 2 * rank), bf16),
            jax.ShapeDtypeStruct((depth_blocks, 2 * rank, half * rank), bf16),
            jax.ShapeDtypeStruct((rank // 2, 2 * rank, rank), bf16),
            jax.ShapeDtypeStruct((width, rank), bf16),
        ),
        in_specs=[pl.BlockSpec(memory_space=pl.ANY)] + [pl.BlockSpec(memory_space=pltpu.HBM)] * 2,
        out_specs=[pl.BlockSpec(memory_space=pltpu.VMEM)] * 4,
        scratch_shapes=[
            pltpu.VMEM((rank, width), bf16),
            pltpu.VMEM(core.shape, bf16),
            pltpu.VMEM((depth_blocks * half * (rank + 1), 2 * rank), f32),
            pltpu.SemaphoreType.DMA((2,)),
        ],
        compiler_params=pltpu.CompilerParams(vmem_limit_bytes=24 * 2**20),
        cost_estimate=pl.CostEstimate(flops=10**9, bytes_accessed=4 * 2**20, transcendentals=0),
        name="first_cubes",
    )(after, factor_depth, core)


def masks_of(relative, sizes):
    ia, ja, ka = lax.axis_index("ia"), lax.axis_index("ja"), lax.axis_index("ka")
    if not relative:
        return 0, 0, 0
    return ja * sizes["ka"] + ka, ka, (ja * sizes["ia"] + ia) * sizes["ka"] + ka


def terms_kernel(relative, sizes, row_spots, col_spots, counts, coords, data, weight, cube, cube_turned, *refs):
    pieces = refs[: 1 + max(at for at, _ in row_spots + col_spots)]
    (
        core,
        depth_turned,
        core_out,
        rows_out,
        cols_out,
        depth_out,
        row_table,
        col_table,
        wide_col,
        backward,
        by_rank,
        second_all,
        depth_all,
        depth_sum,
        spread_data,
        spread_weight,
    ) = refs[len(pieces) :]
    slot = pl.program_id(0)
    slots = pl.num_programs(0)
    _, rows, slab, cols = data.shape
    pairs = core.shape[0]
    rank = 2 * pairs
    half = slab // 2
    depth_blocks = cube.shape[0]
    count = counts[0, 0, 0]
    row_mask, col_mask, core_mask = masks_of(relative, sizes)
    row_base = lax.axis_index("ia") * row_table.shape[0]
    col_base = lax.axis_index("ja") * col_table.shape[0]
    depth_base = lax.axis_index("ka") * depth_blocks

    @pl.when(slot == 0)
    def _():
        second_all[...] = jnp.zeros_like(second_all)
        depth_all[...] = jnp.zeros_like(depth_all)
        depth_sum[...] = jnp.zeros_like(depth_sum)
        rows_out[...] = jnp.zeros_like(rows_out)
        cols_out[...] = jnp.zeros_like(cols_out)
        wide_col[...] = jnp.zeros_like(wide_col)
        for spots, table in ((row_spots, row_table), (col_spots, col_table)):
            for at, (piece, line) in enumerate(spots):
                table[at] = pieces[piece][line]

    @pl.when(slot < count)
    def _():
        row_at = (coords[0, 0, slot, 0] - row_base) ^ row_mask
        col_at = (coords[0, 0, slot, 1] - col_base) ^ col_mask
        depth_at = coords[0, 0, slot, 2] - depth_base
        row_factor = row_table[row_at]
        row_turned = row_factor.astype(f32).T.astype(bf16)
        col_factor = col_table[col_at]
        wide_col[:rank, :cols] = col_factor
        wide_col[rank:, cols:] = col_factor
        own_depth = depth_turned[pl.ds(pl.multiple_of(depth_at * slab, slab), slab), :]
        depth_all[pl.ds(pl.multiple_of(slot * slab, slab), slab), :] = own_depth

        step = 4
        groups = half // step
        wide_factor = wide_col[...]
        for source, target in ((data, spread_data), (weight, spread_weight)):
            for i in range(rows):
                target[i * (slab + 1) : i * (slab + 1) + slab, :] = source[0, i].astype(f32)

        def second_of(g):
            lines = cube[depth_at, g * step * rank : (g + 1) * step * rank, :]
            block = dot(lines, wide_factor).astype(bf16)
            return jnp.concatenate([block[kp * rank : (kp + 1) * rank] for kp in range(step)], axis=1)

        def residual_of(g, model):
            parts = []
            for kp in range(step):
                for h in range(2):
                    lines = pl.ds(h * half + g * step + kp, rows, stride=slab + 1)
                    seen, scale = spread_data[lines, :], spread_weight[lines, :]
                    at = (kp * 2 + h) * cols
                    gap = model[:, at : at + cols] - seen
                    parts.append((scale * gap * resid_scale).astype(bf16))
            return jnp.concatenate(parts, axis=1)

        def keep_back(g, back):
            back = back.astype(bf16)
            for kp in range(step):
                pair = back[:, kp * 2 * cols : (kp + 1) * 2 * cols]
                at = (g * step + kp) * rank
                backward[at : at + rank, :] = pair
                wider = pair.astype(f32)
                for h in range(2):
                    lines = pl.ds(h * half + g * step + kp, rank, stride=slab + 1)
                    by_rank[lines, :] = wider[:, h * cols : (h + 1) * cols]

        row_sum = jnp.zeros((rank, rows), f32)
        seconds = [second_of(g) for g in range(groups)]
        models = [None] * groups
        models[0] = dot(row_turned, seconds[0])
        for g in range(groups):
            if g + 1 < groups:
                models[g + 1] = dot(row_turned, seconds[g + 1])
            residual = residual_of(g, models[g])
            keep_back(g, dot(row_factor, residual))
            row_sum = row_sum + dot(seconds[g], residual, ((1,), (1,)))
        rows_out[row_at] += row_sum
        wide = dot(cube_turned[depth_at], backward[...])
        cols_out[col_at] += wide[:rank, :cols] + wide[rank:, cols:]
        lines = pl.ds(pl.multiple_of(slot * slab, slab), slab)
        for first in range(0, pairs, 8):
            ranked = []
            for pair in range(first, first + 8):
                spots = [at * (slab + 1) for at in (pair, pairs + pair)]
                ranked.append(jnp.concatenate([by_rank[at : at + slab, :].astype(bf16) for at in spots], axis=1))
            ranked = jnp.concatenate(ranked, axis=0)
            second_back = dot(ranked, wide_col[...], ((1,), (1,))).astype(bf16)
            second_all[first : first + 8, lines, :] = second_back.reshape(8, slab, 2 * rank)

    @pl.when(slot == slots - 1)
    def _():
        def one_chunk(at, total):
            pair = at ^ core_mask
            second = second_all[pair]
            total = total + dot(second, core[pair])
            piece = dot(second, depth_all[...], ((0,), (0,)))
            core_out[at] = jnp.concatenate([piece[:rank], piece[rank:]], axis=1)
            return total

        total = lax.fori_loop(0, pairs, one_chunk, jnp.zeros((second_all.shape[1], rank), f32), unroll=16)
        for s in range(second_all.shape[1] // slab):

            @pl.when(s < count)
            def _():
                at = coords[0, 0, s, 2] - depth_base
                lines = pl.ds(pl.multiple_of(at * slab, slab), slab)
                depth_sum[lines, :] += total[s * slab : (s + 1) * slab]

        depth_out[...] = depth_sum[...].T


def terms(relative, sizes, row_spots, col_spots, counts, coords, data, weight, cube, cube_turned, pieces, core, depth):
    slots, rows, slab, cols = data.shape
    rank = core.shape[2]
    half = slab // 2
    depth_blocks = cube.shape[0]

    def live(slot, counts, coords):
        return (jnp.minimum(slot, jnp.maximum(counts[0, 0, 0] - 1, 0)), 0, 0, 0)

    def whole(array):
        return pl.BlockSpec(array.shape, lambda slot, counts, coords: (0,) * len(array.shape))

    outs = (
        jax.ShapeDtypeStruct((rank // 2, rank, 2 * rank), f32),
        jax.ShapeDtypeStruct((len(row_spots), rank, rows), f32),
        jax.ShapeDtypeStruct((len(col_spots), rank, cols), f32),
        jax.ShapeDtypeStruct((rank, depth_blocks * slab), f32),
    )
    return pl.pallas_call(
        functools.partial(terms_kernel, relative, sizes, row_spots, col_spots),
        out_shape=outs,
        grid_spec=pltpu.PrefetchScalarGridSpec(
            num_scalar_prefetch=2,
            grid=(slots,),
            in_specs=[
                pl.BlockSpec((1, rows, slab, cols), live),
                pl.BlockSpec((1, rows, slab, cols), live),
                whole(cube),
                whole(cube_turned),
                *[whole(piece) for piece in pieces],
                whole(core),
                whole(depth),
            ],
            out_specs=[whole(out) for out in outs],
            scratch_shapes=[
                pltpu.VMEM((len(row_spots), rank, rows), bf16),
                pltpu.VMEM((len(col_spots), rank, cols), bf16),
                pltpu.VMEM((2 * rank, 2 * cols), bf16),
                pltpu.VMEM((half * rank, 2 * cols), bf16),
                pltpu.VMEM((rank * (slab + 1), cols), f32),
                pltpu.VMEM((rank // 2, slots * slab, 2 * rank), bf16),
                pltpu.VMEM((slots * slab, rank), bf16),
                pltpu.VMEM((depth_blocks * slab, rank), f32),
                pltpu.VMEM((rows * (slab + 1), cols), f32),
                pltpu.VMEM((rows * (slab + 1), cols), f32),
            ],
        ),
        compiler_params=pltpu.CompilerParams(vmem_limit_bytes=48 * 2**20),
        cost_estimate=pl.CostEstimate(flops=10**9, bytes_accessed=16 * 2**20, transcendentals=0),
        name="terms",
    )(counts, coords, data, weight, cube, cube_turned, *pieces, core, depth)


mark_rows = 16
top_exponent = 14.0


def vmem_call(kernel, out_shape, *operands, name):
    return pl.pallas_call(
        kernel,
        out_shape=out_shape,
        in_specs=[pl.BlockSpec(memory_space=pltpu.VMEM)] * len(operands),
        out_specs=jax.tree.map(lambda _: pl.BlockSpec(memory_space=pltpu.VMEM), out_shape),
        compiler_params=pltpu.CompilerParams(vmem_limit_bytes=24 * 2**20),
        name=name,
    )(*operands)


def power_of(exponent):
    whole = jnp.abs(exponent).astype(jnp.int32)
    value = jnp.ones_like(exponent)
    for bit in range(7):
        factor = jnp.where(exponent < 0, f32(2.0 ** -(2**bit)), f32(2.0 ** (2**bit)))
        value = value * jnp.where((whole >> bit) & 1 == 1, factor, f32(1.0))
    return value


def exponent_of(value):
    lanes = value.shape[-1]
    largest = jnp.max(jnp.max(jnp.abs(value.reshape(-1, 8, lanes)), axis=0), axis=0, keepdims=True)
    largest = jnp.max(largest, axis=1, keepdims=True)
    largest = jnp.broadcast_to(jnp.maximum(largest, f32(1e-30)), (8, lanes))
    return jnp.ceil(jnp.log(largest) * f32(1.4426950408889634)) - f32(top_exponent)


def rounded(value):
    stretched = value * f32(8193.0)
    return stretched - (stretched - value)


def scaled(value):
    exponent = exponent_of(value)
    return rounded(value * power_of(-exponent)[:1]), exponent


def fill_message(out, *parts):
    at = 0
    mark = None
    for which, part in enumerate(parts):
        lanes = part.shape[-1]
        flat, exponent = scaled(part.reshape(-1, lanes))
        out[at : at + flat.shape[0], :] = flat
        at += flat.shape[0]
        exponent = jnp.broadcast_to(exponent[:1], (mark_rows, lanes))
        line = lax.broadcasted_iota(jnp.int32, exponent.shape, 0)
        mark = exponent if mark is None else jnp.where(line >= which, exponent, mark)
    out[at : at + mark_rows, :] = mark


def message_part(message, start, rows, part):
    mark = message.shape[0] - mark_rows + part
    return message[start : start + rows, :] * power_of(message[mark : mark + 1, :])


def message_shape(chunks, rank, lanes):
    return jax.ShapeDtypeStruct((chunks * rank + mark_rows, lanes), f32)


def tree_sum(values):
    values = list(values)
    while len(values) > 1:
        values = [values[at] + values[at + 1] for at in range(0, len(values), 2)]
    return values[0]


def after_cores_kernel(n_ia, n_ka, keep, got, own_core, own_depth, own_rows, *messages):
    half = n_ia * n_ka
    depth = keep[half + n_ka] + got[half + n_ka]
    flat, exponent = scaled(depth)
    own_depth[...] = flat * power_of(exponent)[:1]
    own_core[...] = keep[:n_ka] + got[:n_ka]
    own_rows[...] = keep[half : half + n_ka] + got[half : half + n_ka]
    for mask in range(1, n_ia):
        lines = slice(mask * n_ka, (mask + 1) * n_ka)
        fill_message(messages[mask - 1], keep[lines] + got[lines], depth)


def after_cores(n_ia, n_ka, keep, got):
    _, rank, lanes = keep.shape
    outs = [jax.ShapeDtypeStruct(shape, f32) for shape in ((n_ka, rank, lanes), (rank, lanes), (n_ka, rank, lanes))]
    outs += [message_shape(n_ka + 1, rank, lanes)] * (n_ia - 1)
    outs = vmem_call(functools.partial(after_cores_kernel, n_ia, n_ka), tuple(outs), keep, got, name="after_cores")
    return outs[0], outs[1], outs[2], outs[3:]


def after_rows_kernel(n_ia, n_ka, own_core, own_depth, own_rows, cols_sum, *refs):
    messages, depth_out, outs = refs[: n_ia - 1], refs[n_ia - 1], refs[n_ia:]
    count, rank, lanes = own_core.shape
    core = own_core[...].reshape(count * rank, lanes)
    depths = [own_depth[...]]
    for message in messages:
        core = core + message_part(message, 0, count * rank, 0)
        depths.append(message_part(message, count * rank, rank, 1))
    depth_out[...] = tree_sum(depths)
    for mask in range(n_ka):
        fill_message(outs[mask], core, own_rows[mask], cols_sum[mask])


def after_rows(n_ia, n_ka, own_core, own_depth, own_rows, cols_sum, messages):
    count, rank, lanes = own_core.shape
    outs = (jax.ShapeDtypeStruct((rank, lanes), f32),) + (message_shape(count + 2, rank, lanes),) * n_ka
    outs = vmem_call(
        functools.partial(after_rows_kernel, n_ia, n_ka),
        outs,
        own_core,
        own_depth,
        own_rows,
        cols_sum,
        *messages,
        name="after_rows",
    )
    return outs[0], outs[1:]


def after_depths_kernel(n_ka, rank, *refs):
    messages, out, rows_out = refs[:n_ka], refs[-2], refs[-1]
    cores = []
    for mask, message in enumerate(messages):
        part = message_part(message, 0, n_ka * rank, 0)
        cores.append(jnp.concatenate([part[(at ^ mask) * rank : ((at ^ mask) + 1) * rank] for at in range(n_ka)]))
    rows_out[...] = tree_sum(message_part(message, n_ka * rank, rank, 1) for message in messages)
    cols = tree_sum(message_part(message, (n_ka + 1) * rank, rank, 2) for message in messages)
    fill_message(out, tree_sum(cores), cols)


def after_depths(n_ka, rank, messages):
    lanes = messages[0].shape[1]
    outs = (message_shape(n_ka + 1, rank, lanes), jax.ShapeDtypeStruct((rank, lanes), f32))
    return vmem_call(functools.partial(after_depths_kernel, n_ka, rank), outs, *messages, name="after_depths")


def unpack_kernel(sizes, rank, first_message, *refs):
    n_ia, n_ka = sizes["ia"], sizes["ka"]
    messages = refs[:n_ia]
    core_out, *cols_out, whole, sems = refs[n_ia if first_message == 0 else n_ia + 1 :]
    pairs = rank // 2
    own = masks_of(True, sizes)[2]
    copies = []
    for at in range(n_ia):
        first = pl.multiple_of(((own // n_ka) ^ (first_message + at)) * n_ka, n_ka)
        for mask in range(n_ka):
            piece = message_part(messages[at], mask * rank, rank, 0)
            line = lax.rem(own, n_ka) ^ mask
            whole[at, 0, line] = piece[:, :rank]
            whole[at, 1, line] = piece[:, rank:]
        for h in range(2):
            lines = pl.ds(h * pairs + first, n_ka)
            copies.append(pltpu.make_async_copy(whole.at[at, h], core_out.at[lines], sems.at[2 * at + h]))
            copies[-1].start()
    for out in cols_out:
        out[...] = tree_sum(message_part(message, n_ka * rank, rank, 1) for message in messages)
    for copy in copies:
        copy.wait()


def unpack(sizes, rank, messages, core=None):
    lanes = messages[0].shape[1]
    near = core is None
    out_shape = [jax.ShapeDtypeStruct((rank, rank, rank), f32)]
    out_specs = [pl.BlockSpec(memory_space=pltpu.HBM)]
    if near:
        out_shape.append(jax.ShapeDtypeStruct((rank, lanes), f32))
        out_specs.append(pl.BlockSpec(memory_space=pltpu.VMEM))
    return pl.pallas_call(
        functools.partial(unpack_kernel, sizes, rank, 0 if near else sizes["ia"]),
        out_shape=tuple(out_shape),
        in_specs=[pl.BlockSpec(memory_space=pltpu.VMEM)] * len(messages)
        + ([] if near else [pl.BlockSpec(memory_space=pltpu.HBM)]),
        out_specs=tuple(out_specs),
        scratch_shapes=[
            pltpu.VMEM((len(messages), 2, sizes["ka"], rank, rank), f32),
            pltpu.SemaphoreType.DMA((2 * len(messages),)),
        ],
        input_output_aliases={} if near else {len(messages): 0},
        compiler_params=pltpu.CompilerParams(vmem_limit_bytes=24 * 2**20),
        cost_estimate=pl.CostEstimate(flops=10**6, bytes_accessed=4 * 2**20, transcendentals=0),
        name="unpack_near" if near else "unpack_far",
    )(*messages, *([] if near else [core]))


def power_of_two(n):
    return n & (n - 1) == 0


def swap(value, axis, size, mask):
    return lax.ppermute(value, axis, [(at, at ^ mask) for at in range(size)])


def on_device(sizes, observed, weights, coords, counts, factor_rows, factor_cols, factor_depth, core_tensor):
    n_ia, n_ja, n_ka = sizes["ia"], sizes["ja"], sizes["ka"]
    devices = n_ia * n_ja * n_ka
    rank = core_tensor.shape[0]
    _, _, slots, rows, slab, cols = observed.shape
    data = observed.reshape(observed.shape[2:])
    weight = weights.reshape(weights.shape[2:])
    row_chunks = factor_rows.shape[1] * n_ja * n_ka // rows
    col_chunks = factor_cols.shape[1] * n_ka // cols
    depth_blocks = factor_depth.shape[1] // n_ka // slab
    ia, ja, ka = lax.axis_index("ia"), lax.axis_index("ja"), lax.axis_index("ka")
    by_swaps = (
        n_ja == 2
        and power_of_two(n_ia)
        and power_of_two(n_ka)
        and rank // 2 == devices
        and factor_rows.shape[1] == rows
        and factor_cols.shape[1] == cols
    )

    if by_swaps:
        own = jnp.stack([factor_rows, swap(factor_rows, "ja", n_ja, 1), factor_cols])
        pieces = [own] + [swap(own, "ka", n_ka, mask) for mask in range(1, n_ka)]
        row_spots = [(mask, line) for line in range(n_ja) for mask in range(n_ka)]
        col_spots = [(mask, n_ja) for mask in range(n_ka)]
    else:
        row_table = lax.all_gather(factor_rows, ("ja", "ka"), axis=1, tiled=True)
        row_table = row_table.reshape(rank, row_chunks, rows).transpose(1, 0, 2)
        col_table = lax.all_gather(factor_cols, "ka", axis=1, tiled=True)
        col_table = col_table.reshape(rank, col_chunks, cols).transpose(1, 0, 2)
        pieces = [row_table, col_table]
        row_spots = [(0, line) for line in range(row_chunks)]
        col_spots = [(1, line) for line in range(col_chunks)]

    cube, cube_turned, core_pairs, own_depth = first_cubes(pieces[0], factor_depth, core_tensor, depth_blocks, slab)
    core_sum, rows_sum, cols_sum, depth_sum = terms(
        by_swaps,
        sizes,
        row_spots,
        col_spots,
        counts,
        coords,
        data,
        weight,
        cube,
        cube_turned,
        pieces,
        core_pairs,
        own_depth,
    )

    if not by_swaps:
        rows_whole = rows_sum.transpose(1, 0, 2).reshape(rank, row_chunks * rows)
        cols_whole = cols_sum.transpose(1, 0, 2).reshape(rank, col_chunks * cols)
        core_whole = core_sum.reshape(rank // 2, rank, 2, rank).transpose(2, 0, 1, 3).reshape(rank, rank, rank)
        return (
            lax.psum_scatter(rows_whole, ("ja", "ka"), scatter_dimension=1, tiled=True),
            lax.psum_scatter(lax.psum(cols_whole, "ia"), "ka", scatter_dimension=1, tiled=True),
            lax.psum(depth_sum, ("ia", "ja")),
            lax.psum(core_whole, ("ia", "ja", "ka")),
        )

    half = devices // 2
    keep = jnp.concatenate([core_sum[:half], rows_sum[:n_ka], depth_sum[None]])
    send = jnp.concatenate([core_sum[half:], rows_sum[n_ka:], depth_sum[None]])
    got = swap(send, "ja", n_ja, 1)
    own_core, own_depth, own_rows, messages = after_cores(n_ia, n_ka, keep, got)
    messages = [swap(message.astype(wire), "ia", n_ia, at + 1).astype(f32) for at, message in enumerate(messages)]
    depth_total, messages = after_rows(n_ia, n_ka, own_core, own_depth, own_rows, cols_sum, messages)
    messages = [messages[0]] + [
        swap(messages[mask].astype(wire), "ka", n_ka, mask).astype(f32) for mask in range(1, n_ka)
    ]
    message, rows_total = after_depths(n_ka, rank, messages)
    sent = message.astype(wire)
    sent = [sent] + [swap(sent, "ia", n_ia, mask) for mask in range(1, n_ia)]
    other = [swap(each, "ja", n_ja, 1) for each in sent]
    core_near, cols_total = unpack(sizes, rank, [each.astype(f32) for each in sent])
    (core_total,) = unpack(sizes, rank, [each.astype(f32) for each in other], core_near)
    return (rows_total, cols_total, depth_total, core_total)


def solution(mesh):
    in_specs = (
        P("ia", "ja", "ka", None, None, None),
        P("ia", "ja", "ka", None, None, None),
        P("ia", "ja", "ka", None),
        P("ia", "ja", "ka"),
        P(None, ("ia", "ja", "ka")),
        P(None, ("ja", "ka")),
        P(),
        P(),
    )
    out_specs = (P(None, ("ia", "ja", "ka")), P(None, ("ja", "ka")), P(None, "ka"), P())
    return jax.shard_map(
        functools.partial(on_device, dict(mesh.shape)),
        mesh=mesh,
        in_specs=in_specs,
        out_specs=out_specs,
        check_vma=False,
    )
```

```python
import functools

import jax
import jax.numpy as jnp
from jax import lax
from jax.experimental import pallas as pl
from jax.experimental.pallas import tpu as pltpu
from jax.sharding import PartitionSpec as P

resid_scale = 1.0 / 64.0
f32 = jnp.float32
bf16 = jnp.bfloat16
wire = jnp.float16


def dot(a, b, contract=((1,), (0,))):
    return lax.dot_general(a, b, (contract, ((), ())), preferred_element_type=f32)


def spread_out(source, target):
    rows, slab, _ = source.shape
    for i in range(rows):
        target[i * (slab + 1) : i * (slab + 1) + slab, :] = source[i].astype(f32)


def cube_kernel(
    depth_blocks,
    slab,
    after,
    factor_depth,
    core,
    data,
    weight,
    cube_out,
    cube_turned_out,
    core_out,
    depth_out,
    spread,
    depth_here,
    core_here,
    fetched,
    cube_wide,
    sems,
):
    rank = core.shape[0]
    half = slab // 2
    pairs = rank // 2
    width = depth_blocks * slab
    start = pl.multiple_of(lax.axis_index("ka") * width, width)
    copies = [
        pltpu.make_async_copy(source.at[0], fetched.at[at], sems.at[2 + at]) for at, source in enumerate((data, weight))
    ]
    core_copy = pltpu.make_async_copy(core, core_here, sems.at[0])
    core_copy.start()
    depth_copy = pltpu.make_async_copy(factor_depth.at[:, pl.ds(start, width)], depth_here, sems.at[1])
    depth_copy.start()
    for copy in copies:
        copy.start()
    depth_copy.wait()
    depth = depth_here[...].astype(f32).T
    depth_out[...] = depth.astype(bf16)
    order = [depth[t * slab + h * half : t * slab + (h + 1) * half] for h in range(2) for t in range(depth_blocks)]
    depth = jnp.concatenate(order, axis=0).astype(bf16)
    count = depth_blocks * half
    core_copy.wait()

    def one_rank(r1, carry):
        piece = dot(depth, core_here[r1], ((1,), (1,)))
        wide = jnp.concatenate([piece[:count], piece[count:]], axis=1)
        cube_wide[pl.ds(r1, count, stride=rank + 1), :] = wide
        return carry

    lax.fori_loop(0, rank, one_rank, 0, unroll=16)
    for pair in range(pairs):
        core_out[pair] = jnp.concatenate([core_here[pair], core_here[pairs + pair]], axis=0)
    for t in range(depth_blocks):
        for kp in range(half):
            at = (t * half + kp) * (rank + 1)
            block = cube_wide[at : at + rank, :]
            cube_out[t, kp * rank : (kp + 1) * rank, :] = block.astype(bf16)
        cube_turned_out[t] = cube_out[t].astype(f32).T.astype(bf16)
    for at, copy in enumerate(copies):
        copy.wait()
        spread_out(fetched.at[at], spread.at[at])


def first_cubes(after, factor_depth, core, data, weight, depth_blocks):
    rank = core.shape[0]
    _, rows, slab, cols = data.shape
    half = slab // 2
    width = depth_blocks * slab
    return pl.pallas_call(
        functools.partial(cube_kernel, depth_blocks, slab),
        out_shape=(
            jax.ShapeDtypeStruct((depth_blocks, half * rank, 2 * rank), bf16),
            jax.ShapeDtypeStruct((depth_blocks, 2 * rank, half * rank), bf16),
            jax.ShapeDtypeStruct((rank // 2, 2 * rank, rank), bf16),
            jax.ShapeDtypeStruct((width, rank), bf16),
            jax.ShapeDtypeStruct((2, rows * (slab + 1), cols), f32),
        ),
        in_specs=[pl.BlockSpec(memory_space=pl.ANY)] + [pl.BlockSpec(memory_space=pltpu.HBM)] * 4,
        out_specs=[pl.BlockSpec(memory_space=pltpu.VMEM)] * 5,
        scratch_shapes=[
            pltpu.VMEM((rank, width), bf16),
            pltpu.VMEM(core.shape, bf16),
            pltpu.VMEM((2, rows, slab, cols), bf16),
            pltpu.VMEM((depth_blocks * half * (rank + 1), 2 * rank), f32),
            pltpu.SemaphoreType.DMA((4,)),
        ],
        compiler_params=pltpu.CompilerParams(vmem_limit_bytes=40 * 2**20),
        cost_estimate=pl.CostEstimate(flops=10**9, bytes_accessed=4 * 2**20, transcendentals=0),
        name="first_cubes",
    )(after, factor_depth, core, data, weight)


def masks_of(relative, sizes):
    ia, ja, ka = lax.axis_index("ia"), lax.axis_index("ja"), lax.axis_index("ka")
    if not relative:
        return 0, 0, 0
    return ja * sizes["ka"] + ka, ka, (ja * sizes["ia"] + ia) * sizes["ka"] + ka


def terms_kernel(relative, sizes, row_spots, col_spots, counts, coords, data, weight, cube, cube_turned, *refs):
    pieces = refs[: 1 + max(at for at, _ in row_spots + col_spots)]
    (
        core,
        depth_turned,
        _,
        core_out,
        rows_out,
        cols_out,
        depth_out,
        spread,
        row_table,
        col_table,
        wide_col,
        backward,
        by_rank,
        second_all,
        depth_all,
        depth_sum,
        fetched,
        sems,
    ) = refs[len(pieces) :]
    slots, rows, slab, cols = data.shape
    pairs = core.shape[0]
    rank = 2 * pairs
    half = slab // 2
    depth_blocks = cube.shape[0]
    count = counts[0, 0, 0]
    row_mask, col_mask, core_mask = masks_of(relative, sizes)
    row_base = lax.axis_index("ia") * row_table.shape[0]
    col_base = lax.axis_index("ja") * col_table.shape[0]
    depth_base = lax.axis_index("ka") * depth_blocks

    def fetches(slot):
        side = lax.rem(slot, 2)
        return [
            pltpu.make_async_copy(source.at[slot], fetched.at[side, which], sems.at[side, which])
            for which, source in enumerate((data, weight))
        ]

    def fetch(slot):
        @pl.when(slot < count)
        def _():
            for copy in fetches(slot):
                copy.start()

    def arrive(slot):
        for copy in fetches(slot):
            copy.wait()

    second_all[...] = jnp.zeros_like(second_all)
    depth_all[...] = jnp.zeros_like(depth_all)
    depth_sum[...] = jnp.zeros_like(depth_sum)
    rows_out[...] = jnp.zeros_like(rows_out)
    cols_out[...] = jnp.zeros_like(cols_out)
    wide_col[...] = jnp.zeros_like(wide_col)
    for spots, table in ((row_spots, row_table), (col_spots, col_table)):
        for at, (piece, line) in enumerate(spots):
            table[at] = pieces[piece][line]

    def one_slot(slot, carry):
        fetch(slot + 1)

        @pl.when(slot > 0)
        def _():
            arrive(slot)
            for which in range(2):
                spread_out(fetched.at[lax.rem(slot, 2), which], spread.at[which])

        row_at = (coords[0, 0, slot, 0] - row_base) ^ row_mask
        col_at = (coords[0, 0, slot, 1] - col_base) ^ col_mask
        depth_at = coords[0, 0, slot, 2] - depth_base
        row_factor = row_table[row_at]
        row_turned = row_factor.astype(f32).T.astype(bf16)
        col_factor = col_table[col_at]
        wide_col[:rank, :cols] = col_factor
        wide_col[rank:, cols:] = col_factor
        own_depth = depth_turned[pl.ds(pl.multiple_of(depth_at * slab, slab), slab), :]
        depth_all[pl.ds(pl.multiple_of(slot * slab, slab), slab), :] = own_depth

        step = 4
        groups = half // step
        wide_factor = wide_col[...]
        def second_of(g):
            lines = cube[depth_at, g * step * rank : (g + 1) * step * rank, :]
            block = dot(lines, wide_factor).astype(bf16)
            return jnp.concatenate([block[kp * rank : (kp + 1) * rank] for kp in range(step)], axis=1)

        def residual_of(g, model):
            parts = []
            for kp in range(step):
                for h in range(2):
                    lines = pl.ds(h * half + g * step + kp, rows, stride=slab + 1)
                    seen, scale = spread[0, lines, :], spread[1, lines, :]
                    at = (kp * 2 + h) * cols
                    gap = model[:, at : at + cols] - seen
                    parts.append((scale * gap * resid_scale).astype(bf16))
            return jnp.concatenate(parts, axis=1)

        def keep_back(g, back):
            back = back.astype(bf16)
            for kp in range(step):
                pair = back[:, kp * 2 * cols : (kp + 1) * 2 * cols]
                at = (g * step + kp) * rank
                backward[at : at + rank, :] = pair
                wider = pair.astype(f32)
                for h in range(2):
                    lines = pl.ds(h * half + g * step + kp, rank, stride=slab + 1)
                    by_rank[lines, :] = wider[:, h * cols : (h + 1) * cols]

        row_sum = jnp.zeros((rank, rows), f32)
        seconds = [second_of(g) for g in range(groups)]
        models = [None] * groups
        models[0] = dot(row_turned, seconds[0])
        for g in range(groups):
            if g + 1 < groups:
                models[g + 1] = dot(row_turned, seconds[g + 1])
            residual = residual_of(g, models[g])
            keep_back(g, dot(row_factor, residual))
            row_sum = row_sum + dot(seconds[g], residual, ((1,), (1,)))
        rows_out[row_at] += row_sum
        wide = dot(cube_turned[depth_at], backward[...])
        cols_out[col_at] += wide[:rank, :cols] + wide[rank:, cols:]
        lines = pl.ds(pl.multiple_of(slot * slab, slab), slab)
        for first in range(0, pairs, 8):
            ranked = []
            for pair in range(first, first + 8):
                spots = [at * (slab + 1) for at in (pair, pairs + pair)]
                ranked.append(jnp.concatenate([by_rank[at : at + slab, :].astype(bf16) for at in spots], axis=1))
            ranked = jnp.concatenate(ranked, axis=0)
            second_back = dot(ranked, wide_col[...], ((1,), (1,))).astype(bf16)
            second_all[first : first + 8, lines, :] = second_back.reshape(8, slab, 2 * rank)

        return carry

    lax.fori_loop(0, count, one_slot, 0)

    def one_chunk(at, total):
        pair = at ^ core_mask
        second = second_all[pair]
        total = total + dot(second, core[pair])
        piece = dot(second, depth_all[...], ((0,), (0,)))
        core_out[at] = jnp.concatenate([piece[:rank], piece[rank:]], axis=1)
        return total

    total = lax.fori_loop(0, pairs, one_chunk, jnp.zeros((second_all.shape[1], rank), f32), unroll=16)
    for s in range(slots):

        @pl.when(s < count)
        def _():
            at = coords[0, 0, s, 2] - depth_base
            lines = pl.ds(pl.multiple_of(at * slab, slab), slab)
            depth_sum[lines, :] += total[s * slab : (s + 1) * slab]

    depth_out[...] = depth_sum[...].T


def terms(relative, sizes, row_spots, col_spots, counts, coords, data, weight, cube, cube_turned, pieces, core, depth, spread):
    slots, rows, slab, cols = data.shape
    rank = core.shape[2]
    half = slab // 2
    depth_blocks = cube.shape[0]

    outs = (
        jax.ShapeDtypeStruct((rank // 2, rank, 2 * rank), f32),
        jax.ShapeDtypeStruct((len(row_spots), rank, rows), f32),
        jax.ShapeDtypeStruct((len(col_spots), rank, cols), f32),
        jax.ShapeDtypeStruct((rank, depth_blocks * slab), f32),
        jax.ShapeDtypeStruct(spread.shape, f32),
    )
    return pl.pallas_call(
        functools.partial(terms_kernel, relative, sizes, row_spots, col_spots),
        out_shape=outs,
        grid_spec=pltpu.PrefetchScalarGridSpec(
            num_scalar_prefetch=2,
            grid=(),
            in_specs=[pl.BlockSpec(memory_space=pl.ANY)] * 2
            + [pl.BlockSpec(memory_space=pltpu.VMEM)] * (5 + len(pieces)),
            out_specs=[pl.BlockSpec(memory_space=pltpu.VMEM)] * 5,
            scratch_shapes=[
                pltpu.VMEM((len(row_spots), rank, rows), bf16),
                pltpu.VMEM((len(col_spots), rank, cols), bf16),
                pltpu.VMEM((2 * rank, 2 * cols), bf16),
                pltpu.VMEM((half * rank, 2 * cols), bf16),
                pltpu.VMEM((rank * (slab + 1), cols), f32),
                pltpu.VMEM((rank // 2, slots * slab, 2 * rank), bf16),
                pltpu.VMEM((slots * slab, rank), bf16),
                pltpu.VMEM((depth_blocks * slab, rank), f32),
                pltpu.VMEM((2, 2, rows, slab, cols), bf16),
                pltpu.SemaphoreType.DMA((2, 2)),
            ],
        ),
        input_output_aliases={8 + len(pieces): 4},
        compiler_params=pltpu.CompilerParams(vmem_limit_bytes=40 * 2**20),
        cost_estimate=pl.CostEstimate(flops=10**9, bytes_accessed=16 * 2**20, transcendentals=0),
        name="terms",
    )(counts, coords, data, weight, cube, cube_turned, *pieces, core, depth, spread)


mark_rows = 16
top_exponent = 14.0


def vmem_call(kernel, out_shape, *operands, name):
    return pl.pallas_call(
        kernel,
        out_shape=out_shape,
        in_specs=[pl.BlockSpec(memory_space=pltpu.VMEM)] * len(operands),
        out_specs=jax.tree.map(lambda _: pl.BlockSpec(memory_space=pltpu.VMEM), out_shape),
        compiler_params=pltpu.CompilerParams(vmem_limit_bytes=24 * 2**20),
        name=name,
    )(*operands)


def power_of(exponent):
    whole = jnp.abs(exponent).astype(jnp.int32)
    value = jnp.ones_like(exponent)
    for bit in range(7):
        factor = jnp.where(exponent < 0, f32(2.0 ** -(2**bit)), f32(2.0 ** (2**bit)))
        value = value * jnp.where((whole >> bit) & 1 == 1, factor, f32(1.0))
    return value


def exponent_of(value):
    lanes = value.shape[-1]
    largest = jnp.max(jnp.max(jnp.abs(value.reshape(-1, 8, lanes)), axis=0), axis=0, keepdims=True)
    largest = jnp.max(largest, axis=1, keepdims=True)
    largest = jnp.broadcast_to(jnp.maximum(largest, f32(1e-30)), (8, lanes))
    return jnp.ceil(jnp.log(largest) * f32(1.4426950408889634)) - f32(top_exponent)


def rounded(value):
    stretched = value * f32(8193.0)
    return stretched - (stretched - value)


def scaled(value):
    exponent = exponent_of(value)
    return rounded(value * power_of(-exponent)[:1]), exponent


def fill_message(out, *parts):
    at = 0
    mark = None
    for which, part in enumerate(parts):
        lanes = part.shape[-1]
        flat, exponent = scaled(part.reshape(-1, lanes))
        out[at : at + flat.shape[0], :] = flat
        at += flat.shape[0]
        exponent = jnp.broadcast_to(exponent[:1], (mark_rows, lanes))
        line = lax.broadcasted_iota(jnp.int32, exponent.shape, 0)
        mark = exponent if mark is None else jnp.where(line >= which, exponent, mark)
    out[at : at + mark_rows, :] = mark


def message_part(message, start, rows, part):
    mark = message.shape[0] - mark_rows + part
    return message[start : start + rows, :] * power_of(message[mark : mark + 1, :])


def message_shape(chunks, rank, lanes):
    return jax.ShapeDtypeStruct((chunks * rank + mark_rows, lanes), f32)


def tree_sum(values):
    values = list(values)
    while len(values) > 1:
        values = [values[at] + values[at + 1] for at in range(0, len(values), 2)]
    return values[0]


def after_cores_kernel(n_ia, n_ka, keep, got, own_core, own_depth, own_rows, *messages):
    half = n_ia * n_ka
    depth = keep[half + n_ka] + got[half + n_ka]
    flat, exponent = scaled(depth)
    own_depth[...] = flat * power_of(exponent)[:1]
    own_core[...] = keep[:n_ka] + got[:n_ka]
    own_rows[...] = keep[half : half + n_ka] + got[half : half + n_ka]
    for mask in range(1, n_ia):
        lines = slice(mask * n_ka, (mask + 1) * n_ka)
        fill_message(messages[mask - 1], keep[lines] + got[lines], depth)


def after_cores(n_ia, n_ka, keep, got):
    _, rank, lanes = keep.shape
    outs = [jax.ShapeDtypeStruct(shape, f32) for shape in ((n_ka, rank, lanes), (rank, lanes), (n_ka, rank, lanes))]
    outs += [message_shape(n_ka + 1, rank, lanes)] * (n_ia - 1)
    outs = vmem_call(functools.partial(after_cores_kernel, n_ia, n_ka), tuple(outs), keep, got, name="after_cores")
    return outs[0], outs[1], outs[2], outs[3:]


def after_rows_kernel(n_ia, n_ka, own_core, own_depth, own_rows, cols_sum, *refs):
    messages, depth_out, outs = refs[: n_ia - 1], refs[n_ia - 1], refs[n_ia:]
    count, rank, lanes = own_core.shape
    core = own_core[...].reshape(count * rank, lanes)
    depths = [own_depth[...]]
    for message in messages:
        core = core + message_part(message, 0, count * rank, 0)
        depths.append(message_part(message, count * rank, rank, 1))
    depth_out[...] = tree_sum(depths)
    for mask in range(n_ka):
        fill_message(outs[mask], core, own_rows[mask], cols_sum[mask])


def after_rows(n_ia, n_ka, own_core, own_depth, own_rows, cols_sum, messages):
    count, rank, lanes = own_core.shape
    outs = (jax.ShapeDtypeStruct((rank, lanes), f32),) + (message_shape(count + 2, rank, lanes),) * n_ka
    outs = vmem_call(
        functools.partial(after_rows_kernel, n_ia, n_ka),
        outs,
        own_core,
        own_depth,
        own_rows,
        cols_sum,
        *messages,
        name="after_rows",
    )
    return outs[0], outs[1:]


def after_depths_kernel(n_ka, rank, *refs):
    messages, out, rows_out = refs[:n_ka], refs[-2], refs[-1]
    cores = []
    for mask, message in enumerate(messages):
        part = message_part(message, 0, n_ka * rank, 0)
        cores.append(jnp.concatenate([part[(at ^ mask) * rank : ((at ^ mask) + 1) * rank] for at in range(n_ka)]))
    rows_out[...] = tree_sum(message_part(message, n_ka * rank, rank, 1) for message in messages)
    cols = tree_sum(message_part(message, (n_ka + 1) * rank, rank, 2) for message in messages)
    fill_message(out, tree_sum(cores), cols)


def after_depths(n_ka, rank, messages):
    lanes = messages[0].shape[1]
    outs = (message_shape(n_ka + 1, rank, lanes), jax.ShapeDtypeStruct((rank, lanes), f32))
    return vmem_call(functools.partial(after_depths_kernel, n_ka, rank), outs, *messages, name="after_depths")


def unpack_kernel(sizes, rank, first_message, *refs):
    n_ia, n_ka = sizes["ia"], sizes["ka"]
    messages = refs[:n_ia]
    core_out, *cols_out, whole, sems = refs[n_ia if first_message == 0 else n_ia + 1 :]
    pairs = rank // 2
    own = masks_of(True, sizes)[2]
    copies = []
    for at in range(n_ia):
        first = pl.multiple_of(((own // n_ka) ^ (first_message + at)) * n_ka, n_ka)
        for mask in range(n_ka):
            piece = message_part(messages[at], mask * rank, rank, 0)
            line = lax.rem(own, n_ka) ^ mask
            whole[at, 0, line] = piece[:, :rank]
            whole[at, 1, line] = piece[:, rank:]
        for h in range(2):
            lines = pl.ds(h * pairs + first, n_ka)
            copies.append(pltpu.make_async_copy(whole.at[at, h], core_out.at[lines], sems.at[2 * at + h]))
            copies[-1].start()
    for out in cols_out:
        out[...] = tree_sum(message_part(message, n_ka * rank, rank, 1) for message in messages)
    for copy in copies:
        copy.wait()


def unpack(sizes, rank, messages, core=None):
    lanes = messages[0].shape[1]
    near = core is None
    out_shape = [jax.ShapeDtypeStruct((rank, rank, rank), f32)]
    out_specs = [pl.BlockSpec(memory_space=pltpu.HBM)]
    if near:
        out_shape.append(jax.ShapeDtypeStruct((rank, lanes), f32))
        out_specs.append(pl.BlockSpec(memory_space=pltpu.VMEM))
    return pl.pallas_call(
        functools.partial(unpack_kernel, sizes, rank, 0 if near else sizes["ia"]),
        out_shape=tuple(out_shape),
        in_specs=[pl.BlockSpec(memory_space=pltpu.VMEM)] * len(messages)
        + ([] if near else [pl.BlockSpec(memory_space=pltpu.HBM)]),
        out_specs=tuple(out_specs),
        scratch_shapes=[
            pltpu.VMEM((len(messages), 2, sizes["ka"], rank, rank), f32),
            pltpu.SemaphoreType.DMA((2 * len(messages),)),
        ],
        input_output_aliases={} if near else {len(messages): 0},
        compiler_params=pltpu.CompilerParams(vmem_limit_bytes=24 * 2**20),
        cost_estimate=pl.CostEstimate(flops=10**6, bytes_accessed=4 * 2**20, transcendentals=0),
        name="unpack_near" if near else "unpack_far",
    )(*messages, *([] if near else [core]))


def power_of_two(n):
    return n & (n - 1) == 0


def swap(value, axis, size, mask):
    return lax.ppermute(value, axis, [(at, at ^ mask) for at in range(size)])


def on_device(sizes, observed, weights, coords, counts, factor_rows, factor_cols, factor_depth, core_tensor):
    n_ia, n_ja, n_ka = sizes["ia"], sizes["ja"], sizes["ka"]
    devices = n_ia * n_ja * n_ka
    rank = core_tensor.shape[0]
    _, _, slots, rows, slab, cols = observed.shape
    data = pltpu.with_memory_space_constraint(observed.reshape(observed.shape[2:]), pltpu.HBM)
    weight = pltpu.with_memory_space_constraint(weights.reshape(weights.shape[2:]), pltpu.HBM)
    core_here = pltpu.with_memory_space_constraint(core_tensor, pltpu.HBM)
    depth_here = pltpu.with_memory_space_constraint(factor_depth, pltpu.HBM)
    row_chunks = factor_rows.shape[1] * n_ja * n_ka // rows
    col_chunks = factor_cols.shape[1] * n_ka // cols
    depth_blocks = factor_depth.shape[1] // n_ka // slab
    ia, ja, ka = lax.axis_index("ia"), lax.axis_index("ja"), lax.axis_index("ka")
    by_swaps = (
        n_ja == 2
        and power_of_two(n_ia)
        and power_of_two(n_ka)
        and rank // 2 == devices
        and factor_rows.shape[1] == rows
        and factor_cols.shape[1] == cols
    )

    if by_swaps:
        own = jnp.stack([factor_rows, swap(factor_rows, "ja", n_ja, 1), factor_cols])
        pieces = [own] + [swap(own, "ka", n_ka, mask) for mask in range(1, n_ka)]
        row_spots = [(mask, line) for line in range(n_ja) for mask in range(n_ka)]
        col_spots = [(mask, n_ja) for mask in range(n_ka)]
    else:
        row_table = lax.all_gather(factor_rows, ("ja", "ka"), axis=1, tiled=True)
        row_table = row_table.reshape(rank, row_chunks, rows).transpose(1, 0, 2)
        col_table = lax.all_gather(factor_cols, "ka", axis=1, tiled=True)
        col_table = col_table.reshape(rank, col_chunks, cols).transpose(1, 0, 2)
        pieces = [row_table, col_table]
        row_spots = [(0, line) for line in range(row_chunks)]
        col_spots = [(1, line) for line in range(col_chunks)]

    cube, cube_turned, core_pairs, own_depth, spread = first_cubes(
        pieces[0], depth_here, core_here, data, weight, depth_blocks
    )
    core_sum, rows_sum, cols_sum, depth_sum, _ = terms(
        by_swaps,
        sizes,
        row_spots,
        col_spots,
        counts,
        coords,
        data,
        weight,
        cube,
        cube_turned,
        pieces,
        core_pairs,
        own_depth,
        spread,
    )

    if not by_swaps:
        rows_whole = rows_sum.transpose(1, 0, 2).reshape(rank, row_chunks * rows)
        cols_whole = cols_sum.transpose(1, 0, 2).reshape(rank, col_chunks * cols)
        core_whole = core_sum.reshape(rank // 2, rank, 2, rank).transpose(2, 0, 1, 3).reshape(rank, rank, rank)
        return (
            lax.psum_scatter(rows_whole, ("ja", "ka"), scatter_dimension=1, tiled=True),
            lax.psum_scatter(lax.psum(cols_whole, "ia"), "ka", scatter_dimension=1, tiled=True),
            lax.psum(depth_sum, ("ia", "ja")),
            lax.psum(core_whole, ("ia", "ja", "ka")),
        )

    half = devices // 2
    keep = jnp.concatenate([core_sum[:half], rows_sum[:n_ka], depth_sum[None]])
    send = jnp.concatenate([core_sum[half:], rows_sum[n_ka:], depth_sum[None]])
    got = swap(send, "ja", n_ja, 1)
    own_core, own_depth, own_rows, messages = after_cores(n_ia, n_ka, keep, got)
    messages = [swap(message.astype(wire), "ia", n_ia, at + 1).astype(f32) for at, message in enumerate(messages)]
    depth_total, messages = after_rows(n_ia, n_ka, own_core, own_depth, own_rows, cols_sum, messages)
    messages = [messages[0]] + [
        swap(messages[mask].astype(wire), "ka", n_ka, mask).astype(f32) for mask in range(1, n_ka)
    ]
    message, rows_total = after_depths(n_ka, rank, messages)
    sent = message.astype(wire)
    sent = [sent] + [swap(sent, "ia", n_ia, mask) for mask in range(1, n_ia)]
    other = [swap(each, "ja", n_ja, 1) for each in sent]
    core_near, cols_total = unpack(sizes, rank, [each.astype(f32) for each in sent])
    (core_total,) = unpack(sizes, rank, [each.astype(f32) for each in other], core_near)
    return (rows_total, cols_total, depth_total, core_total)


def solution(mesh):
    in_specs = (
        P("ia", "ja", "ka", None, None, None),
        P("ia", "ja", "ka", None, None, None),
        P("ia", "ja", "ka", None),
        P("ia", "ja", "ka"),
        P(None, ("ia", "ja", "ka")),
        P(None, ("ja", "ka")),
        P(),
        P(),
    )
    out_specs = (P(None, ("ia", "ja", "ka")), P(None, ("ja", "ka")), P(None, "ka"), P())
    return jax.shard_map(
        functools.partial(on_device, dict(mesh.shape)),
        mesh=mesh,
        in_specs=in_specs,
        out_specs=out_specs,
        check_vma=False,
    )
```

```python
import functools

import jax
import jax.numpy as jnp
from jax import lax
from jax.experimental import pallas as pl
from jax.experimental.pallas import tpu as pltpu
from jax.sharding import PartitionSpec as P

resid_scale = 1.0 / 64.0
f32 = jnp.float32
bf16 = jnp.bfloat16
wire = jnp.float16


def dot(a, b, contract=((1,), (0,))):
    return lax.dot_general(a, b, (contract, ((), ())), preferred_element_type=f32)


def spread_out(source, target):
    rows, slab, _ = source.shape
    for i in range(rows):
        target[i * (slab + 1) : i * (slab + 1) + slab, :] = source[i].astype(f32)


def cube_kernel(
    depth_blocks,
    slab,
    after,
    factor_depth,
    core,
    coords,
    cube_out,
    core_out,
    depth_out,
    coords_out,
    depth_here,
    core_here,
    cube_wide,
    sems,
):
    rank = core.shape[0]
    half = slab // 2
    pairs = rank // 2
    width = depth_blocks * slab
    start = pl.multiple_of(lax.axis_index("ka") * width, width)
    core_copy = pltpu.make_async_copy(core, core_here, sems.at[0])
    depth_copy = pltpu.make_async_copy(factor_depth.at[:, pl.ds(start, width)], depth_here, sems.at[1])
    coords_copy = pltpu.make_async_copy(coords, coords_out, sems.at[2])
    for copy in (depth_copy, core_copy, coords_copy):
        copy.start()
    depth_copy.wait()
    depth = depth_here[...].astype(f32).T
    depth_out[...] = depth.astype(bf16)
    order = [depth[t * slab + h * half : t * slab + (h + 1) * half] for h in range(2) for t in range(depth_blocks)]
    depth = jnp.concatenate(order, axis=0).astype(bf16)
    count = depth_blocks * half
    core_copy.wait()

    def one_rank(r1, carry):
        piece = dot(depth, core_here[r1], ((1,), (1,)))
        wide = jnp.concatenate([piece[:count], piece[count:]], axis=1)
        cube_wide[pl.ds(r1, count, stride=rank + 1), :] = wide
        return carry

    lax.fori_loop(0, rank, one_rank, 0, unroll=16)
    for pair in range(pairs):
        core_out[pair] = jnp.concatenate([core_here[pair], core_here[pairs + pair]], axis=0)
    for t in range(depth_blocks):
        for kp in range(half):
            at = (t * half + kp) * (rank + 1)
            block = cube_wide[at : at + rank, :]
            cube_out[t, kp * rank : (kp + 1) * rank, :] = block.astype(bf16)
    coords_copy.wait()


def first_cubes(after, factor_depth, core, coords, depth_blocks, slab):
    rank = core.shape[0]
    half = slab // 2
    width = depth_blocks * slab
    return pl.pallas_call(
        functools.partial(cube_kernel, depth_blocks, slab),
        out_shape=(
            jax.ShapeDtypeStruct((depth_blocks, half * rank, 2 * rank), bf16),
            jax.ShapeDtypeStruct((rank // 2, 2 * rank, rank), bf16),
            jax.ShapeDtypeStruct((width, rank), bf16),
            jax.ShapeDtypeStruct(coords.shape, coords.dtype),
        ),
        in_specs=[pl.BlockSpec(memory_space=pl.ANY)] + [pl.BlockSpec(memory_space=pltpu.HBM)] * 3,
        out_specs=[pl.BlockSpec(memory_space=pltpu.VMEM)] * 3 + [pl.BlockSpec(memory_space=pltpu.SMEM)],
        scratch_shapes=[
            pltpu.VMEM((rank, width), bf16),
            pltpu.VMEM(core.shape, bf16),
            pltpu.VMEM((depth_blocks * half * (rank + 1), 2 * rank), f32),
            pltpu.SemaphoreType.DMA((3,)),
        ],
        compiler_params=pltpu.CompilerParams(vmem_limit_bytes=24 * 2**20),
        cost_estimate=pl.CostEstimate(flops=10**9, bytes_accessed=4 * 2**20, transcendentals=0),
        name="first_cubes",
    )(after, factor_depth, core, coords)


def first_slot_kernel(after, cube, data, weight, turned, spread, fetched, sems):
    copies = [
        pltpu.make_async_copy(source.at[0], fetched.at[at], sems.at[at]) for at, source in enumerate((data, weight))
    ]
    for copy in copies:
        copy.start()
    for t in range(cube.shape[0]):
        turned[t] = cube[t].astype(f32).T.astype(bf16)
    for at, copy in enumerate(copies):
        copy.wait()
        spread_out(fetched.at[at], spread.at[at])


def first_slot(after, cube, data, weight):
    _, rows, slab, cols = data.shape
    blocks, height, width = cube.shape
    return pl.pallas_call(
        first_slot_kernel,
        out_shape=(
            jax.ShapeDtypeStruct((blocks, width, height), bf16),
            jax.ShapeDtypeStruct((2, rows * (slab + 1), cols), f32),
        ),
        in_specs=[
            pl.BlockSpec(memory_space=pl.ANY),
            pl.BlockSpec(memory_space=pltpu.VMEM),
            pl.BlockSpec(memory_space=pltpu.HBM),
            pl.BlockSpec(memory_space=pltpu.HBM),
        ],
        out_specs=[pl.BlockSpec(memory_space=pltpu.VMEM)] * 2,
        scratch_shapes=[pltpu.VMEM((2, rows, slab, cols), bf16), pltpu.SemaphoreType.DMA((2,))],
        compiler_params=pltpu.CompilerParams(vmem_limit_bytes=32 * 2**20),
        cost_estimate=pl.CostEstimate(flops=10**9, bytes_accessed=4 * 2**20, transcendentals=0),
        name="first_slot",
    )(after, cube, data, weight)


def masks_of(relative, sizes):
    ia, ja, ka = lax.axis_index("ia"), lax.axis_index("ja"), lax.axis_index("ka")
    if not relative:
        return 0, 0, 0
    return ja * sizes["ka"] + ka, ka, (ja * sizes["ia"] + ia) * sizes["ka"] + ka


def terms_kernel(relative, sizes, row_spots, col_spots, counts, coords, data, weight, cube, cube_turned, *refs):
    pieces = refs[: 1 + max(at for at, _ in row_spots + col_spots)]
    (
        core,
        depth_turned,
        _,
        core_out,
        rows_out,
        cols_out,
        depth_out,
        spread,
        row_table,
        col_table,
        wide_col,
        backward,
        by_rank,
        second_all,
        depth_all,
        depth_sum,
        fetched,
        sems,
    ) = refs[len(pieces) :]
    slots, rows, slab, cols = data.shape
    pairs = core.shape[0]
    rank = 2 * pairs
    half = slab // 2
    depth_blocks = cube.shape[0]
    count = counts[0, 0, 0]
    row_mask, col_mask, core_mask = masks_of(relative, sizes)
    row_base = lax.axis_index("ia") * row_table.shape[0]
    col_base = lax.axis_index("ja") * col_table.shape[0]
    depth_base = lax.axis_index("ka") * depth_blocks

    def fetches(slot):
        side = lax.rem(slot, 2)
        return [
            pltpu.make_async_copy(source.at[slot], fetched.at[side, which], sems.at[side, which])
            for which, source in enumerate((data, weight))
        ]

    def fetch(slot):
        @pl.when(slot < count)
        def _():
            for copy in fetches(slot):
                copy.start()

    def arrive(slot):
        for copy in fetches(slot):
            copy.wait()

    for s in range(slots):

        @pl.when(s >= count)
        def _():
            lines = slice(s * slab, (s + 1) * slab)
            second_all[:, lines, :] = jnp.zeros((pairs, slab, 2 * rank), bf16)
            depth_all[lines, :] = jnp.zeros((slab, rank), bf16)

    depth_sum[...] = jnp.zeros_like(depth_sum)
    rows_out[...] = jnp.zeros_like(rows_out)
    cols_out[...] = jnp.zeros_like(cols_out)
    wide_col[...] = jnp.zeros_like(wide_col)
    for spots, table in ((row_spots, row_table), (col_spots, col_table)):
        for at, (piece, line) in enumerate(spots):
            table[at] = pieces[piece][line]

    def one_slot(slot, carry):
        fetch(slot + 1)

        @pl.when(slot > 0)
        def _():
            arrive(slot)
            for which in range(2):
                spread_out(fetched.at[lax.rem(slot, 2), which], spread.at[which])

        row_at = (coords[0, 0, 0, slot] - row_base) ^ row_mask
        col_at = (coords[0, 1, 0, slot] - col_base) ^ col_mask
        depth_at = coords[0, 2, 0, slot] - depth_base
        row_factor = row_table[row_at]
        row_turned = row_factor.astype(f32).T.astype(bf16)
        col_factor = col_table[col_at]
        wide_col[:rank, :cols] = col_factor
        wide_col[rank:, cols:] = col_factor
        own_depth = depth_turned[pl.ds(pl.multiple_of(depth_at * slab, slab), slab), :]
        depth_all[pl.ds(pl.multiple_of(slot * slab, slab), slab), :] = own_depth

        step = 8
        groups = half // step
        wide_factor = wide_col[...]
        def second_of(g):
            lines = cube[depth_at, g * step * rank : (g + 1) * step * rank, :]
            block = dot(lines, wide_factor).astype(bf16)
            return jnp.concatenate([block[kp * rank : (kp + 1) * rank] for kp in range(step)], axis=1)

        def residual_of(g, model):
            parts = []
            for kp in range(step):
                for h in range(2):
                    lines = pl.ds(h * half + g * step + kp, rows, stride=slab + 1)
                    seen, scale = spread[0, lines, :], spread[1, lines, :]
                    at = (kp * 2 + h) * cols
                    gap = model[:, at : at + cols] - seen
                    parts.append((scale * gap * resid_scale).astype(bf16))
            return jnp.concatenate(parts, axis=1)

        def keep_back(g, back):
            back = back.astype(bf16)
            for kp in range(step):
                pair = back[:, kp * 2 * cols : (kp + 1) * 2 * cols]
                at = (g * step + kp) * rank
                backward[at : at + rank, :] = pair
                wider = pair.astype(f32)
                for h in range(2):
                    lines = pl.ds(h * half + g * step + kp, rank, stride=slab + 1)
                    by_rank[lines, :] = wider[:, h * cols : (h + 1) * cols]

        row_sum = jnp.zeros((rows, rank), f32)
        seconds = [second_of(g) for g in range(groups)]
        models = [None] * groups
        models[0] = dot(row_turned, seconds[0])
        for g in range(groups):
            if g + 1 < groups:
                models[g + 1] = dot(row_turned, seconds[g + 1])
            residual = residual_of(g, models[g])
            keep_back(g, dot(row_factor, residual))
            row_sum = row_sum + dot(residual, seconds[g], ((1,), (1,)))
        rows_out[row_at] += row_sum.T
        wide = dot(cube_turned[depth_at], backward[...])
        cols_out[col_at] += wide[:rank, :cols] + wide[rank:, cols:]
        lines = pl.ds(pl.multiple_of(slot * slab, slab), slab)
        for first in range(0, pairs, 8):
            ranked = []
            for pair in range(first, first + 8):
                spots = [at * (slab + 1) for at in (pair, pairs + pair)]
                ranked.append(jnp.concatenate([by_rank[at : at + slab, :].astype(bf16) for at in spots], axis=1))
            ranked = jnp.concatenate(ranked, axis=0)
            second_back = dot(ranked, wide_col[...], ((1,), (1,))).astype(bf16)
            second_all[first : first + 8, lines, :] = second_back.reshape(8, slab, 2 * rank)

        return carry

    lax.fori_loop(0, count, one_slot, 0)

    def one_chunk(at, total):
        pair = at ^ core_mask
        second = second_all[pair]
        total = total + dot(second, core[pair])
        piece = dot(second, depth_all[...], ((0,), (0,)))
        core_out[at] = jnp.concatenate([piece[:rank], piece[rank:]], axis=1)
        return total

    total = lax.fori_loop(0, pairs, one_chunk, jnp.zeros((second_all.shape[1], rank), f32), unroll=32)
    for s in range(slots):

        @pl.when(s < count)
        def _():
            at = coords[0, 2, 0, s] - depth_base
            lines = pl.ds(pl.multiple_of(at * slab, slab), slab)
            depth_sum[lines, :] += total[s * slab : (s + 1) * slab]

    depth_out[...] = depth_sum[...].T


def terms(relative, sizes, row_spots, col_spots, counts, coords, data, weight, cube, cube_turned, pieces, core, depth, spread):
    slots, rows, slab, cols = data.shape
    rank = core.shape[2]
    half = slab // 2
    depth_blocks = cube.shape[0]

    outs = (
        jax.ShapeDtypeStruct((rank // 2, rank, 2 * rank), f32),
        jax.ShapeDtypeStruct((len(row_spots), rank, rows), f32),
        jax.ShapeDtypeStruct((len(col_spots), rank, cols), f32),
        jax.ShapeDtypeStruct((rank, depth_blocks * slab), f32),
        jax.ShapeDtypeStruct(spread.shape, f32),
    )
    return pl.pallas_call(
        functools.partial(terms_kernel, relative, sizes, row_spots, col_spots),
        out_shape=outs,
        grid_spec=pltpu.PrefetchScalarGridSpec(
            num_scalar_prefetch=0,
            grid=(),
            in_specs=[pl.BlockSpec(memory_space=pltpu.SMEM)] * 2
            + [pl.BlockSpec(memory_space=pltpu.HBM)] * 2
            + [pl.BlockSpec(memory_space=pltpu.VMEM)] * (5 + len(pieces)),
            out_specs=[pl.BlockSpec(memory_space=pltpu.VMEM)] * 5,
            scratch_shapes=[
                pltpu.VMEM((len(row_spots), rank, rows), bf16),
                pltpu.VMEM((len(col_spots), rank, cols), bf16),
                pltpu.VMEM((2 * rank, 2 * cols), bf16),
                pltpu.VMEM((half * rank, 2 * cols), bf16),
                pltpu.VMEM((rank * (slab + 1), cols), f32),
                pltpu.VMEM((rank // 2, slots * slab, 2 * rank), bf16),
                pltpu.VMEM((slots * slab, rank), bf16),
                pltpu.VMEM((depth_blocks * slab, rank), f32),
                pltpu.VMEM((2, 2, rows, slab, cols), bf16),
                pltpu.SemaphoreType.DMA((2, 2)),
            ],
        ),
        input_output_aliases={8 + len(pieces): 4},
        compiler_params=pltpu.CompilerParams(vmem_limit_bytes=40 * 2**20),
        cost_estimate=pl.CostEstimate(flops=10**9, bytes_accessed=16 * 2**20, transcendentals=0),
        name="terms",
    )(counts, coords, data, weight, cube, cube_turned, *pieces, core, depth, spread)


mark_rows = 16
top_exponent = 14.0


def vmem_call(kernel, out_shape, *operands, name):
    return pl.pallas_call(
        kernel,
        out_shape=out_shape,
        in_specs=[pl.BlockSpec(memory_space=pltpu.VMEM)] * len(operands),
        out_specs=jax.tree.map(lambda _: pl.BlockSpec(memory_space=pltpu.VMEM), out_shape),
        compiler_params=pltpu.CompilerParams(vmem_limit_bytes=24 * 2**20),
        name=name,
    )(*operands)


def power_of(exponent):
    whole = jnp.abs(exponent).astype(jnp.int32)
    value = jnp.ones_like(exponent)
    for bit in range(7):
        factor = jnp.where(exponent < 0, f32(2.0 ** -(2**bit)), f32(2.0 ** (2**bit)))
        value = value * jnp.where((whole >> bit) & 1 == 1, factor, f32(1.0))
    return value


def exponent_of(value):
    lanes = value.shape[-1]
    largest = jnp.max(jnp.max(jnp.abs(value.reshape(-1, 8, lanes)), axis=0), axis=0, keepdims=True)
    largest = jnp.max(largest, axis=1, keepdims=True)
    largest = jnp.broadcast_to(jnp.maximum(largest, f32(1e-30)), (8, lanes))
    return jnp.ceil(jnp.log(largest) * f32(1.4426950408889634)) - f32(top_exponent)


def rounded(value):
    stretched = value * f32(8193.0)
    return stretched - (stretched - value)


def scaled(value):
    exponent = exponent_of(value)
    return rounded(value * power_of(-exponent)[:1]), exponent


def fill_message(out, *parts):
    at = 0
    mark = None
    for which, (flat, exponent) in enumerate(parts):
        out[at : at + flat.shape[0], :] = flat
        at += flat.shape[0]
        exponent = jnp.broadcast_to(exponent[:1], (mark_rows, flat.shape[1]))
        line = lax.broadcasted_iota(jnp.int32, exponent.shape, 0)
        mark = exponent if mark is None else jnp.where(line >= which, exponent, mark)
    out[at : at + mark_rows, :] = mark


def message_part(message, start, rows, part):
    mark = message.shape[0] - mark_rows + part
    return message[start : start + rows, :] * power_of(message[mark : mark + 1, :])


def message_shape(chunks, rank, lanes):
    return jax.ShapeDtypeStruct((chunks * rank + mark_rows, lanes), f32)


def tree_sum(values):
    values = list(values)
    while len(values) > 1:
        values = [values[at] + values[at + 1] for at in range(0, len(values), 2)]
    return values[0]


def after_cores_kernel(n_ia, n_ka, keep, got, own_core, own_depth, own_rows, *messages):
    half = n_ia * n_ka
    depth = keep[half + n_ka] + got[half + n_ka]
    flat, exponent = scaled(depth)
    own_depth[...] = flat * power_of(exponent)[:1]
    own_core[...] = keep[:n_ka] + got[:n_ka]
    own_rows[...] = keep[half : half + n_ka] + got[half : half + n_ka]
    for mask in range(1, n_ia):
        lines = slice(mask * n_ka, (mask + 1) * n_ka)
        core = (keep[lines] + got[lines]).reshape(-1, depth.shape[1])
        fill_message(messages[mask - 1], scaled(core), (flat, exponent))


def after_cores(n_ia, n_ka, keep, got):
    _, rank, lanes = keep.shape
    outs = [jax.ShapeDtypeStruct(shape, f32) for shape in ((n_ka, rank, lanes), (rank, lanes), (n_ka, rank, lanes))]
    outs += [message_shape(n_ka + 1, rank, lanes)] * (n_ia - 1)
    outs = vmem_call(functools.partial(after_cores_kernel, n_ia, n_ka), tuple(outs), keep, got, name="after_cores")
    return outs[0], outs[1], outs[2], outs[3:]


def after_rows_kernel(n_ia, n_ka, own_core, own_depth, own_rows, cols_sum, *refs):
    messages, depth_out, outs = refs[: n_ia - 1], refs[n_ia - 1], refs[n_ia:]
    count, rank, lanes = own_core.shape
    core = own_core[...].reshape(count * rank, lanes)
    depths = [own_depth[...]]
    for message in messages:
        core = core + message_part(message, 0, count * rank, 0)
        depths.append(message_part(message, count * rank, rank, 1))
    depth_out[...] = tree_sum(depths)
    flat, exponent = scaled(core)
    for mask in range(n_ka):
        fill_message(outs[mask], (flat, exponent), scaled(own_rows[mask]), scaled(cols_sum[mask]))


def after_rows(n_ia, n_ka, own_core, own_depth, own_rows, cols_sum, messages):
    count, rank, lanes = own_core.shape
    outs = (jax.ShapeDtypeStruct((rank, lanes), f32),) + (message_shape(count + 2, rank, lanes),) * n_ka
    outs = vmem_call(
        functools.partial(after_rows_kernel, n_ia, n_ka),
        outs,
        own_core,
        own_depth,
        own_rows,
        cols_sum,
        *messages,
        name="after_rows",
    )
    return outs[0], outs[1:]


def after_depths_kernel(n_ka, rank, *refs):
    messages, out, rows_out = refs[:n_ka], refs[-2], refs[-1]
    cores = []
    for mask, message in enumerate(messages):
        part = message_part(message, 0, n_ka * rank, 0)
        cores.append(jnp.concatenate([part[(at ^ mask) * rank : ((at ^ mask) + 1) * rank] for at in range(n_ka)]))
    rows_out[...] = tree_sum(message_part(message, n_ka * rank, rank, 1) for message in messages)
    cols = tree_sum(message_part(message, (n_ka + 1) * rank, rank, 2) for message in messages)
    fill_message(out, scaled(tree_sum(cores)), scaled(cols))


def after_depths(n_ka, rank, messages):
    lanes = messages[0].shape[1]
    outs = (message_shape(n_ka + 1, rank, lanes), jax.ShapeDtypeStruct((rank, lanes), f32))
    return vmem_call(functools.partial(after_depths_kernel, n_ka, rank), outs, *messages, name="after_depths")


def unpack_kernel(sizes, rank, first_message, *refs):
    n_ia, n_ka = sizes["ia"], sizes["ka"]
    messages = refs[:n_ia]
    core_out, *cols_out, whole, sems = refs[n_ia if first_message == 0 else n_ia + 1 :]
    pairs = rank // 2
    own = masks_of(True, sizes)[2]
    copies = []
    for at in range(n_ia):
        first = pl.multiple_of(((own // n_ka) ^ (first_message + at)) * n_ka, n_ka)
        for mask in range(n_ka):
            piece = message_part(messages[at], mask * rank, rank, 0)
            line = lax.rem(own, n_ka) ^ mask
            whole[at, 0, line] = piece[:, :rank]
            whole[at, 1, line] = piece[:, rank:]
        for h in range(2):
            lines = pl.ds(h * pairs + first, n_ka)
            copies.append(pltpu.make_async_copy(whole.at[at, h], core_out.at[lines], sems.at[2 * at + h]))
            copies[-1].start()
    for out in cols_out:
        out[...] = tree_sum(message_part(message, n_ka * rank, rank, 1) for message in messages)
    for copy in copies:
        copy.wait()


def unpack(sizes, rank, messages, core=None):
    lanes = messages[0].shape[1]
    near = core is None
    out_shape = [jax.ShapeDtypeStruct((rank, rank, rank), f32)]
    out_specs = [pl.BlockSpec(memory_space=pltpu.HBM)]
    if near:
        out_shape.append(jax.ShapeDtypeStruct((rank, lanes), f32))
        out_specs.append(pl.BlockSpec(memory_space=pltpu.VMEM))
    return pl.pallas_call(
        functools.partial(unpack_kernel, sizes, rank, 0 if near else sizes["ia"]),
        out_shape=tuple(out_shape),
        in_specs=[pl.BlockSpec(memory_space=pltpu.VMEM)] * len(messages)
        + ([] if near else [pl.BlockSpec(memory_space=pltpu.HBM)]),
        out_specs=tuple(out_specs),
        scratch_shapes=[
            pltpu.VMEM((len(messages), 2, sizes["ka"], rank, rank), f32),
            pltpu.SemaphoreType.DMA((2 * len(messages),)),
        ],
        input_output_aliases={} if near else {len(messages): 0},
        compiler_params=pltpu.CompilerParams(vmem_limit_bytes=24 * 2**20),
        cost_estimate=pl.CostEstimate(flops=10**6, bytes_accessed=4 * 2**20, transcendentals=0),
        name="unpack_near" if near else "unpack_far",
    )(*messages, *([] if near else [core]))


def power_of_two(n):
    return n & (n - 1) == 0


def swap(value, axis, size, mask):
    return lax.ppermute(value, axis, [(at, at ^ mask) for at in range(size)])


def on_device(sizes, observed, weights, coords, counts, factor_rows, factor_cols, factor_depth, core_tensor):
    n_ia, n_ja, n_ka = sizes["ia"], sizes["ja"], sizes["ka"]
    devices = n_ia * n_ja * n_ka
    rank = core_tensor.shape[0]
    _, _, slots, rows, slab, cols = observed.shape
    data = pltpu.with_memory_space_constraint(observed.reshape(observed.shape[2:]), pltpu.HBM)
    weight = pltpu.with_memory_space_constraint(weights.reshape(weights.shape[2:]), pltpu.HBM)
    core_here = pltpu.with_memory_space_constraint(core_tensor, pltpu.HBM)
    depth_here = pltpu.with_memory_space_constraint(factor_depth, pltpu.HBM)
    row_chunks = factor_rows.shape[1] * n_ja * n_ka // rows
    col_chunks = factor_cols.shape[1] * n_ka // cols
    depth_blocks = factor_depth.shape[1] // n_ka // slab
    ia, ja, ka = lax.axis_index("ia"), lax.axis_index("ja"), lax.axis_index("ka")
    by_swaps = (
        n_ja == 2
        and power_of_two(n_ia)
        and power_of_two(n_ka)
        and rank // 2 == devices
        and factor_rows.shape[1] == rows
        and factor_cols.shape[1] == cols
    )

    if by_swaps:
        own = jnp.stack([factor_rows, factor_cols])
        near = [own] + [swap(own, "ka", n_ka, mask) for mask in range(1, n_ka)]
        near_rows = jnp.stack([piece[0] for piece in near])
        pieces = near + [swap(near_rows, "ja", n_ja, 1)]
        row_spots = [(mask, 0) for mask in range(n_ka)] + [(n_ka, mask) for mask in range(n_ka)]
        col_spots = [(mask, 1) for mask in range(n_ka)]
    else:
        row_table = lax.all_gather(factor_rows, ("ja", "ka"), axis=1, tiled=True)
        row_table = row_table.reshape(rank, row_chunks, rows).transpose(1, 0, 2)
        col_table = lax.all_gather(factor_cols, "ka", axis=1, tiled=True)
        col_table = col_table.reshape(rank, col_chunks, cols).transpose(1, 0, 2)
        pieces = [row_table, col_table]
        row_spots = [(0, line) for line in range(row_chunks)]
        own, near_rows = row_table, row_table
        col_spots = [(1, line) for line in range(col_chunks)]

    cube, core_pairs, own_depth, coords = first_cubes(
        own,
        depth_here,
        core_here,
        pltpu.with_memory_space_constraint(coords.transpose(0, 3, 1, 2), pltpu.HBM),
        depth_blocks,
        slab,
    )
    cube_turned, spread = first_slot(near_rows, cube, data, weight)
    core_sum, rows_sum, cols_sum, depth_sum, _ = terms(
        by_swaps,
        sizes,
        row_spots,
        col_spots,
        counts,
        coords,
        data,
        weight,
        cube,
        cube_turned,
        pieces,
        core_pairs,
        own_depth,
        spread,
    )

    if not by_swaps:
        rows_whole = rows_sum.transpose(1, 0, 2).reshape(rank, row_chunks * rows)
        cols_whole = cols_sum.transpose(1, 0, 2).reshape(rank, col_chunks * cols)
        core_whole = core_sum.reshape(rank // 2, rank, 2, rank).transpose(2, 0, 1, 3).reshape(rank, rank, rank)
        return (
            lax.psum_scatter(rows_whole, ("ja", "ka"), scatter_dimension=1, tiled=True),
            lax.psum_scatter(lax.psum(cols_whole, "ia"), "ka", scatter_dimension=1, tiled=True),
            lax.psum(depth_sum, ("ia", "ja")),
            lax.psum(core_whole, ("ia", "ja", "ka")),
        )

    half = devices // 2
    keep = jnp.concatenate([core_sum[:half], rows_sum[:n_ka], depth_sum[None]])
    send = jnp.concatenate([core_sum[half:], rows_sum[n_ka:], depth_sum[None]])
    got = swap(send, "ja", n_ja, 1)
    own_core, own_depth, own_rows, messages = after_cores(n_ia, n_ka, keep, got)
    messages = [swap(message.astype(wire), "ia", n_ia, at + 1).astype(f32) for at, message in enumerate(messages)]
    depth_total, messages = after_rows(n_ia, n_ka, own_core, own_depth, own_rows, cols_sum, messages)
    messages = [messages[0]] + [
        swap(messages[mask].astype(wire), "ka", n_ka, mask).astype(f32) for mask in range(1, n_ka)
    ]
    message, rows_total = after_depths(n_ka, rank, messages)
    sent = message.astype(wire)
    sent = [sent] + [swap(sent, "ia", n_ia, mask) for mask in range(1, n_ia)]
    other = [swap(each, "ja", n_ja, 1) for each in sent]
    core_near, cols_total = unpack(sizes, rank, [each.astype(f32) for each in sent])
    (core_total,) = unpack(sizes, rank, [each.astype(f32) for each in other], core_near)
    return (rows_total, cols_total, depth_total, core_total)


def solution(mesh):
    in_specs = (
        P("ia", "ja", "ka", None, None, None),
        P("ia", "ja", "ka", None, None, None),
        P("ia", "ja", "ka", None),
        P("ia", "ja", "ka"),
        P(None, ("ia", "ja", "ka")),
        P(None, ("ja", "ka")),
        P(),
        P(),
    )
    out_specs = (P(None, ("ia", "ja", "ka")), P(None, ("ja", "ka")), P(None, "ka"), P())
    return jax.shard_map(
        functools.partial(on_device, dict(mesh.shape)),
        mesh=mesh,
        in_specs=in_specs,
        out_specs=out_specs,
        check_vma=False,
    )
```

```python
import functools

import jax
import jax.numpy as jnp
from jax import lax
from jax.experimental import pallas as pl
from jax.experimental.pallas import tpu as pltpu
from jax.sharding import PartitionSpec as P

resid_scale = 1.0 / 64.0
f32 = jnp.float32
bf16 = jnp.bfloat16
wire = jnp.float16


def dot(a, b, contract=((1,), (0,))):
    return lax.dot_general(a, b, (contract, ((), ())), preferred_element_type=f32)


def spread_out(source, target):
    rows, slab, _ = source.shape
    for i in range(rows):
        target[i * (slab + 1) : i * (slab + 1) + slab, :] = source[i].astype(f32)


def bring_kernel(factor_depth, core, coords, core_out, depth_out, coords_out, depth_here, core_here, sems):
    width = depth_here.shape[1]
    pairs = core_out.shape[0]
    start = pl.multiple_of(lax.axis_index("ka") * width, width)
    copies = [
        pltpu.make_async_copy(factor_depth.at[:, pl.ds(start, width)], depth_here, sems.at[0]),
        pltpu.make_async_copy(core, core_here, sems.at[1]),
        pltpu.make_async_copy(coords, coords_out, sems.at[2]),
    ]
    for copy in copies:
        copy.start()
    copies[0].wait()
    depth_out[...] = depth_here[...].astype(f32).T.astype(bf16)
    copies[1].wait()
    for pair in range(pairs):
        core_out[pair] = jnp.concatenate([core_here[pair], core_here[pairs + pair]], axis=0)
    copies[2].wait()


def bring(factor_depth, core, coords, width):
    rank = core.shape[0]
    return pl.pallas_call(
        bring_kernel,
        out_shape=(
            jax.ShapeDtypeStruct((rank // 2, 2 * rank, rank), bf16),
            jax.ShapeDtypeStruct((width, rank), bf16),
            jax.ShapeDtypeStruct(coords.shape, coords.dtype),
        ),
        in_specs=[pl.BlockSpec(memory_space=pltpu.HBM)] * 3,
        out_specs=[pl.BlockSpec(memory_space=pltpu.VMEM)] * 2 + [pl.BlockSpec(memory_space=pltpu.SMEM)],
        scratch_shapes=[
            pltpu.VMEM((rank, width), bf16),
            pltpu.VMEM(core.shape, bf16),
            pltpu.SemaphoreType.DMA((3,)),
        ],
        compiler_params=pltpu.CompilerParams(vmem_limit_bytes=16 * 2**20),
        cost_estimate=pl.CostEstimate(flops=10**6, bytes_accessed=4 * 2**20, transcendentals=0),
        name="bring",
    )(factor_depth, core, coords)


def cube_kernel(slab, after, core, depth, data, weight, cube_out, cube_turned_out, spread, fetched, cube_wide, sems):
    pairs, _, rank = core.shape
    half = slab // 2
    depth_blocks = cube_out.shape[0]
    copies = [
        pltpu.make_async_copy(source.at[0], fetched.at[at], sems.at[at]) for at, source in enumerate((data, weight))
    ]
    for copy in copies:
        copy.start()
    order = [depth[t * slab + h * half : t * slab + (h + 1) * half] for h in range(2) for t in range(depth_blocks)]
    ordered = jnp.concatenate(order, axis=0)
    count = depth_blocks * half

    def one_pair(pair, carry):
        piece = dot(ordered, core[pair], ((1,), (1,)))
        for which in range(2):
            here = piece[:, which * rank : (which + 1) * rank]
            wide = jnp.concatenate([here[:count], here[count:]], axis=1)
            cube_wide[pl.ds(which * pairs + pair, count, stride=rank + 1), :] = wide
        return carry

    lax.fori_loop(0, pairs, one_pair, 0, unroll=8)
    for t in range(depth_blocks):
        for kp in range(half):
            at = (t * half + kp) * (rank + 1)
            block = cube_wide[at : at + rank, :]
            cube_out[t, kp * rank : (kp + 1) * rank, :] = block.astype(bf16)
        cube_turned_out[t] = cube_out[t].astype(f32).T.astype(bf16)
    for at, copy in enumerate(copies):
        copy.wait()
        spread_out(fetched.at[at], spread.at[at])


def first_cubes(after, core, depth, data, weight):
    pairs, _, rank = core.shape
    _, rows, slab, cols = data.shape
    half = slab // 2
    depth_blocks = depth.shape[0] // slab
    return pl.pallas_call(
        functools.partial(cube_kernel, slab),
        out_shape=(
            jax.ShapeDtypeStruct((depth_blocks, half * rank, 2 * rank), bf16),
            jax.ShapeDtypeStruct((depth_blocks, 2 * rank, half * rank), bf16),
            jax.ShapeDtypeStruct((2, rows * (slab + 1), cols), f32),
        ),
        in_specs=[pl.BlockSpec(memory_space=pl.ANY)]
        + [pl.BlockSpec(memory_space=pltpu.VMEM)] * 2
        + [pl.BlockSpec(memory_space=pltpu.HBM)] * 2,
        out_specs=[pl.BlockSpec(memory_space=pltpu.VMEM)] * 3,
        scratch_shapes=[
            pltpu.VMEM((2, rows, slab, cols), bf16),
            pltpu.VMEM((depth_blocks * half * (rank + 1), 2 * rank), f32),
            pltpu.SemaphoreType.DMA((2,)),
        ],
        compiler_params=pltpu.CompilerParams(vmem_limit_bytes=40 * 2**20),
        cost_estimate=pl.CostEstimate(flops=10**9, bytes_accessed=4 * 2**20, transcendentals=0),
        name="first_cubes",
    )(after, core, depth, data, weight)


def masks_of(relative, sizes):
    ia, ja, ka = lax.axis_index("ia"), lax.axis_index("ja"), lax.axis_index("ka")
    if not relative:
        return 0, 0, 0
    return ja * sizes["ka"] + ka, ka, (ja * sizes["ia"] + ia) * sizes["ka"] + ka


def terms_kernel(relative, sizes, row_spots, col_spots, counts, coords, data, weight, cube, cube_turned, *refs):
    pieces = refs[: 1 + max(at for at, _ in row_spots + col_spots)]
    (
        core,
        depth_turned,
        _,
        *outs,
        cols_out,
        spread,
        rows_out,
        row_table,
        col_table,
        wide_col,
        backward,
        by_rank,
        second_all,
        depth_all,
        depth_sum,
        fetched,
        sems,
    ) = refs[len(pieces) :]
    slots, rows, slab, cols = data.shape
    pairs = core.shape[0]
    rank = 2 * pairs
    half = slab // 2
    depth_blocks = cube.shape[0]
    count = counts[0, 0, 0]
    row_mask, col_mask, core_mask = masks_of(relative, sizes)
    row_base = lax.axis_index("ia") * row_table.shape[0]
    col_base = lax.axis_index("ja") * col_table.shape[0]
    depth_base = lax.axis_index("ka") * depth_blocks

    def fetches(slot):
        side = lax.rem(slot, 2)
        return [
            pltpu.make_async_copy(source.at[slot], fetched.at[side, which], sems.at[side, which])
            for which, source in enumerate((data, weight))
        ]

    def fetch(slot):
        @pl.when(slot < count)
        def _():
            for copy in fetches(slot):
                copy.start()

    def arrive(slot):
        for copy in fetches(slot):
            copy.wait()

    for s in range(slots):

        @pl.when(s >= count)
        def _():
            lines = slice(s * slab, (s + 1) * slab)
            second_all[:, lines, :] = jnp.zeros((pairs, slab, 2 * rank), bf16)
            depth_all[lines, :] = jnp.zeros((slab, rank), bf16)

    depth_sum[...] = jnp.zeros_like(depth_sum)
    rows_out[...] = jnp.zeros_like(rows_out)
    cols_out[...] = jnp.zeros_like(cols_out)
    wide_col[...] = jnp.zeros_like(wide_col)
    for spots, table in ((row_spots, row_table), (col_spots, col_table)):
        for at, (piece, line) in enumerate(spots):
            table[at] = pieces[piece][line]

    def one_slot(slot, carry):
        fetch(slot + 1)

        @pl.when(slot > 0)
        def _():
            arrive(slot)
            for which in range(2):
                spread_out(fetched.at[lax.rem(slot, 2), which], spread.at[which])

        row_at = (coords[0, 0, 0, slot] - row_base) ^ row_mask
        col_at = (coords[0, 1, 0, slot] - col_base) ^ col_mask
        depth_at = coords[0, 2, 0, slot] - depth_base
        row_factor = row_table[row_at]
        row_turned = row_factor.astype(f32).T.astype(bf16)
        col_factor = col_table[col_at]
        wide_col[:rank, :cols] = col_factor
        wide_col[rank:, cols:] = col_factor
        own_depth = depth_turned[pl.ds(pl.multiple_of(depth_at * slab, slab), slab), :]
        depth_all[pl.ds(pl.multiple_of(slot * slab, slab), slab), :] = own_depth

        step = 8
        groups = half // step
        wide_factor = wide_col[...]
        def second_of(g):
            lines = cube[depth_at, g * step * rank : (g + 1) * step * rank, :]
            block = dot(lines, wide_factor).astype(bf16)
            return jnp.concatenate([block[kp * rank : (kp + 1) * rank] for kp in range(step)], axis=1)

        def residual_of(g, model):
            parts = []
            for kp in range(step):
                for h in range(2):
                    lines = pl.ds(h * half + g * step + kp, rows, stride=slab + 1)
                    seen, scale = spread[0, lines, :], spread[1, lines, :]
                    at = (kp * 2 + h) * cols
                    gap = model[:, at : at + cols] - seen
                    parts.append((scale * gap * resid_scale).astype(bf16))
            return jnp.concatenate(parts, axis=1)

        def keep_back(g, back):
            back = back.astype(bf16)
            for kp in range(step):
                pair = back[:, kp * 2 * cols : (kp + 1) * 2 * cols]
                at = (g * step + kp) * rank
                backward[at : at + rank, :] = pair
                wider = pair.astype(f32)
                for h in range(2):
                    lines = pl.ds(h * half + g * step + kp, rank, stride=slab + 1)
                    by_rank[lines, :] = wider[:, h * cols : (h + 1) * cols]

        row_sum = jnp.zeros((rows, rank), f32)
        seconds = [second_of(g) for g in range(groups)]
        models = [None] * groups
        models[0] = dot(row_turned, seconds[0])
        for g in range(groups):
            if g + 1 < groups:
                models[g + 1] = dot(row_turned, seconds[g + 1])
            residual = residual_of(g, models[g])
            keep_back(g, dot(row_factor, residual))
            row_sum = row_sum + dot(residual, seconds[g], ((1,), (1,)))
        rows_out[row_at] += row_sum.T
        wide = dot(cube_turned[depth_at], backward[...])
        cols_out[col_at] += wide[:rank, :cols] + wide[rank:, cols:]
        lines = pl.ds(pl.multiple_of(slot * slab, slab), slab)
        for first in range(0, pairs, 8):
            ranked = []
            for pair in range(first, first + 8):
                spots = [at * (slab + 1) for at in (pair, pairs + pair)]
                ranked.append(jnp.concatenate([by_rank[at : at + slab, :].astype(bf16) for at in spots], axis=1))
            ranked = jnp.concatenate(ranked, axis=0)
            second_back = dot(ranked, wide_col[...], ((1,), (1,))).astype(bf16)
            second_all[first : first + 8, lines, :] = second_back.reshape(8, slab, 2 * rank)

        return carry

    lax.fori_loop(0, count, one_slot, 0)

    if relative:
        sides = [(outs[0], 0), (outs[1], 0)]
        core_spots = [sides[at // (pairs // 2)] + (at % (pairs // 2),) for at in range(pairs)]
        row_count = len(row_spots) // 2
        row_places = [sides[at // row_count] + (pairs // 2 + at % row_count,) for at in range(2 * row_count)]
    else:
        core_spots = [(outs[0], 0, at) for at in range(pairs)]
        row_places = [(outs[1], 0, at) for at in range(len(row_spots))]
    total = jnp.zeros((second_all.shape[1], rank), f32)
    for at in range(pairs):
        pair = at ^ core_mask
        second = second_all[pair]
        total = total + dot(second, core[pair])
        piece = dot(second, depth_all[...], ((0,), (0,)))
        out, _, line = core_spots[at]
        out[line] = jnp.concatenate([piece[:rank], piece[rank:]], axis=1)
    for at, (out, _, line) in enumerate(row_places):
        out[line] = rows_out[at]
    for s in range(slots):

        @pl.when(s < count)
        def _():
            at = coords[0, 2, 0, s] - depth_base
            lines = pl.ds(pl.multiple_of(at * slab, slab), slab)
            depth_sum[lines, :] += total[s * slab : (s + 1) * slab]

    depth = depth_sum[...].T
    if relative:
        for out in outs:
            out[pairs // 2 + row_count] = depth
    else:
        outs[2][...] = depth


def terms(relative, sizes, row_spots, col_spots, counts, coords, data, weight, cube, cube_turned, pieces, core, depth, spread):
    slots, rows, slab, cols = data.shape
    rank = core.shape[2]
    half = slab // 2
    depth_blocks = cube.shape[0]

    width = depth_blocks * slab
    if relative:
        chunks = (rank // 2 + len(row_spots)) // 2 + 1
        outs = (jax.ShapeDtypeStruct((chunks, rank, rows), f32),) * 2
    else:
        outs = (
            jax.ShapeDtypeStruct((rank // 2, rank, 2 * rank), f32),
            jax.ShapeDtypeStruct((len(row_spots), rank, rows), f32),
            jax.ShapeDtypeStruct((rank, width), f32),
        )
    outs += (
        jax.ShapeDtypeStruct((len(col_spots), rank, cols), f32),
        jax.ShapeDtypeStruct(spread.shape, f32),
    )
    return pl.pallas_call(
        functools.partial(terms_kernel, relative, sizes, row_spots, col_spots),
        out_shape=outs,
        grid_spec=pltpu.PrefetchScalarGridSpec(
            num_scalar_prefetch=0,
            grid=(),
            in_specs=[pl.BlockSpec(memory_space=pltpu.SMEM)] * 2
            + [pl.BlockSpec(memory_space=pltpu.HBM)] * 2
            + [pl.BlockSpec(memory_space=pltpu.VMEM)] * (5 + len(pieces)),
            out_specs=[pl.BlockSpec(memory_space=pltpu.VMEM)] * len(outs),
            scratch_shapes=[
                pltpu.VMEM((len(row_spots), rank, rows), f32),
                pltpu.VMEM((len(row_spots), rank, rows), bf16),
                pltpu.VMEM((len(col_spots), rank, cols), bf16),
                pltpu.VMEM((2 * rank, 2 * cols), bf16),
                pltpu.VMEM((half * rank, 2 * cols), bf16),
                pltpu.VMEM((rank * (slab + 1), cols), f32),
                pltpu.VMEM((rank // 2, slots * slab, 2 * rank), bf16),
                pltpu.VMEM((slots * slab, rank), bf16),
                pltpu.VMEM((depth_blocks * slab, rank), f32),
                pltpu.VMEM((2, 2, rows, slab, cols), bf16),
                pltpu.SemaphoreType.DMA((2, 2)),
            ],
        ),
        input_output_aliases={8 + len(pieces): len(outs) - 1},
        compiler_params=pltpu.CompilerParams(vmem_limit_bytes=40 * 2**20),
        cost_estimate=pl.CostEstimate(flops=10**9, bytes_accessed=16 * 2**20, transcendentals=0),
        name="terms",
    )(counts, coords, data, weight, cube, cube_turned, *pieces, core, depth, spread)


mark_rows = 16
top_exponent = 14.0


def vmem_call(kernel, out_shape, *operands, name):
    return pl.pallas_call(
        kernel,
        out_shape=out_shape,
        in_specs=[pl.BlockSpec(memory_space=pltpu.VMEM)] * len(operands),
        out_specs=jax.tree.map(lambda _: pl.BlockSpec(memory_space=pltpu.VMEM), out_shape),
        compiler_params=pltpu.CompilerParams(vmem_limit_bytes=24 * 2**20),
        name=name,
    )(*operands)


def power_of(exponent):
    whole = jnp.abs(exponent).astype(jnp.int32)
    value = jnp.ones_like(exponent)
    for bit in range(7):
        factor = jnp.where(exponent < 0, f32(2.0 ** -(2**bit)), f32(2.0 ** (2**bit)))
        value = value * jnp.where((whole >> bit) & 1 == 1, factor, f32(1.0))
    return value


def exponent_of(value):
    lanes = value.shape[-1]
    largest = jnp.max(jnp.max(jnp.abs(value.reshape(-1, 8, lanes)), axis=0), axis=0, keepdims=True)
    largest = jnp.max(largest, axis=1, keepdims=True)
    largest = jnp.broadcast_to(jnp.maximum(largest, f32(1e-30)), (8, lanes))
    return jnp.ceil(jnp.log(largest) * f32(1.4426950408889634)) - f32(top_exponent)


def rounded(value):
    stretched = value * f32(8193.0)
    return stretched - (stretched - value)


def scaled(value):
    exponent = exponent_of(value)
    return rounded(value * power_of(-exponent)[:1]), exponent


def fill_message(out, *parts):
    at = 0
    mark = None
    for which, (flat, exponent) in enumerate(parts):
        out[at : at + flat.shape[0], :] = flat
        at += flat.shape[0]
        exponent = jnp.broadcast_to(exponent[:1], (mark_rows, flat.shape[1]))
        line = lax.broadcasted_iota(jnp.int32, exponent.shape, 0)
        mark = exponent if mark is None else jnp.where(line >= which, exponent, mark)
    out[at : at + mark_rows, :] = mark


def message_part(message, start, rows, part):
    mark = message.shape[0] - mark_rows + part
    return message[start : start + rows, :] * power_of(message[mark : mark + 1, :])


def message_shape(chunks, rank, lanes):
    return jax.ShapeDtypeStruct((chunks * rank + mark_rows, lanes), f32)


def tree_sum(values):
    values = list(values)
    while len(values) > 1:
        values = [values[at] + values[at + 1] for at in range(0, len(values), 2)]
    return values[0]


def after_cores_kernel(n_ia, n_ka, keep, got, own_core, own_depth, own_rows, *messages):
    half = n_ia * n_ka
    depth = keep[half + n_ka] + got[half + n_ka]
    flat, exponent = scaled(depth)
    own_depth[...] = flat * power_of(exponent)[:1]
    own_core[...] = keep[:n_ka] + got[:n_ka]
    own_rows[...] = keep[half : half + n_ka] + got[half : half + n_ka]
    for mask in range(1, n_ia):
        lines = slice(mask * n_ka, (mask + 1) * n_ka)
        core = (keep[lines] + got[lines]).reshape(-1, depth.shape[1])
        fill_message(messages[mask - 1], scaled(core), (flat, exponent))


def after_cores(n_ia, n_ka, keep, got):
    _, rank, lanes = keep.shape
    outs = [jax.ShapeDtypeStruct(shape, f32) for shape in ((n_ka, rank, lanes), (rank, lanes), (n_ka, rank, lanes))]
    outs += [message_shape(n_ka + 1, rank, lanes)] * (n_ia - 1)
    outs = vmem_call(functools.partial(after_cores_kernel, n_ia, n_ka), tuple(outs), keep, got, name="after_cores")
    return outs[0], outs[1], outs[2], outs[3:]


def after_rows_kernel(n_ia, n_ka, own_core, own_depth, own_rows, cols_sum, *refs):
    messages, depth_out, outs = refs[: n_ia - 1], refs[n_ia - 1], refs[n_ia:]
    count, rank, lanes = own_core.shape
    core = own_core[...].reshape(count * rank, lanes)
    depths = [own_depth[...]]
    for message in messages:
        core = core + message_part(message, 0, count * rank, 0)
        depths.append(message_part(message, count * rank, rank, 1))
    depth_out[...] = tree_sum(depths)
    flat, exponent = scaled(core)
    for mask in range(n_ka):
        fill_message(outs[mask], (flat, exponent), scaled(own_rows[mask]), scaled(cols_sum[mask]))


def after_rows(n_ia, n_ka, own_core, own_depth, own_rows, cols_sum, messages):
    count, rank, lanes = own_core.shape
    outs = (jax.ShapeDtypeStruct((rank, lanes), f32),) + (message_shape(count + 2, rank, lanes),) * n_ka
    outs = vmem_call(
        functools.partial(after_rows_kernel, n_ia, n_ka),
        outs,
        own_core,
        own_depth,
        own_rows,
        cols_sum,
        *messages,
        name="after_rows",
    )
    return outs[0], outs[1:]


def after_depths_kernel(n_ka, rank, *refs):
    messages, out, rows_out = refs[:n_ka], refs[-2], refs[-1]
    cores = []
    for mask, message in enumerate(messages):
        part = message_part(message, 0, n_ka * rank, 0)
        cores.append(jnp.concatenate([part[(at ^ mask) * rank : ((at ^ mask) + 1) * rank] for at in range(n_ka)]))
    rows_out[...] = tree_sum(message_part(message, n_ka * rank, rank, 1) for message in messages)
    cols = tree_sum(message_part(message, (n_ka + 1) * rank, rank, 2) for message in messages)
    fill_message(out, scaled(tree_sum(cores)), scaled(cols))


def after_depths(n_ka, rank, messages):
    lanes = messages[0].shape[1]
    outs = (message_shape(n_ka + 1, rank, lanes), jax.ShapeDtypeStruct((rank, lanes), f32))
    return vmem_call(functools.partial(after_depths_kernel, n_ka, rank), outs, *messages, name="after_depths")


def unpack_kernel(sizes, rank, first_message, *refs):
    n_ia, n_ka = sizes["ia"], sizes["ka"]
    messages = refs[:n_ia]
    core_out, *cols_out, whole, sems = refs[n_ia if first_message == 0 else n_ia + 1 :]
    pairs = rank // 2
    own = masks_of(True, sizes)[2]
    copies = []
    for at in range(n_ia):
        first = pl.multiple_of(((own // n_ka) ^ (first_message + at)) * n_ka, n_ka)
        for mask in range(n_ka):
            piece = message_part(messages[at], mask * rank, rank, 0)
            line = lax.rem(own, n_ka) ^ mask
            whole[at, 0, line] = piece[:, :rank]
            whole[at, 1, line] = piece[:, rank:]
        for h in range(2):
            lines = pl.ds(h * pairs + first, n_ka)
            copies.append(pltpu.make_async_copy(whole.at[at, h], core_out.at[lines], sems.at[2 * at + h]))
            copies[-1].start()
    for out in cols_out:
        out[...] = tree_sum(message_part(message, n_ka * rank, rank, 1) for message in messages)
    for copy in copies:
        copy.wait()


def unpack(sizes, rank, messages, core=None):
    lanes = messages[0].shape[1]
    near = core is None
    out_shape = [jax.ShapeDtypeStruct((rank, rank, rank), f32)]
    out_specs = [pl.BlockSpec(memory_space=pltpu.HBM)]
    if near:
        out_shape.append(jax.ShapeDtypeStruct((rank, lanes), f32))
        out_specs.append(pl.BlockSpec(memory_space=pltpu.VMEM))
    return pl.pallas_call(
        functools.partial(unpack_kernel, sizes, rank, 0 if near else sizes["ia"]),
        out_shape=tuple(out_shape),
        in_specs=[pl.BlockSpec(memory_space=pltpu.VMEM)] * len(messages)
        + ([] if near else [pl.BlockSpec(memory_space=pltpu.HBM)]),
        out_specs=tuple(out_specs),
        scratch_shapes=[
            pltpu.VMEM((len(messages), 2, sizes["ka"], rank, rank), f32),
            pltpu.SemaphoreType.DMA((2 * len(messages),)),
        ],
        input_output_aliases={} if near else {len(messages): 0},
        compiler_params=pltpu.CompilerParams(vmem_limit_bytes=24 * 2**20),
        cost_estimate=pl.CostEstimate(flops=10**6, bytes_accessed=4 * 2**20, transcendentals=0),
        name="unpack_near" if near else "unpack_far",
    )(*messages, *([] if near else [core]))


def power_of_two(n):
    return n & (n - 1) == 0


def swap(value, axis, size, mask):
    return lax.ppermute(value, axis, [(at, at ^ mask) for at in range(size)])


def on_device(sizes, observed, weights, coords, counts, factor_rows, factor_cols, factor_depth, core_tensor):
    n_ia, n_ja, n_ka = sizes["ia"], sizes["ja"], sizes["ka"]
    devices = n_ia * n_ja * n_ka
    rank = core_tensor.shape[0]
    _, _, slots, rows, slab, cols = observed.shape
    data = pltpu.with_memory_space_constraint(observed.reshape(observed.shape[2:]), pltpu.HBM)
    weight = pltpu.with_memory_space_constraint(weights.reshape(weights.shape[2:]), pltpu.HBM)
    core_here = pltpu.with_memory_space_constraint(core_tensor, pltpu.HBM)
    depth_here = pltpu.with_memory_space_constraint(factor_depth, pltpu.HBM)
    row_chunks = factor_rows.shape[1] * n_ja * n_ka // rows
    col_chunks = factor_cols.shape[1] * n_ka // cols
    depth_blocks = factor_depth.shape[1] // n_ka // slab
    ia, ja, ka = lax.axis_index("ia"), lax.axis_index("ja"), lax.axis_index("ka")
    by_swaps = (
        n_ja == 2
        and power_of_two(n_ia)
        and power_of_two(n_ka)
        and rank // 2 == devices
        and factor_rows.shape[1] == rows
        and factor_cols.shape[1] == cols
        and rows == cols == 2 * rank == depth_blocks * slab
    )

    core_pairs, own_depth, coords = bring(
        depth_here,
        core_here,
        pltpu.with_memory_space_constraint(coords.transpose(0, 3, 1, 2), pltpu.HBM),
        depth_blocks * slab,
    )
    if by_swaps:
        other_rows = swap(factor_rows, "ja", n_ja, 1)
        other_rows, core_pairs = lax.optimization_barrier((other_rows, core_pairs))
        own = jnp.stack([factor_rows, other_rows, factor_cols])
        pieces = [own] + [swap(own, "ka", n_ka, mask) for mask in range(1, n_ka)]
        row_spots = [(mask, line) for line in range(n_ja) for mask in range(n_ka)]
        col_spots = [(mask, n_ja) for mask in range(n_ka)]
    else:
        row_table = lax.all_gather(factor_rows, ("ja", "ka"), axis=1, tiled=True)
        row_table = row_table.reshape(rank, row_chunks, rows).transpose(1, 0, 2)
        col_table = lax.all_gather(factor_cols, "ka", axis=1, tiled=True)
        col_table = col_table.reshape(rank, col_chunks, cols).transpose(1, 0, 2)
        pieces = [row_table, col_table]
        row_spots = [(0, line) for line in range(row_chunks)]
        own = row_table
        col_spots = [(1, line) for line in range(col_chunks)]

    cube, cube_turned, spread = first_cubes(own, core_pairs, own_depth, data, weight)
    *sums, cols_sum, _ = terms(
        by_swaps,
        sizes,
        row_spots,
        col_spots,
        counts,
        coords,
        data,
        weight,
        cube,
        cube_turned,
        pieces,
        core_pairs,
        own_depth,
        spread,
    )

    if not by_swaps:
        core_sum, rows_sum, depth_sum = sums
        rows_whole = rows_sum.transpose(1, 0, 2).reshape(rank, row_chunks * rows)
        cols_whole = cols_sum.transpose(1, 0, 2).reshape(rank, col_chunks * cols)
        core_whole = core_sum.reshape(rank // 2, rank, 2, rank).transpose(2, 0, 1, 3).reshape(rank, rank, rank)
        return (
            lax.psum_scatter(rows_whole, ("ja", "ka"), scatter_dimension=1, tiled=True),
            lax.psum_scatter(lax.psum(cols_whole, "ia"), "ka", scatter_dimension=1, tiled=True),
            lax.psum(depth_sum, ("ia", "ja")),
            lax.psum(core_whole, ("ia", "ja", "ka")),
        )

    keep, send = sums
    got = swap(send, "ja", n_ja, 1)
    own_core, own_depth, own_rows, messages = after_cores(n_ia, n_ka, keep, got)
    messages = [swap(message.astype(wire), "ia", n_ia, at + 1).astype(f32) for at, message in enumerate(messages)]
    depth_total, messages = after_rows(n_ia, n_ka, own_core, own_depth, own_rows, cols_sum, messages)
    messages = [messages[0]] + [
        swap(messages[mask].astype(wire), "ka", n_ka, mask).astype(f32) for mask in range(1, n_ka)
    ]
    message, rows_total = after_depths(n_ka, rank, messages)
    sent = message.astype(wire)
    sent = [sent] + [swap(sent, "ia", n_ia, mask) for mask in range(1, n_ia)]
    other = [swap(each, "ja", n_ja, 1) for each in sent]
    core_near, cols_total = unpack(sizes, rank, [each.astype(f32) for each in sent])
    (core_total,) = unpack(sizes, rank, [each.astype(f32) for each in other], core_near)
    return (rows_total, cols_total, depth_total, core_total)


def solution(mesh):
    in_specs = (
        P("ia", "ja", "ka", None, None, None),
        P("ia", "ja", "ka", None, None, None),
        P("ia", "ja", "ka", None),
        P("ia", "ja", "ka"),
        P(None, ("ia", "ja", "ka")),
        P(None, ("ja", "ka")),
        P(),
        P(),
    )
    out_specs = (P(None, ("ia", "ja", "ka")), P(None, ("ja", "ka")), P(None, "ka"), P())
    return jax.shard_map(
        functools.partial(on_device, dict(mesh.shape)),
        mesh=mesh,
        in_specs=in_specs,
        out_specs=out_specs,
        check_vma=False,
    )
```

```python
import functools

import jax
import jax.numpy as jnp
from jax import lax
from jax.experimental import pallas as pl
from jax.experimental.pallas import tpu as pltpu
from jax.sharding import PartitionSpec as P

resid_scale = 1.0 / 64.0
f32 = jnp.float32
bf16 = jnp.bfloat16
wire = jnp.float16


def dot(a, b, contract=((1,), (0,))):
    return lax.dot_general(a, b, (contract, ((), ())), preferred_element_type=f32)


def spread_out(source, target):
    rows, slab, _ = source.shape
    for i in range(rows):
        target[i * (slab + 1) : i * (slab + 1) + slab, :] = source[i].astype(f32)


def cube_kernel(
    slab,
    after,
    factor_depth,
    core,
    coords,
    data,
    weight,
    cube_out,
    cube_turned_out,
    core_out,
    depth_out,
    coords_out,
    spread,
    depth_here,
    core_here,
    fetched,
    cube_wide,
    sems,
):
    pairs, _, rank = core_out.shape
    half = slab // 2
    depth_blocks = cube_out.shape[0]
    width = depth_here.shape[1]
    start = pl.multiple_of(lax.axis_index("ka") * width, width)
    copies = [
        pltpu.make_async_copy(factor_depth.at[:, pl.ds(start, width)], depth_here, sems.at[0]),
        pltpu.make_async_copy(core, core_here, sems.at[1]),
        pltpu.make_async_copy(coords, coords_out, sems.at[2]),
        pltpu.make_async_copy(data.at[0], fetched.at[0], sems.at[3]),
        pltpu.make_async_copy(weight.at[0], fetched.at[1], sems.at[4]),
    ]
    for copy in copies:
        copy.start()
    copies[0].wait()
    depth = depth_here[...].astype(f32).T.astype(bf16)
    depth_out[...] = depth
    order = [depth[t * slab + h * half : t * slab + (h + 1) * half] for h in range(2) for t in range(depth_blocks)]
    ordered = jnp.concatenate(order, axis=0)
    count = depth_blocks * half
    copies[1].wait()
    for pair in range(pairs):
        core_out[pair] = jnp.concatenate([core_here[pair], core_here[pairs + pair]], axis=0)

    def one_pair(pair, carry):
        piece = dot(ordered, core_out[pair], ((1,), (1,)))
        for which in range(2):
            here = piece[:, which * rank : (which + 1) * rank]
            wide = jnp.concatenate([here[:count], here[count:]], axis=1)
            cube_wide[pl.ds(which * pairs + pair, count, stride=rank + 1), :] = wide
        return carry

    lax.fori_loop(0, pairs, one_pair, 0, unroll=8)
    for t in range(depth_blocks):
        for kp in range(half):
            at = (t * half + kp) * (rank + 1)
            block = cube_wide[at : at + rank, :]
            cube_out[t, kp * rank : (kp + 1) * rank, :] = block.astype(bf16)
        cube_turned_out[t] = cube_out[t].astype(f32).T.astype(bf16)
    for copy in copies[2:]:
        copy.wait()
    for at in range(2):
        spread_out(fetched.at[at], spread.at[at])


def first_cubes(after, factor_depth, core, coords, data, weight, depth_blocks):
    rank = core.shape[0]
    _, rows, slab, cols = data.shape
    half = slab // 2
    width = depth_blocks * slab
    return pl.pallas_call(
        functools.partial(cube_kernel, slab),
        out_shape=(
            jax.ShapeDtypeStruct((depth_blocks, half * rank, 2 * rank), bf16),
            jax.ShapeDtypeStruct((depth_blocks, 2 * rank, half * rank), bf16),
            jax.ShapeDtypeStruct((rank // 2, 2 * rank, rank), bf16),
            jax.ShapeDtypeStruct((width, rank), bf16),
            jax.ShapeDtypeStruct(coords.shape, coords.dtype),
            jax.ShapeDtypeStruct((2, rows * (slab + 1), cols), f32),
        ),
        in_specs=[pl.BlockSpec(memory_space=pl.ANY)] + [pl.BlockSpec(memory_space=pltpu.HBM)] * 5,
        out_specs=[pl.BlockSpec(memory_space=pltpu.VMEM)] * 4
        + [pl.BlockSpec(memory_space=pltpu.SMEM), pl.BlockSpec(memory_space=pltpu.VMEM)],
        scratch_shapes=[
            pltpu.VMEM((rank, width), bf16),
            pltpu.VMEM(core.shape, bf16),
            pltpu.VMEM((2, rows, slab, cols), bf16),
            pltpu.VMEM((depth_blocks * half * (rank + 1), 2 * rank), f32),
            pltpu.SemaphoreType.DMA((5,)),
        ],
        compiler_params=pltpu.CompilerParams(vmem_limit_bytes=40 * 2**20),
        cost_estimate=pl.CostEstimate(flops=10**9, bytes_accessed=4 * 2**20, transcendentals=0),
        name="first_cubes",
    )(after, factor_depth, core, coords, data, weight)


def masks_of(relative, sizes):
    ia, ja, ka = lax.axis_index("ia"), lax.axis_index("ja"), lax.axis_index("ka")
    if not relative:
        return 0, 0, 0
    return ja * sizes["ka"] + ka, ka, (ja * sizes["ia"] + ia) * sizes["ka"] + ka


def terms_kernel(relative, sizes, row_spots, col_spots, counts, coords, data, weight, cube, cube_turned, *refs):
    pieces = refs[: 1 + max(at for at, _ in row_spots + col_spots)]
    (
        core,
        depth_turned,
        _,
        *outs,
        cols_out,
        spread,
        rows_out,
        row_table,
        col_table,
        wide_col,
        backward,
        by_rank,
        second_all,
        depth_all,
        depth_sum,
        fetched,
        sems,
    ) = refs[len(pieces) :]
    slots, rows, slab, cols = data.shape
    pairs = core.shape[0]
    rank = 2 * pairs
    half = slab // 2
    depth_blocks = cube.shape[0]
    count = counts[0, 0, 0]
    row_mask, col_mask, core_mask = masks_of(relative, sizes)
    row_base = lax.axis_index("ia") * row_table.shape[0]
    col_base = lax.axis_index("ja") * col_table.shape[0]
    depth_base = lax.axis_index("ka") * depth_blocks

    def fetches(slot):
        side = lax.rem(slot, 2)
        return [
            pltpu.make_async_copy(source.at[slot], fetched.at[side, which], sems.at[side, which])
            for which, source in enumerate((data, weight))
        ]

    def fetch(slot):
        @pl.when(slot < count)
        def _():
            for copy in fetches(slot):
                copy.start()

    def arrive(slot):
        for copy in fetches(slot):
            copy.wait()

    for s in range(slots):

        @pl.when(s >= count)
        def _():
            lines = slice(s * slab, (s + 1) * slab)
            second_all[:, lines, :] = jnp.zeros((pairs, slab, 2 * rank), bf16)
            depth_all[lines, :] = jnp.zeros((slab, rank), bf16)

    depth_sum[...] = jnp.zeros_like(depth_sum)
    rows_out[...] = jnp.zeros_like(rows_out)
    cols_out[...] = jnp.zeros_like(cols_out)
    wide_col[...] = jnp.zeros_like(wide_col)
    for spots, table in ((row_spots, row_table), (col_spots, col_table)):
        for at, (piece, line) in enumerate(spots):
            table[at] = pieces[piece][line]

    def one_slot(slot, carry):
        fetch(slot + 1)

        @pl.when(slot > 0)
        def _():
            arrive(slot)
            for which in range(2):
                spread_out(fetched.at[lax.rem(slot, 2), which], spread.at[which])

        row_at = (coords[0, 0, 0, slot] - row_base) ^ row_mask
        col_at = (coords[0, 1, 0, slot] - col_base) ^ col_mask
        depth_at = coords[0, 2, 0, slot] - depth_base
        row_factor = row_table[row_at]
        row_turned = row_factor.astype(f32).T.astype(bf16)
        col_factor = col_table[col_at]
        wide_col[:rank, :cols] = col_factor
        wide_col[rank:, cols:] = col_factor
        own_depth = depth_turned[pl.ds(pl.multiple_of(depth_at * slab, slab), slab), :]
        depth_all[pl.ds(pl.multiple_of(slot * slab, slab), slab), :] = own_depth

        step = 8
        groups = half // step
        wide_factor = wide_col[...]
        def second_of(g):
            lines = cube[depth_at, g * step * rank : (g + 1) * step * rank, :]
            block = dot(lines, wide_factor).astype(bf16)
            return jnp.concatenate([block[kp * rank : (kp + 1) * rank] for kp in range(step)], axis=1)

        def residual_of(g, model):
            parts = []
            for kp in range(step):
                for h in range(2):
                    lines = pl.ds(h * half + g * step + kp, rows, stride=slab + 1)
                    seen, scale = spread[0, lines, :], spread[1, lines, :]
                    at = (kp * 2 + h) * cols
                    gap = model[:, at : at + cols] - seen
                    parts.append((scale * gap * resid_scale).astype(bf16))
            return jnp.concatenate(parts, axis=1)

        def keep_back(g, back):
            back = back.astype(bf16)
            for kp in range(step):
                pair = back[:, kp * 2 * cols : (kp + 1) * 2 * cols]
                at = (g * step + kp) * rank
                backward[at : at + rank, :] = pair
                wider = pair.astype(f32)
                for h in range(2):
                    lines = pl.ds(h * half + g * step + kp, rank, stride=slab + 1)
                    by_rank[lines, :] = wider[:, h * cols : (h + 1) * cols]

        row_sum = jnp.zeros((rows, rank), f32)
        seconds = [second_of(g) for g in range(groups)]
        models = [None] * groups
        models[0] = dot(row_turned, seconds[0])
        for g in range(groups):
            if g + 1 < groups:
                models[g + 1] = dot(row_turned, seconds[g + 1])
            residual = residual_of(g, models[g])
            keep_back(g, dot(row_factor, residual))
            row_sum = row_sum + dot(residual, seconds[g], ((1,), (1,)))
        rows_out[row_at] += row_sum.T
        wide = dot(cube_turned[depth_at], backward[...])
        cols_out[col_at] += wide[:rank, :cols] + wide[rank:, cols:]
        lines = pl.ds(pl.multiple_of(slot * slab, slab), slab)
        for first in range(0, pairs, 8):
            ranked = []
            for pair in range(first, first + 8):
                spots = [at * (slab + 1) for at in (pair, pairs + pair)]
                ranked.append(jnp.concatenate([by_rank[at : at + slab, :].astype(bf16) for at in spots], axis=1))
            ranked = jnp.concatenate(ranked, axis=0)
            second_back = dot(ranked, wide_col[...], ((1,), (1,))).astype(bf16)
            second_all[first : first + 8, lines, :] = second_back.reshape(8, slab, 2 * rank)

        return carry

    lax.fori_loop(0, count, one_slot, 0)

    if relative:
        sides = [(outs[0], 0), (outs[1], 0)]
        core_spots = [sides[at // (pairs // 2)] + (at % (pairs // 2),) for at in range(pairs)]
        row_count = len(row_spots) // 2
        row_places = [sides[at // row_count] + (pairs // 2 + at % row_count,) for at in range(2 * row_count)]
    else:
        core_spots = [(outs[0], 0, at) for at in range(pairs)]
        row_places = [(outs[1], 0, at) for at in range(len(row_spots))]
    total = jnp.zeros((second_all.shape[1], rank), f32)
    for at in range(pairs):
        pair = at ^ core_mask
        second = second_all[pair]
        total = total + dot(second, core[pair])
        piece = dot(second, depth_all[...], ((0,), (0,)))
        out, _, line = core_spots[at]
        out[line] = jnp.concatenate([piece[:rank], piece[rank:]], axis=1)
    for at, (out, _, line) in enumerate(row_places):
        out[line] = rows_out[at]
    for s in range(slots):

        @pl.when(s < count)
        def _():
            at = coords[0, 2, 0, s] - depth_base
            lines = pl.ds(pl.multiple_of(at * slab, slab), slab)
            depth_sum[lines, :] += total[s * slab : (s + 1) * slab]

    depth = depth_sum[...].T
    if relative:
        for out in outs:
            out[pairs // 2 + row_count] = depth
    else:
        outs[2][...] = depth


def terms(relative, sizes, row_spots, col_spots, counts, coords, data, weight, cube, cube_turned, pieces, core, depth, spread):
    slots, rows, slab, cols = data.shape
    rank = core.shape[2]
    half = slab // 2
    depth_blocks = cube.shape[0]

    width = depth_blocks * slab
    if relative:
        chunks = (rank // 2 + len(row_spots)) // 2 + 1
        outs = (jax.ShapeDtypeStruct((chunks, rank, rows), f32),) * 2
    else:
        outs = (
            jax.ShapeDtypeStruct((rank // 2, rank, 2 * rank), f32),
            jax.ShapeDtypeStruct((len(row_spots), rank, rows), f32),
            jax.ShapeDtypeStruct((rank, width), f32),
        )
    outs += (
        jax.ShapeDtypeStruct((len(col_spots), rank, cols), f32),
        jax.ShapeDtypeStruct(spread.shape, f32),
    )
    return pl.pallas_call(
        functools.partial(terms_kernel, relative, sizes, row_spots, col_spots),
        out_shape=outs,
        grid_spec=pltpu.PrefetchScalarGridSpec(
            num_scalar_prefetch=0,
            grid=(),
            in_specs=[pl.BlockSpec(memory_space=pltpu.SMEM)] * 2
            + [pl.BlockSpec(memory_space=pltpu.HBM)] * 2
            + [pl.BlockSpec(memory_space=pltpu.VMEM)] * (5 + len(pieces)),
            out_specs=[pl.BlockSpec(memory_space=pltpu.VMEM)] * len(outs),
            scratch_shapes=[
                pltpu.VMEM((len(row_spots), rank, rows), f32),
                pltpu.VMEM((len(row_spots), rank, rows), bf16),
                pltpu.VMEM((len(col_spots), rank, cols), bf16),
                pltpu.VMEM((2 * rank, 2 * cols), bf16),
                pltpu.VMEM((half * rank, 2 * cols), bf16),
                pltpu.VMEM((rank * (slab + 1), cols), f32),
                pltpu.VMEM((rank // 2, slots * slab, 2 * rank), bf16),
                pltpu.VMEM((slots * slab, rank), bf16),
                pltpu.VMEM((depth_blocks * slab, rank), f32),
                pltpu.VMEM((2, 2, rows, slab, cols), bf16),
                pltpu.SemaphoreType.DMA((2, 2)),
            ],
        ),
        input_output_aliases={8 + len(pieces): len(outs) - 1},
        compiler_params=pltpu.CompilerParams(vmem_limit_bytes=40 * 2**20),
        cost_estimate=pl.CostEstimate(flops=10**9, bytes_accessed=16 * 2**20, transcendentals=0),
        name="terms",
    )(counts, coords, data, weight, cube, cube_turned, *pieces, core, depth, spread)


mark_rows = 16
top_exponent = 14.0


def vmem_call(kernel, out_shape, *operands, name):
    return pl.pallas_call(
        kernel,
        out_shape=out_shape,
        in_specs=[pl.BlockSpec(memory_space=pltpu.VMEM)] * len(operands),
        out_specs=jax.tree.map(lambda _: pl.BlockSpec(memory_space=pltpu.VMEM), out_shape),
        compiler_params=pltpu.CompilerParams(vmem_limit_bytes=24 * 2**20),
        name=name,
    )(*operands)


def power_of(exponent):
    whole = jnp.abs(exponent).astype(jnp.int32)
    value = jnp.ones_like(exponent)
    for bit in range(7):
        factor = jnp.where(exponent < 0, f32(2.0 ** -(2**bit)), f32(2.0 ** (2**bit)))
        value = value * jnp.where((whole >> bit) & 1 == 1, factor, f32(1.0))
    return value


def exponent_of(value):
    lanes = value.shape[-1]
    largest = jnp.max(jnp.max(jnp.abs(value.reshape(-1, 8, lanes)), axis=0), axis=0, keepdims=True)
    largest = jnp.max(largest, axis=1, keepdims=True)
    largest = jnp.broadcast_to(jnp.maximum(largest, f32(1e-30)), (8, lanes))
    return jnp.ceil(jnp.log(largest) * f32(1.4426950408889634)) - f32(top_exponent)


def rounded(value):
    stretched = value * f32(8193.0)
    return stretched - (stretched - value)


def scaled(value):
    exponent = exponent_of(value)
    return rounded(value * power_of(-exponent)[:1]), exponent


def fill_message(out, *parts):
    at = 0
    mark = None
    for which, (flat, exponent) in enumerate(parts):
        out[at : at + flat.shape[0], :] = flat
        at += flat.shape[0]
        exponent = jnp.broadcast_to(exponent[:1], (mark_rows, flat.shape[1]))
        line = lax.broadcasted_iota(jnp.int32, exponent.shape, 0)
        mark = exponent if mark is None else jnp.where(line >= which, exponent, mark)
    out[at : at + mark_rows, :] = mark


def message_part(message, start, rows, part):
    mark = message.shape[0] - mark_rows + part
    return message[start : start + rows, :] * power_of(message[mark : mark + 1, :])


def message_shape(chunks, rank, lanes):
    return jax.ShapeDtypeStruct((chunks * rank + mark_rows, lanes), f32)


def tree_sum(values):
    values = list(values)
    while len(values) > 1:
        values = [values[at] + values[at + 1] for at in range(0, len(values), 2)]
    return values[0]


def after_cores_kernel(n_ia, n_ka, keep, got, own_core, own_depth, own_rows, *messages):
    half = n_ia * n_ka
    depth = keep[half + n_ka] + got[half + n_ka]
    flat, exponent = scaled(depth)
    own_depth[...] = flat * power_of(exponent)[:1]
    own_core[...] = keep[:n_ka] + got[:n_ka]
    own_rows[...] = keep[half : half + n_ka] + got[half : half + n_ka]
    for mask in range(1, n_ia):
        lines = slice(mask * n_ka, (mask + 1) * n_ka)
        core = (keep[lines] + got[lines]).reshape(-1, depth.shape[1])
        fill_message(messages[mask - 1], scaled(core), (flat, exponent))


def after_cores(n_ia, n_ka, keep, got):
    _, rank, lanes = keep.shape
    outs = [jax.ShapeDtypeStruct(shape, f32) for shape in ((n_ka, rank, lanes), (rank, lanes), (n_ka, rank, lanes))]
    outs += [message_shape(n_ka + 1, rank, lanes)] * (n_ia - 1)
    outs = vmem_call(functools.partial(after_cores_kernel, n_ia, n_ka), tuple(outs), keep, got, name="after_cores")
    return outs[0], outs[1], outs[2], outs[3:]


def after_rows_kernel(n_ia, n_ka, own_core, own_depth, own_rows, cols_sum, *refs):
    messages, depth_out, outs = refs[: n_ia - 1], refs[n_ia - 1], refs[n_ia:]
    count, rank, lanes = own_core.shape
    core = own_core[...].reshape(count * rank, lanes)
    depths = [own_depth[...]]
    for message in messages:
        core = core + message_part(message, 0, count * rank, 0)
        depths.append(message_part(message, count * rank, rank, 1))
    depth_out[...] = tree_sum(depths)
    flat, exponent = scaled(core)
    for mask in range(n_ka):
        fill_message(outs[mask], (flat, exponent), scaled(own_rows[mask]), scaled(cols_sum[mask]))


def after_rows(n_ia, n_ka, own_core, own_depth, own_rows, cols_sum, messages):
    count, rank, lanes = own_core.shape
    outs = (jax.ShapeDtypeStruct((rank, lanes), f32),) + (message_shape(count + 2, rank, lanes),) * n_ka
    outs = vmem_call(
        functools.partial(after_rows_kernel, n_ia, n_ka),
        outs,
        own_core,
        own_depth,
        own_rows,
        cols_sum,
        *messages,
        name="after_rows",
    )
    return outs[0], outs[1:]


def after_depths_kernel(n_ka, rank, *refs):
    messages, out, rows_out = refs[:n_ka], refs[-2], refs[-1]
    cores = []
    for mask, message in enumerate(messages):
        part = message_part(message, 0, n_ka * rank, 0)
        cores.append(jnp.concatenate([part[(at ^ mask) * rank : ((at ^ mask) + 1) * rank] for at in range(n_ka)]))
    rows_out[...] = tree_sum(message_part(message, n_ka * rank, rank, 1) for message in messages)
    cols = tree_sum(message_part(message, (n_ka + 1) * rank, rank, 2) for message in messages)
    fill_message(out, scaled(tree_sum(cores)), scaled(cols))


def after_depths(n_ka, rank, messages):
    lanes = messages[0].shape[1]
    outs = (message_shape(n_ka + 1, rank, lanes), jax.ShapeDtypeStruct((rank, lanes), f32))
    return vmem_call(functools.partial(after_depths_kernel, n_ka, rank), outs, *messages, name="after_depths")


def unpack_kernel(sizes, rank, first_message, *refs):
    n_ia, n_ka = sizes["ia"], sizes["ka"]
    messages = refs[:n_ia]
    core_out, *cols_out, whole, sems = refs[n_ia if first_message == 0 else n_ia + 1 :]
    pairs = rank // 2
    own = masks_of(True, sizes)[2]
    copies = []
    for at in range(n_ia):
        first = pl.multiple_of(((own // n_ka) ^ (first_message + at)) * n_ka, n_ka)
        for mask in range(n_ka):
            piece = message_part(messages[at], mask * rank, rank, 0)
            line = lax.rem(own, n_ka) ^ mask
            whole[at, 0, line] = piece[:, :rank]
            whole[at, 1, line] = piece[:, rank:]
        for h in range(2):
            lines = pl.ds(h * pairs + first, n_ka)
            copies.append(pltpu.make_async_copy(whole.at[at, h], core_out.at[lines], sems.at[2 * at + h]))
            copies[-1].start()
    for out in cols_out:
        out[...] = tree_sum(message_part(message, n_ka * rank, rank, 1) for message in messages)
    for copy in copies:
        copy.wait()


def unpack(sizes, rank, messages, core=None):
    lanes = messages[0].shape[1]
    near = core is None
    out_shape = [jax.ShapeDtypeStruct((rank, rank, rank), f32)]
    out_specs = [pl.BlockSpec(memory_space=pltpu.HBM)]
    if near:
        out_shape.append(jax.ShapeDtypeStruct((rank, lanes), f32))
        out_specs.append(pl.BlockSpec(memory_space=pltpu.VMEM))
    return pl.pallas_call(
        functools.partial(unpack_kernel, sizes, rank, 0 if near else sizes["ia"]),
        out_shape=tuple(out_shape),
        in_specs=[pl.BlockSpec(memory_space=pltpu.VMEM)] * len(messages)
        + ([] if near else [pl.BlockSpec(memory_space=pltpu.HBM)]),
        out_specs=tuple(out_specs),
        scratch_shapes=[
            pltpu.VMEM((len(messages), 2, sizes["ka"], rank, rank), f32),
            pltpu.SemaphoreType.DMA((2 * len(messages),)),
        ],
        input_output_aliases={} if near else {len(messages): 0},
        compiler_params=pltpu.CompilerParams(vmem_limit_bytes=24 * 2**20),
        cost_estimate=pl.CostEstimate(flops=10**6, bytes_accessed=4 * 2**20, transcendentals=0),
        name="unpack_near" if near else "unpack_far",
    )(*messages, *([] if near else [core]))


def power_of_two(n):
    return n & (n - 1) == 0


def swap(value, axis, size, mask):
    return lax.ppermute(value, axis, [(at, at ^ mask) for at in range(size)])


def on_device(sizes, observed, weights, coords, counts, factor_rows, factor_cols, factor_depth, core_tensor):
    n_ia, n_ja, n_ka = sizes["ia"], sizes["ja"], sizes["ka"]
    devices = n_ia * n_ja * n_ka
    rank = core_tensor.shape[0]
    _, _, slots, rows, slab, cols = observed.shape
    data = pltpu.with_memory_space_constraint(observed.reshape(observed.shape[2:]), pltpu.HBM)
    weight = pltpu.with_memory_space_constraint(weights.reshape(weights.shape[2:]), pltpu.HBM)
    core_here = pltpu.with_memory_space_constraint(core_tensor, pltpu.HBM)
    depth_here = pltpu.with_memory_space_constraint(factor_depth, pltpu.HBM)
    row_chunks = factor_rows.shape[1] * n_ja * n_ka // rows
    col_chunks = factor_cols.shape[1] * n_ka // cols
    depth_blocks = factor_depth.shape[1] // n_ka // slab
    ia, ja, ka = lax.axis_index("ia"), lax.axis_index("ja"), lax.axis_index("ka")
    by_swaps = (
        n_ja == 2
        and power_of_two(n_ia)
        and power_of_two(n_ka)
        and rank // 2 == devices
        and factor_rows.shape[1] == rows
        and factor_cols.shape[1] == cols
        and rows == cols == 2 * rank == depth_blocks * slab
    )

    if by_swaps:
        own = jnp.stack([factor_rows, swap(factor_rows, "ja", n_ja, 1), factor_cols])
        pieces = [own] + [swap(own, "ka", n_ka, mask) for mask in range(1, n_ka)]
        row_spots = [(mask, line) for line in range(n_ja) for mask in range(n_ka)]
        col_spots = [(mask, n_ja) for mask in range(n_ka)]
    else:
        row_table = lax.all_gather(factor_rows, ("ja", "ka"), axis=1, tiled=True)
        row_table = row_table.reshape(rank, row_chunks, rows).transpose(1, 0, 2)
        col_table = lax.all_gather(factor_cols, "ka", axis=1, tiled=True)
        col_table = col_table.reshape(rank, col_chunks, cols).transpose(1, 0, 2)
        pieces = [row_table, col_table]
        row_spots = [(0, line) for line in range(row_chunks)]
        own = row_table
        col_spots = [(1, line) for line in range(col_chunks)]

    cube, cube_turned, core_pairs, own_depth, coords, spread = first_cubes(
        own,
        depth_here,
        core_here,
        pltpu.with_memory_space_constraint(coords.transpose(0, 3, 1, 2), pltpu.HBM),
        data,
        weight,
        depth_blocks,
    )
    *sums, cols_sum, _ = terms(
        by_swaps,
        sizes,
        row_spots,
        col_spots,
        counts,
        coords,
        data,
        weight,
        cube,
        cube_turned,
        pieces,
        core_pairs,
        own_depth,
        spread,
    )

    if not by_swaps:
        core_sum, rows_sum, depth_sum = sums
        rows_whole = rows_sum.transpose(1, 0, 2).reshape(rank, row_chunks * rows)
        cols_whole = cols_sum.transpose(1, 0, 2).reshape(rank, col_chunks * cols)
        core_whole = core_sum.reshape(rank // 2, rank, 2, rank).transpose(2, 0, 1, 3).reshape(rank, rank, rank)
        return (
            lax.psum_scatter(rows_whole, ("ja", "ka"), scatter_dimension=1, tiled=True),
            lax.psum_scatter(lax.psum(cols_whole, "ia"), "ka", scatter_dimension=1, tiled=True),
            lax.psum(depth_sum, ("ia", "ja")),
            lax.psum(core_whole, ("ia", "ja", "ka")),
        )

    keep, send = sums
    got = swap(send, "ja", n_ja, 1)
    own_core, own_depth, own_rows, messages = after_cores(n_ia, n_ka, keep, got)
    messages = [swap(message.astype(wire), "ia", n_ia, at + 1).astype(f32) for at, message in enumerate(messages)]
    depth_total, messages = after_rows(n_ia, n_ka, own_core, own_depth, own_rows, cols_sum, messages)
    messages = [messages[0]] + [
        swap(messages[mask].astype(wire), "ka", n_ka, mask).astype(f32) for mask in range(1, n_ka)
    ]
    message, rows_total = after_depths(n_ka, rank, messages)
    sent = message.astype(wire)
    sent = [sent] + [swap(sent, "ia", n_ia, mask) for mask in range(1, n_ia)]
    other = [swap(each, "ja", n_ja, 1) for each in sent]
    core_near, cols_total = unpack(sizes, rank, [each.astype(f32) for each in sent])
    (core_total,) = unpack(sizes, rank, [each.astype(f32) for each in other], core_near)
    return (rows_total, cols_total, depth_total, core_total)


def solution(mesh):
    in_specs = (
        P("ia", "ja", "ka", None, None, None),
        P("ia", "ja", "ka", None, None, None),
        P("ia", "ja", "ka", None),
        P("ia", "ja", "ka"),
        P(None, ("ia", "ja", "ka")),
        P(None, ("ja", "ka")),
        P(),
        P(),
    )
    out_specs = (P(None, ("ia", "ja", "ka")), P(None, ("ja", "ka")), P(None, "ka"), P())
    return jax.shard_map(
        functools.partial(on_device, dict(mesh.shape)),
        mesh=mesh,
        in_specs=in_specs,
        out_specs=out_specs,
        check_vma=False,
    )
```

```python
import functools

import jax
import jax.numpy as jnp
from jax import lax
from jax.experimental import pallas as pl
from jax.experimental.pallas import tpu as pltpu
from jax.sharding import PartitionSpec as P

resid_scale = 1.0 / 64.0
f32 = jnp.float32
bf16 = jnp.bfloat16
wire = jnp.float16


def dot(a, b, contract=((1,), (0,))):
    return lax.dot_general(a, b, (contract, ((), ())), preferred_element_type=f32)


def spread_out(source, target):
    rows, slab, _ = source.shape
    for i in range(rows):
        target[i * (slab + 1) : i * (slab + 1) + slab, :] = source[i].astype(f32)


def cube_kernel(
    slab,
    after,
    factor_depth,
    core,
    coords,
    data,
    weight,
    cube_out,
    cube_turned_out,
    core_out,
    depth_out,
    coords_out,
    spread,
    depth_here,
    core_here,
    fetched,
    cube_wide,
    sems,
):
    pairs, _, rank = core_out.shape
    half = slab // 2
    depth_blocks = cube_out.shape[0]
    width = depth_here.shape[1]
    start = pl.multiple_of(lax.axis_index("ka") * width, width)
    copies = [
        pltpu.make_async_copy(factor_depth.at[:, pl.ds(start, width)], depth_here, sems.at[0]),
        pltpu.make_async_copy(core, core_here, sems.at[1]),
        pltpu.make_async_copy(coords, coords_out, sems.at[2]),
        pltpu.make_async_copy(data.at[0], fetched.at[0], sems.at[3]),
        pltpu.make_async_copy(weight.at[0], fetched.at[1], sems.at[4]),
    ]
    for copy in copies:
        copy.start()
    copies[0].wait()
    depth = depth_here[...].astype(f32).T.astype(bf16)
    depth_out[...] = depth
    order = [depth[t * slab + h * half : t * slab + (h + 1) * half] for h in range(2) for t in range(depth_blocks)]
    ordered = jnp.concatenate(order, axis=0)
    count = depth_blocks * half
    copies[1].wait()
    for pair in range(pairs):
        core_out[pair] = jnp.concatenate([core_here[pair], core_here[pairs + pair]], axis=0)

    def one_pair(pair, carry):
        piece = dot(ordered, core_out[pair], ((1,), (1,)))
        for which in range(2):
            here = piece[:, which * rank : (which + 1) * rank]
            wide = jnp.concatenate([here[:count], here[count:]], axis=1)
            cube_wide[pl.ds(which * pairs + pair, count, stride=rank + 1), :] = wide
        return carry

    lax.fori_loop(0, pairs, one_pair, 0, unroll=8)
    for t in range(depth_blocks):
        for kp in range(half):
            at = (t * half + kp) * (rank + 1)
            block = cube_wide[at : at + rank, :]
            cube_out[t, kp * rank : (kp + 1) * rank, :] = block.astype(bf16)
        cube_turned_out[t] = cube_out[t].astype(f32).T.astype(bf16)
    for copy in copies[2:]:
        copy.wait()
    for at in range(2):
        spread_out(fetched.at[at], spread.at[at])


def first_cubes(after, factor_depth, core, coords, data, weight, depth_blocks):
    rank = core.shape[0]
    _, rows, slab, cols = data.shape
    half = slab // 2
    width = depth_blocks * slab
    return pl.pallas_call(
        functools.partial(cube_kernel, slab),
        out_shape=(
            jax.ShapeDtypeStruct((depth_blocks, half * rank, 2 * rank), bf16),
            jax.ShapeDtypeStruct((depth_blocks, 2 * rank, half * rank), bf16),
            jax.ShapeDtypeStruct((rank // 2, 2 * rank, rank), bf16),
            jax.ShapeDtypeStruct((width, rank), bf16),
            jax.ShapeDtypeStruct(coords.shape, coords.dtype),
            jax.ShapeDtypeStruct((2, rows * (slab + 1), cols), f32),
        ),
        in_specs=[pl.BlockSpec(memory_space=pl.ANY)] + [pl.BlockSpec(memory_space=pltpu.HBM)] * 5,
        out_specs=[pl.BlockSpec(memory_space=pltpu.VMEM)] * 4
        + [pl.BlockSpec(memory_space=pltpu.SMEM), pl.BlockSpec(memory_space=pltpu.VMEM)],
        scratch_shapes=[
            pltpu.VMEM((rank, width), bf16),
            pltpu.VMEM(core.shape, bf16),
            pltpu.VMEM((2, rows, slab, cols), bf16),
            pltpu.VMEM((depth_blocks * half * (rank + 1), 2 * rank), f32),
            pltpu.SemaphoreType.DMA((5,)),
        ],
        compiler_params=pltpu.CompilerParams(vmem_limit_bytes=40 * 2**20),
        cost_estimate=pl.CostEstimate(flops=10**9, bytes_accessed=4 * 2**20, transcendentals=0),
        name="first_cubes",
    )(after, factor_depth, core, coords, data, weight)


def masks_of(relative, sizes):
    ia, ja, ka = lax.axis_index("ia"), lax.axis_index("ja"), lax.axis_index("ka")
    if not relative:
        return 0, 0, 0
    return ja * sizes["ka"] + ka, ka, (ja * sizes["ia"] + ia) * sizes["ka"] + ka


def terms_kernel(relative, sizes, row_spots, col_spots, counts, coords, data, weight, cube, cube_turned, *refs):
    pieces = refs[: 1 + max(at for at, _ in row_spots + col_spots)]
    (
        core,
        depth_turned,
        _,
        *outs,
        cols_out,
        spread,
        rows_out,
        row_table,
        col_table,
        wide_col,
        backward,
        by_rank,
        second_all,
        depth_all,
        depth_sum,
        fetched,
        sems,
    ) = refs[len(pieces) :]
    slots, rows, slab, cols = data.shape
    pairs = core.shape[0]
    rank = 2 * pairs
    half = slab // 2
    depth_blocks = cube.shape[0]
    count = counts[0, 0, 0]
    row_mask, col_mask, core_mask = masks_of(relative, sizes)
    row_base = lax.axis_index("ia") * row_table.shape[0]
    col_base = lax.axis_index("ja") * col_table.shape[0]
    depth_base = lax.axis_index("ka") * depth_blocks

    def fetches(slot):
        side = lax.rem(slot, 2)
        return [
            pltpu.make_async_copy(source.at[slot], fetched.at[side, which], sems.at[side, which])
            for which, source in enumerate((data, weight))
        ]

    def fetch(slot):
        @pl.when(slot < count)
        def _():
            for copy in fetches(slot):
                copy.start()

    def arrive(slot):
        for copy in fetches(slot):
            copy.wait()

    for s in range(slots):

        @pl.when(s >= count)
        def _():
            lines = slice(s * slab, (s + 1) * slab)
            second_all[:, lines, :] = jnp.zeros((pairs, slab, 2 * rank), bf16)
            depth_all[lines, :] = jnp.zeros((slab, rank), bf16)

    depth_sum[...] = jnp.zeros_like(depth_sum)
    rows_out[...] = jnp.zeros_like(rows_out)
    cols_out[...] = jnp.zeros_like(cols_out)
    wide_col[...] = jnp.zeros_like(wide_col)
    for spots, table in ((row_spots, row_table), (col_spots, col_table)):
        for at, (piece, line) in enumerate(spots):
            table[at] = pieces[piece][line]

    def one_slot(slot, carry):
        fetch(slot + 1)

        @pl.when(slot > 0)
        def _():
            arrive(slot)
            for which in range(2):
                spread_out(fetched.at[lax.rem(slot, 2), which], spread.at[which])

        row_at = (coords[0, 0, 0, slot] - row_base) ^ row_mask
        col_at = (coords[0, 1, 0, slot] - col_base) ^ col_mask
        depth_at = coords[0, 2, 0, slot] - depth_base
        row_factor = row_table[row_at]
        row_turned = row_factor.astype(f32).T.astype(bf16)
        col_factor = col_table[col_at]
        wide_col[:rank, :cols] = col_factor
        wide_col[rank:, cols:] = col_factor
        own_depth = depth_turned[pl.ds(pl.multiple_of(depth_at * slab, slab), slab), :]
        depth_all[pl.ds(pl.multiple_of(slot * slab, slab), slab), :] = own_depth

        step = 8
        groups = half // step
        wide_factor = wide_col[...]
        def second_of(g):
            lines = cube[depth_at, g * step * rank : (g + 1) * step * rank, :]
            block = dot(lines, wide_factor).astype(bf16)
            return jnp.concatenate([block[kp * rank : (kp + 1) * rank] for kp in range(step)], axis=1)

        def residual_of(g, model):
            parts = []
            for kp in range(step):
                for h in range(2):
                    lines = pl.ds(h * half + g * step + kp, rows, stride=slab + 1)
                    seen, scale = spread[0, lines, :], spread[1, lines, :]
                    at = (kp * 2 + h) * cols
                    gap = model[:, at : at + cols] - seen
                    parts.append((scale * gap * resid_scale).astype(bf16))
            return jnp.concatenate(parts, axis=1)

        def keep_back(g, back):
            back = back.astype(bf16)
            for kp in range(step):
                pair = back[:, kp * 2 * cols : (kp + 1) * 2 * cols]
                at = (g * step + kp) * rank
                backward[at : at + rank, :] = pair
                wider = pair.astype(f32)
                for h in range(2):
                    lines = pl.ds(h * half + g * step + kp, rank, stride=slab + 1)
                    by_rank[lines, :] = wider[:, h * cols : (h + 1) * cols]

        row_sum = jnp.zeros((rows, rank), f32)
        seconds = [second_of(g) for g in range(groups)]
        models = [None] * groups
        models[0] = dot(row_turned, seconds[0])
        for g in range(groups):
            if g + 1 < groups:
                models[g + 1] = dot(row_turned, seconds[g + 1])
            residual = residual_of(g, models[g])
            keep_back(g, dot(row_factor, residual))
            row_sum = row_sum + dot(residual, seconds[g], ((1,), (1,)))
        rows_out[row_at] += row_sum.T
        wide = dot(cube_turned[depth_at], backward[...])
        cols_out[col_at] += wide[:rank, :cols] + wide[rank:, cols:]
        lines = pl.ds(pl.multiple_of(slot * slab, slab), slab)
        for first in range(0, pairs, 8):
            ranked = []
            for pair in range(first, first + 8):
                spots = [at * (slab + 1) for at in (pair, pairs + pair)]
                ranked.append(jnp.concatenate([by_rank[at : at + slab, :].astype(bf16) for at in spots], axis=1))
            ranked = jnp.concatenate(ranked, axis=0)
            second_back = dot(ranked, wide_col[...], ((1,), (1,))).astype(bf16)
            second_all[first : first + 8, lines, :] = second_back.reshape(8, slab, 2 * rank)

        return carry

    lax.fori_loop(0, count, one_slot, 0)

    if relative:
        sides = [(outs[0], 0), (outs[1], 0)]
        core_spots = [sides[at // (pairs // 2)] + (at % (pairs // 2),) for at in range(pairs)]
        row_count = len(row_spots) // 2
        row_places = [sides[at // row_count] + (pairs // 2 + at % row_count,) for at in range(2 * row_count)]
    else:
        core_spots = [(outs[0], 0, at) for at in range(pairs)]
        row_places = [(outs[1], 0, at) for at in range(len(row_spots))]
    deep = jnp.concatenate([second_all[pair] for pair in range(pairs)], axis=1)
    total = dot(deep, core[...].reshape(pairs * 2 * rank, rank))
    for at in range(pairs):
        pair = at ^ core_mask
        second = second_all[pair]
        piece = dot(second, depth_all[...], ((0,), (0,)))
        out, _, line = core_spots[at]
        out[line] = jnp.concatenate([piece[:rank], piece[rank:]], axis=1)
    for at, (out, _, line) in enumerate(row_places):
        out[line] = rows_out[at]
    for s in range(slots):

        @pl.when(s < count)
        def _():
            at = coords[0, 2, 0, s] - depth_base
            lines = pl.ds(pl.multiple_of(at * slab, slab), slab)
            depth_sum[lines, :] += total[s * slab : (s + 1) * slab]

    depth = depth_sum[...].T
    if relative:
        for out in outs:
            out[pairs // 2 + row_count] = depth
    else:
        outs[2][...] = depth


def terms(relative, sizes, row_spots, col_spots, counts, coords, data, weight, cube, cube_turned, pieces, core, depth, spread):
    slots, rows, slab, cols = data.shape
    rank = core.shape[2]
    half = slab // 2
    depth_blocks = cube.shape[0]

    width = depth_blocks * slab
    if relative:
        chunks = (rank // 2 + len(row_spots)) // 2 + 1
        outs = (jax.ShapeDtypeStruct((chunks, rank, rows), f32),) * 2
    else:
        outs = (
            jax.ShapeDtypeStruct((rank // 2, rank, 2 * rank), f32),
            jax.ShapeDtypeStruct((len(row_spots), rank, rows), f32),
            jax.ShapeDtypeStruct((rank, width), f32),
        )
    outs += (
        jax.ShapeDtypeStruct((len(col_spots), rank, cols), f32),
        jax.ShapeDtypeStruct(spread.shape, f32),
    )
    return pl.pallas_call(
        functools.partial(terms_kernel, relative, sizes, row_spots, col_spots),
        out_shape=outs,
        grid_spec=pltpu.PrefetchScalarGridSpec(
            num_scalar_prefetch=0,
            grid=(),
            in_specs=[pl.BlockSpec(memory_space=pltpu.SMEM)] * 2
            + [pl.BlockSpec(memory_space=pltpu.HBM)] * 2
            + [pl.BlockSpec(memory_space=pltpu.VMEM)] * (5 + len(pieces)),
            out_specs=[pl.BlockSpec(memory_space=pltpu.VMEM)] * len(outs),
            scratch_shapes=[
                pltpu.VMEM((len(row_spots), rank, rows), f32),
                pltpu.VMEM((len(row_spots), rank, rows), bf16),
                pltpu.VMEM((len(col_spots), rank, cols), bf16),
                pltpu.VMEM((2 * rank, 2 * cols), bf16),
                pltpu.VMEM((half * rank, 2 * cols), bf16),
                pltpu.VMEM((rank * (slab + 1), cols), f32),
                pltpu.VMEM((rank // 2, slots * slab, 2 * rank), bf16),
                pltpu.VMEM((slots * slab, rank), bf16),
                pltpu.VMEM((depth_blocks * slab, rank), f32),
                pltpu.VMEM((2, 2, rows, slab, cols), bf16),
                pltpu.SemaphoreType.DMA((2, 2)),
            ],
        ),
        input_output_aliases={8 + len(pieces): len(outs) - 1},
        compiler_params=pltpu.CompilerParams(vmem_limit_bytes=40 * 2**20),
        cost_estimate=pl.CostEstimate(flops=10**9, bytes_accessed=16 * 2**20, transcendentals=0),
        name="terms",
    )(counts, coords, data, weight, cube, cube_turned, *pieces, core, depth, spread)


mark_rows = 16
top_exponent = 14.0


def vmem_call(kernel, out_shape, *operands, name):
    return pl.pallas_call(
        kernel,
        out_shape=out_shape,
        in_specs=[pl.BlockSpec(memory_space=pltpu.VMEM)] * len(operands),
        out_specs=jax.tree.map(lambda _: pl.BlockSpec(memory_space=pltpu.VMEM), out_shape),
        compiler_params=pltpu.CompilerParams(vmem_limit_bytes=24 * 2**20),
        name=name,
    )(*operands)


def power_of(exponent):
    whole = jnp.abs(exponent).astype(jnp.int32)
    value = jnp.ones_like(exponent)
    for bit in range(7):
        factor = jnp.where(exponent < 0, f32(2.0 ** -(2**bit)), f32(2.0 ** (2**bit)))
        value = value * jnp.where((whole >> bit) & 1 == 1, factor, f32(1.0))
    return value


def exponent_of(value):
    lanes = value.shape[-1]
    largest = jnp.max(jnp.max(jnp.abs(value.reshape(-1, 8, lanes)), axis=0), axis=0, keepdims=True)
    largest = jnp.max(largest, axis=1, keepdims=True)
    largest = jnp.broadcast_to(jnp.maximum(largest, f32(1e-30)), (8, lanes))
    return jnp.ceil(jnp.log(largest) * f32(1.4426950408889634)) - f32(top_exponent)


def rounded(value):
    stretched = value * f32(8193.0)
    return stretched - (stretched - value)


def scaled(value):
    exponent = exponent_of(value)
    return rounded(value * power_of(-exponent)[:1]), exponent


def fill_message(out, *parts):
    at = 0
    mark = None
    for which, (flat, exponent) in enumerate(parts):
        out[at : at + flat.shape[0], :] = flat
        at += flat.shape[0]
        exponent = jnp.broadcast_to(exponent[:1], (mark_rows, flat.shape[1]))
        line = lax.broadcasted_iota(jnp.int32, exponent.shape, 0)
        mark = exponent if mark is None else jnp.where(line >= which, exponent, mark)
    out[at : at + mark_rows, :] = mark


def message_part(message, start, rows, part):
    mark = message.shape[0] - mark_rows + part
    return message[start : start + rows, :] * power_of(message[mark : mark + 1, :])


def message_shape(chunks, rank, lanes):
    return jax.ShapeDtypeStruct((chunks * rank + mark_rows, lanes), f32)


def tree_sum(values):
    values = list(values)
    while len(values) > 1:
        values = [values[at] + values[at + 1] for at in range(0, len(values), 2)]
    return values[0]


def after_cores_kernel(n_ia, n_ka, keep, got, own_core, own_depth, own_rows, *messages):
    half = n_ia * n_ka
    depth = keep[half + n_ka] + got[half + n_ka]
    flat, exponent = scaled(depth)
    own_depth[...] = flat * power_of(exponent)[:1]
    own_core[...] = keep[:n_ka] + got[:n_ka]
    own_rows[...] = keep[half : half + n_ka] + got[half : half + n_ka]
    for mask in range(1, n_ia):
        lines = slice(mask * n_ka, (mask + 1) * n_ka)
        core = (keep[lines] + got[lines]).reshape(-1, depth.shape[1])
        fill_message(messages[mask - 1], scaled(core), (flat, exponent))


def after_cores(n_ia, n_ka, keep, got):
    _, rank, lanes = keep.shape
    outs = [jax.ShapeDtypeStruct(shape, f32) for shape in ((n_ka, rank, lanes), (rank, lanes), (n_ka, rank, lanes))]
    outs += [message_shape(n_ka + 1, rank, lanes)] * (n_ia - 1)
    outs = vmem_call(functools.partial(after_cores_kernel, n_ia, n_ka), tuple(outs), keep, got, name="after_cores")
    return outs[0], outs[1], outs[2], outs[3:]


def after_rows_kernel(n_ia, n_ka, own_core, own_depth, own_rows, cols_sum, *refs):
    messages, depth_out, outs = refs[: n_ia - 1], refs[n_ia - 1], refs[n_ia:]
    count, rank, lanes = own_core.shape
    core = own_core[...].reshape(count * rank, lanes)
    depths = [own_depth[...]]
    for message in messages:
        core = core + message_part(message, 0, count * rank, 0)
        depths.append(message_part(message, count * rank, rank, 1))
    depth_out[...] = tree_sum(depths)
    flat, exponent = scaled(core)
    for mask in range(n_ka):
        fill_message(outs[mask], (flat, exponent), scaled(own_rows[mask]), scaled(cols_sum[mask]))


def after_rows(n_ia, n_ka, own_core, own_depth, own_rows, cols_sum, messages):
    count, rank, lanes = own_core.shape
    outs = (jax.ShapeDtypeStruct((rank, lanes), f32),) + (message_shape(count + 2, rank, lanes),) * n_ka
    outs = vmem_call(
        functools.partial(after_rows_kernel, n_ia, n_ka),
        outs,
        own_core,
        own_depth,
        own_rows,
        cols_sum,
        *messages,
        name="after_rows",
    )
    return outs[0], outs[1:]


def after_depths_kernel(n_ka, rank, *refs):
    messages, out, rows_out = refs[:n_ka], refs[-2], refs[-1]
    cores = []
    for mask, message in enumerate(messages):
        part = message_part(message, 0, n_ka * rank, 0)
        cores.append(jnp.concatenate([part[(at ^ mask) * rank : ((at ^ mask) + 1) * rank] for at in range(n_ka)]))
    rows_out[...] = tree_sum(message_part(message, n_ka * rank, rank, 1) for message in messages)
    cols = tree_sum(message_part(message, (n_ka + 1) * rank, rank, 2) for message in messages)
    fill_message(out, scaled(tree_sum(cores)), scaled(cols))


def after_depths(n_ka, rank, messages):
    lanes = messages[0].shape[1]
    outs = (message_shape(n_ka + 1, rank, lanes), jax.ShapeDtypeStruct((rank, lanes), f32))
    return vmem_call(functools.partial(after_depths_kernel, n_ka, rank), outs, *messages, name="after_depths")


def unpack_kernel(sizes, rank, first_message, count, with_cols, *refs):
    n_ka = sizes["ka"]
    messages, refs = refs[:count], refs[count:]
    cols_from, refs = refs[:with_cols], refs[with_cols:]
    core_out, *cols_out, whole, sems = refs[0 if first_message == 0 else 1 :]
    pairs = rank // 2
    own = masks_of(True, sizes)[2]
    copies = []
    for at in range(count):
        first = pl.multiple_of(((own // n_ka) ^ (first_message + at)) * n_ka, n_ka)
        for mask in range(n_ka):
            piece = message_part(messages[at], mask * rank, rank, 0)
            line = lax.rem(own, n_ka) ^ mask
            whole[at, 0, line] = piece[:, :rank]
            whole[at, 1, line] = piece[:, rank:]
        for h in range(2):
            lines = pl.ds(h * pairs + first, n_ka)
            copies.append(pltpu.make_async_copy(whole.at[at, h], core_out.at[lines], sems.at[2 * at + h]))
            copies[-1].start()
    if with_cols:
        cols_out[0][...] = tree_sum(message_part(message, n_ka * rank, rank, 1) for message in cols_from)
    for copy in copies:
        copy.wait()


def unpack(sizes, rank, first_message, messages, core=None, cols_from=()):
    lanes = messages[0].shape[1]
    count = len(messages)
    given = [] if core is None else [core]
    out_shape = [jax.ShapeDtypeStruct((rank, rank, rank), f32)]
    out_specs = [pl.BlockSpec(memory_space=pltpu.HBM)]
    if cols_from:
        out_shape.append(jax.ShapeDtypeStruct((rank, lanes), f32))
        out_specs.append(pl.BlockSpec(memory_space=pltpu.VMEM))
    return pl.pallas_call(
        functools.partial(unpack_kernel, sizes, rank, first_message, count, len(cols_from)),
        out_shape=tuple(out_shape),
        in_specs=[pl.BlockSpec(memory_space=pltpu.VMEM)] * (count + len(cols_from))
        + [pl.BlockSpec(memory_space=pltpu.HBM)] * len(given),
        out_specs=tuple(out_specs),
        scratch_shapes=[
            pltpu.VMEM((count, 2, sizes["ka"], rank, rank), f32),
            pltpu.SemaphoreType.DMA((2 * count,)),
        ],
        input_output_aliases={count + len(cols_from): 0} if given else {},
        compiler_params=pltpu.CompilerParams(vmem_limit_bytes=24 * 2**20),
        cost_estimate=pl.CostEstimate(flops=10**6, bytes_accessed=4 * 2**20, transcendentals=0),
        name=f"unpack_{first_message}",
    )(*messages, *cols_from, *given)


def power_of_two(n):
    return n & (n - 1) == 0


def swap(value, axis, size, mask):
    return lax.ppermute(value, axis, [(at, at ^ mask) for at in range(size)])


def on_device(sizes, observed, weights, coords, counts, factor_rows, factor_cols, factor_depth, core_tensor):
    n_ia, n_ja, n_ka = sizes["ia"], sizes["ja"], sizes["ka"]
    devices = n_ia * n_ja * n_ka
    rank = core_tensor.shape[0]
    _, _, slots, rows, slab, cols = observed.shape
    data = pltpu.with_memory_space_constraint(observed.reshape(observed.shape[2:]), pltpu.HBM)
    weight = pltpu.with_memory_space_constraint(weights.reshape(weights.shape[2:]), pltpu.HBM)
    core_here = pltpu.with_memory_space_constraint(core_tensor, pltpu.HBM)
    depth_here = pltpu.with_memory_space_constraint(factor_depth, pltpu.HBM)
    row_chunks = factor_rows.shape[1] * n_ja * n_ka // rows
    col_chunks = factor_cols.shape[1] * n_ka // cols
    depth_blocks = factor_depth.shape[1] // n_ka // slab
    ia, ja, ka = lax.axis_index("ia"), lax.axis_index("ja"), lax.axis_index("ka")
    by_swaps = (
        n_ja == 2
        and power_of_two(n_ia)
        and power_of_two(n_ka)
        and rank // 2 == devices
        and factor_rows.shape[1] == rows
        and factor_cols.shape[1] == cols
        and rows == cols == 2 * rank == depth_blocks * slab
    )

    if by_swaps:
        own = jnp.stack([factor_rows, swap(factor_rows, "ja", n_ja, 1), factor_cols])
        pieces = [own] + [swap(own, "ka", n_ka, mask) for mask in range(1, n_ka)]
        row_spots = [(mask, line) for line in range(n_ja) for mask in range(n_ka)]
        col_spots = [(mask, n_ja) for mask in range(n_ka)]
    else:
        row_table = lax.all_gather(factor_rows, ("ja", "ka"), axis=1, tiled=True)
        row_table = row_table.reshape(rank, row_chunks, rows).transpose(1, 0, 2)
        col_table = lax.all_gather(factor_cols, "ka", axis=1, tiled=True)
        col_table = col_table.reshape(rank, col_chunks, cols).transpose(1, 0, 2)
        pieces = [row_table, col_table]
        row_spots = [(0, line) for line in range(row_chunks)]
        own = row_table
        col_spots = [(1, line) for line in range(col_chunks)]

    cube, cube_turned, core_pairs, own_depth, coords, spread = first_cubes(
        own,
        depth_here,
        core_here,
        pltpu.with_memory_space_constraint(coords.transpose(0, 3, 1, 2), pltpu.HBM),
        data,
        weight,
        depth_blocks,
    )
    *sums, cols_sum, _ = terms(
        by_swaps,
        sizes,
        row_spots,
        col_spots,
        counts,
        coords,
        data,
        weight,
        cube,
        cube_turned,
        pieces,
        core_pairs,
        own_depth,
        spread,
    )

    if not by_swaps:
        core_sum, rows_sum, depth_sum = sums
        rows_whole = rows_sum.transpose(1, 0, 2).reshape(rank, row_chunks * rows)
        cols_whole = cols_sum.transpose(1, 0, 2).reshape(rank, col_chunks * cols)
        core_whole = core_sum.reshape(rank // 2, rank, 2, rank).transpose(2, 0, 1, 3).reshape(rank, rank, rank)
        return (
            lax.psum_scatter(rows_whole, ("ja", "ka"), scatter_dimension=1, tiled=True),
            lax.psum_scatter(lax.psum(cols_whole, "ia"), "ka", scatter_dimension=1, tiled=True),
            lax.psum(depth_sum, ("ia", "ja")),
            lax.psum(core_whole, ("ia", "ja", "ka")),
        )

    keep, send = sums
    got = swap(send, "ja", n_ja, 1)
    own_core, own_depth, own_rows, messages = after_cores(n_ia, n_ka, keep, got)
    messages = [swap(message.astype(wire), "ia", n_ia, at + 1).astype(f32) for at, message in enumerate(messages)]
    depth_total, messages = after_rows(n_ia, n_ka, own_core, own_depth, own_rows, cols_sum, messages)
    messages = [messages[0]] + [
        swap(messages[mask].astype(wire), "ka", n_ka, mask).astype(f32) for mask in range(1, n_ka)
    ]
    message, rows_total = after_depths(n_ka, rank, messages)
    sent = message.astype(wire)
    sent = [sent] + [swap(sent, "ia", n_ia, mask) for mask in range(1, n_ia)]
    other = [swap(each, "ja", n_ja, 1) for each in sent]
    near = [message] + [each.astype(f32) for each in sent[1:]]
    (core_own,) = unpack(sizes, rank, 0, near[:1])
    core_near, cols_total = unpack(sizes, rank, 1, near[1:], core_own, near)
    (core_total,) = unpack(sizes, rank, n_ia, [each.astype(f32) for each in other], core_near)
    return (rows_total, cols_total, depth_total, core_total)


def solution(mesh):
    in_specs = (
        P("ia", "ja", "ka", None, None, None),
        P("ia", "ja", "ka", None, None, None),
        P("ia", "ja", "ka", None),
        P("ia", "ja", "ka"),
        P(None, ("ia", "ja", "ka")),
        P(None, ("ja", "ka")),
        P(),
        P(),
    )
    out_specs = (P(None, ("ia", "ja", "ka")), P(None, ("ja", "ka")), P(None, "ka"), P())
    return jax.shard_map(
        functools.partial(on_device, dict(mesh.shape)),
        mesh=mesh,
        in_specs=in_specs,
        out_specs=out_specs,
        check_vma=False,
    )
```

```python
import functools

import jax
import jax.numpy as jnp
from jax import lax
from jax.experimental import pallas as pl
from jax.experimental.pallas import tpu as pltpu
from jax.sharding import PartitionSpec as P

resid_scale = 1.0 / 64.0
f32 = jnp.float32
bf16 = jnp.bfloat16
wire = jnp.float16


def dot(a, b, contract=((1,), (0,))):
    return lax.dot_general(a, b, (contract, ((), ())), preferred_element_type=f32)


def spread_out(source, target):
    rows, slab, _ = source.shape
    for i in range(rows):
        target[i * (slab + 1) : i * (slab + 1) + slab, :] = source[i].astype(f32)


def cube_kernel(
    slab,
    after,
    factor_depth,
    core,
    coords,
    data,
    weight,
    cube_out,
    cube_turned_out,
    core_out,
    depth_out,
    coords_out,
    spread,
    depth_here,
    core_here,
    fetched,
    cube_wide,
    sems,
):
    pairs, _, rank = core_out.shape
    half = slab // 2
    depth_blocks = cube_out.shape[0]
    width = depth_here.shape[1]
    start = pl.multiple_of(lax.axis_index("ka") * width, width)
    copies = [
        pltpu.make_async_copy(factor_depth.at[:, pl.ds(start, width)], depth_here, sems.at[0]),
        pltpu.make_async_copy(core, core_here, sems.at[1]),
        pltpu.make_async_copy(coords, coords_out, sems.at[2]),
        pltpu.make_async_copy(data.at[0], fetched.at[0], sems.at[3]),
        pltpu.make_async_copy(weight.at[0], fetched.at[1], sems.at[4]),
    ]
    for copy in copies:
        copy.start()
    copies[0].wait()
    depth = depth_here[...].astype(f32).T.astype(bf16)
    depth_out[...] = depth
    order = [depth[t * slab + h * half : t * slab + (h + 1) * half] for h in range(2) for t in range(depth_blocks)]
    ordered = jnp.concatenate(order, axis=0)
    count = depth_blocks * half
    copies[1].wait()
    for pair in range(pairs):
        core_out[pair] = jnp.concatenate([core_here[pair], core_here[pairs + pair]], axis=0)

    def one_pair(pair, carry):
        piece = dot(ordered, core_out[pair], ((1,), (1,)))
        for which in range(2):
            here = piece[:, which * rank : (which + 1) * rank]
            wide = jnp.concatenate([here[:count], here[count:]], axis=1)
            cube_wide[pl.ds(which * pairs + pair, count, stride=rank + 1), :] = wide
        return carry

    lax.fori_loop(0, pairs, one_pair, 0, unroll=8)
    for t in range(depth_blocks):
        for kp in range(half):
            at = (t * half + kp) * (rank + 1)
            block = cube_wide[at : at + rank, :]
            cube_out[t, kp * rank : (kp + 1) * rank, :] = block.astype(bf16)
        cube_turned_out[t] = cube_out[t].astype(f32).T.astype(bf16)
    for copy in copies[2:]:
        copy.wait()
    for at in range(2):
        spread_out(fetched.at[at], spread.at[at])


def first_cubes(after, factor_depth, core, coords, data, weight, depth_blocks):
    rank = core.shape[0]
    _, rows, slab, cols = data.shape
    half = slab // 2
    width = depth_blocks * slab
    return pl.pallas_call(
        functools.partial(cube_kernel, slab),
        out_shape=(
            jax.ShapeDtypeStruct((depth_blocks, half * rank, 2 * rank), bf16),
            jax.ShapeDtypeStruct((depth_blocks, 2 * rank, half * rank), bf16),
            jax.ShapeDtypeStruct((rank // 2, 2 * rank, rank), bf16),
            jax.ShapeDtypeStruct((width, rank), bf16),
            jax.ShapeDtypeStruct(coords.shape, coords.dtype),
            jax.ShapeDtypeStruct((2, rows * (slab + 1), cols), f32),
        ),
        in_specs=[pl.BlockSpec(memory_space=pl.ANY)] + [pl.BlockSpec(memory_space=pltpu.HBM)] * 5,
        out_specs=[pl.BlockSpec(memory_space=pltpu.VMEM)] * 4
        + [pl.BlockSpec(memory_space=pltpu.SMEM), pl.BlockSpec(memory_space=pltpu.VMEM)],
        scratch_shapes=[
            pltpu.VMEM((rank, width), bf16),
            pltpu.VMEM(core.shape, bf16),
            pltpu.VMEM((2, rows, slab, cols), bf16),
            pltpu.VMEM((depth_blocks * half * (rank + 1), 2 * rank), f32),
            pltpu.SemaphoreType.DMA((5,)),
        ],
        compiler_params=pltpu.CompilerParams(vmem_limit_bytes=40 * 2**20),
        cost_estimate=pl.CostEstimate(flops=10**9, bytes_accessed=4 * 2**20, transcendentals=0),
        name="first_cubes",
    )(after, factor_depth, core, coords, data, weight)


def masks_of(relative, sizes):
    ia, ja, ka = lax.axis_index("ia"), lax.axis_index("ja"), lax.axis_index("ka")
    if not relative:
        return 0, 0, 0
    return ja * sizes["ka"] + ka, ka, (ja * sizes["ia"] + ia) * sizes["ka"] + ka


def terms_kernel(relative, sizes, row_spots, col_spots, counts, coords, data, weight, cube, cube_turned, *refs):
    pieces = refs[: 1 + max(at for at, _ in row_spots + col_spots)]
    (
        core,
        depth_turned,
        _,
        *outs,
        cols_out,
        spread,
        rows_out,
        row_table,
        col_table,
        wide_col,
        backward,
        by_rank,
        second_all,
        depth_all,
        depth_sum,
        fetched,
        sems,
    ) = refs[len(pieces) :]
    slots, rows, slab, cols = data.shape
    pairs = core.shape[0]
    rank = 2 * pairs
    half = slab // 2
    depth_blocks = cube.shape[0]
    count = counts[0, 0, 0]
    row_mask, col_mask, core_mask = masks_of(relative, sizes)
    row_base = lax.axis_index("ia") * row_table.shape[0]
    col_base = lax.axis_index("ja") * col_table.shape[0]
    depth_base = lax.axis_index("ka") * depth_blocks

    def fetches(slot):
        side = lax.rem(slot, 2)
        return [
            pltpu.make_async_copy(source.at[slot], fetched.at[side, which], sems.at[side, which])
            for which, source in enumerate((data, weight))
        ]

    def fetch(slot):
        @pl.when(slot < count)
        def _():
            for copy in fetches(slot):
                copy.start()

    def arrive(slot):
        for copy in fetches(slot):
            copy.wait()

    for s in range(slots):

        @pl.when(s >= count)
        def _():
            lines = slice(s * slab, (s + 1) * slab)
            second_all[:, lines, :] = jnp.zeros((pairs, slab, 2 * rank), bf16)
            depth_all[lines, :] = jnp.zeros((slab, rank), bf16)

    depth_sum[...] = jnp.zeros_like(depth_sum)
    rows_out[...] = jnp.zeros_like(rows_out)
    cols_out[...] = jnp.zeros_like(cols_out)
    wide_col[...] = jnp.zeros_like(wide_col)
    for spots, table in ((row_spots, row_table), (col_spots, col_table)):
        for at, (piece, line) in enumerate(spots):
            table[at] = pieces[piece][line]

    def one_slot(slot, carry):
        fetch(slot + 1)

        @pl.when(slot > 0)
        def _():
            arrive(slot)
            for which in range(2):
                spread_out(fetched.at[lax.rem(slot, 2), which], spread.at[which])

        row_at = (coords[0, 0, 0, slot] - row_base) ^ row_mask
        col_at = (coords[0, 1, 0, slot] - col_base) ^ col_mask
        depth_at = coords[0, 2, 0, slot] - depth_base
        row_factor = row_table[row_at]
        row_turned = row_factor.astype(f32).T.astype(bf16)
        col_factor = col_table[col_at]
        wide_col[:rank, :cols] = col_factor
        wide_col[rank:, cols:] = col_factor
        own_depth = depth_turned[pl.ds(pl.multiple_of(depth_at * slab, slab), slab), :]
        depth_all[pl.ds(pl.multiple_of(slot * slab, slab), slab), :] = own_depth

        step = 8
        groups = half // step
        wide_factor = wide_col[...]
        def second_of(g):
            lines = cube[depth_at, g * step * rank : (g + 1) * step * rank, :]
            block = dot(lines, wide_factor).astype(bf16)
            return jnp.concatenate([block[kp * rank : (kp + 1) * rank] for kp in range(step)], axis=1)

        def residual_of(g, model):
            parts = []
            for kp in range(step):
                for h in range(2):
                    lines = pl.ds(h * half + g * step + kp, rows, stride=slab + 1)
                    seen, scale = spread[0, lines, :], spread[1, lines, :]
                    at = (kp * 2 + h) * cols
                    gap = model[:, at : at + cols] - seen
                    parts.append((scale * gap * resid_scale).astype(bf16))
            return jnp.concatenate(parts, axis=1)

        def keep_back(g, back):
            back = back.astype(bf16)
            for kp in range(step):
                pair = back[:, kp * 2 * cols : (kp + 1) * 2 * cols]
                at = (g * step + kp) * rank
                backward[at : at + rank, :] = pair
                wider = pair.astype(f32)
                for h in range(2):
                    lines = pl.ds(h * half + g * step + kp, rank, stride=slab + 1)
                    by_rank[lines, :] = wider[:, h * cols : (h + 1) * cols]

        row_sum = jnp.zeros((rows, rank), f32)
        seconds = [second_of(g) for g in range(groups)]
        models = [None] * groups
        models[0] = dot(row_turned, seconds[0])
        for g in range(groups):
            if g + 1 < groups:
                models[g + 1] = dot(row_turned, seconds[g + 1])
            residual = residual_of(g, models[g])
            keep_back(g, dot(row_factor, residual))
            row_sum = row_sum + dot(residual, seconds[g], ((1,), (1,)))
        rows_out[row_at] += row_sum.T
        wide = dot(cube_turned[depth_at], backward[...])
        cols_out[col_at] += wide[:rank, :cols] + wide[rank:, cols:]
        lines = pl.ds(pl.multiple_of(slot * slab, slab), slab)
        for first in range(0, pairs, 8):
            ranked = []
            for pair in range(first, first + 8):
                spots = [at * (slab + 1) for at in (pair, pairs + pair)]
                ranked.append(jnp.concatenate([by_rank[at : at + slab, :].astype(bf16) for at in spots], axis=1))
            ranked = jnp.concatenate(ranked, axis=0)
            second_back = dot(ranked, wide_col[...], ((1,), (1,))).astype(bf16)
            second_all[first : first + 8, lines, :] = second_back.reshape(8, slab, 2 * rank)

        return carry

    lax.fori_loop(0, count, one_slot, 0)

    if relative:
        sides = [(outs[0], 0), (outs[1], 0)]
        core_spots = [sides[at // (pairs // 2)] + (at % (pairs // 2),) for at in range(pairs)]
        row_count = len(row_spots) // 2
        row_places = [sides[at // row_count] + (pairs // 2 + at % row_count,) for at in range(2 * row_count)]
    else:
        core_spots = [(outs[0], 0, at) for at in range(pairs)]
        row_places = [(outs[1], 0, at) for at in range(len(row_spots))]
    total = jnp.zeros((second_all.shape[1], rank), f32)
    for at in range(pairs):
        pair = at ^ core_mask
        second = second_all[pair]
        total = total + dot(second, core[pair])
        piece = dot(second, depth_all[...], ((0,), (0,)))
        out, _, line = core_spots[at]
        out[line] = jnp.concatenate([piece[:rank], piece[rank:]], axis=1)
    for at, (out, _, line) in enumerate(row_places):
        out[line] = rows_out[at]
    for s in range(slots):

        @pl.when(s < count)
        def _():
            at = coords[0, 2, 0, s] - depth_base
            lines = pl.ds(pl.multiple_of(at * slab, slab), slab)
            depth_sum[lines, :] += total[s * slab : (s + 1) * slab]

    depth = depth_sum[...].T
    if relative:
        for out in outs:
            out[pairs // 2 + row_count] = depth
    else:
        outs[2][...] = depth


def terms(relative, sizes, row_spots, col_spots, counts, coords, data, weight, cube, cube_turned, pieces, core, depth, spread):
    slots, rows, slab, cols = data.shape
    rank = core.shape[2]
    half = slab // 2
    depth_blocks = cube.shape[0]

    width = depth_blocks * slab
    if relative:
        chunks = (rank // 2 + len(row_spots)) // 2 + 1
        outs = (jax.ShapeDtypeStruct((chunks, rank, rows), f32),) * 2
    else:
        outs = (
            jax.ShapeDtypeStruct((rank // 2, rank, 2 * rank), f32),
            jax.ShapeDtypeStruct((len(row_spots), rank, rows), f32),
            jax.ShapeDtypeStruct((rank, width), f32),
        )
    outs += (
        jax.ShapeDtypeStruct((len(col_spots), rank, cols), f32),
        jax.ShapeDtypeStruct(spread.shape, f32),
    )
    return pl.pallas_call(
        functools.partial(terms_kernel, relative, sizes, row_spots, col_spots),
        out_shape=outs,
        grid_spec=pltpu.PrefetchScalarGridSpec(
            num_scalar_prefetch=0,
            grid=(),
            in_specs=[pl.BlockSpec(memory_space=pltpu.SMEM)] * 2
            + [pl.BlockSpec(memory_space=pltpu.HBM)] * 2
            + [pl.BlockSpec(memory_space=pltpu.VMEM)] * (5 + len(pieces)),
            out_specs=[pl.BlockSpec(memory_space=pltpu.VMEM)] * len(outs),
            scratch_shapes=[
                pltpu.VMEM((len(row_spots), rank, rows), f32),
                pltpu.VMEM((len(row_spots), rank, rows), bf16),
                pltpu.VMEM((len(col_spots), rank, cols), bf16),
                pltpu.VMEM((2 * rank, 2 * cols), bf16),
                pltpu.VMEM((half * rank, 2 * cols), bf16),
                pltpu.VMEM((rank * (slab + 1), cols), f32),
                pltpu.VMEM((rank // 2, slots * slab, 2 * rank), bf16),
                pltpu.VMEM((slots * slab, rank), bf16),
                pltpu.VMEM((depth_blocks * slab, rank), f32),
                pltpu.VMEM((2, 2, rows, slab, cols), bf16),
                pltpu.SemaphoreType.DMA((2, 2)),
            ],
        ),
        input_output_aliases={8 + len(pieces): len(outs) - 1},
        compiler_params=pltpu.CompilerParams(vmem_limit_bytes=40 * 2**20),
        cost_estimate=pl.CostEstimate(flops=10**9, bytes_accessed=16 * 2**20, transcendentals=0),
        name="terms",
    )(counts, coords, data, weight, cube, cube_turned, *pieces, core, depth, spread)


mark_rows = 16
top_exponent = 14.0


def vmem_call(kernel, out_shape, *operands, name, to_hbm=None):
    spaces = [pltpu.HBM if at == to_hbm else pltpu.VMEM for at in range(len(out_shape))]
    scratch = []
    if to_hbm is not None:
        scratch = [pltpu.VMEM(out_shape[to_hbm].shape, out_shape[to_hbm].dtype), pltpu.SemaphoreType.DMA]
    return pl.pallas_call(
        kernel,
        out_shape=out_shape,
        in_specs=[pl.BlockSpec(memory_space=pltpu.VMEM)] * len(operands),
        out_specs=tuple(pl.BlockSpec(memory_space=space) for space in spaces),
        scratch_shapes=scratch,
        compiler_params=pltpu.CompilerParams(vmem_limit_bytes=24 * 2**20),
        name=name,
    )(*operands)


def power_of(exponent):
    whole = jnp.abs(exponent).astype(jnp.int32)
    value = jnp.ones_like(exponent)
    for bit in range(7):
        factor = jnp.where(exponent < 0, f32(2.0 ** -(2**bit)), f32(2.0 ** (2**bit)))
        value = value * jnp.where((whole >> bit) & 1 == 1, factor, f32(1.0))
    return value


def exponent_of(value):
    lanes = value.shape[-1]
    largest = jnp.max(jnp.max(jnp.abs(value.reshape(-1, 8, lanes)), axis=0), axis=0, keepdims=True)
    largest = jnp.max(largest, axis=1, keepdims=True)
    largest = jnp.broadcast_to(jnp.maximum(largest, f32(1e-30)), (8, lanes))
    return jnp.ceil(jnp.log(largest) * f32(1.4426950408889634)) - f32(top_exponent)


def rounded(value):
    stretched = value * f32(8193.0)
    return stretched - (stretched - value)


def scaled(value):
    exponent = exponent_of(value)
    return rounded(value * power_of(-exponent)[:1]), exponent


def fill_message(out, *parts):
    at = 0
    mark = None
    for which, (flat, exponent) in enumerate(parts):
        out[at : at + flat.shape[0], :] = flat
        at += flat.shape[0]
        exponent = jnp.broadcast_to(exponent[:1], (mark_rows, flat.shape[1]))
        line = lax.broadcasted_iota(jnp.int32, exponent.shape, 0)
        mark = exponent if mark is None else jnp.where(line >= which, exponent, mark)
    out[at : at + mark_rows, :] = mark


def message_part(message, start, rows, part):
    mark = message.shape[0] - mark_rows + part
    return message[start : start + rows, :] * power_of(message[mark : mark + 1, :])


def message_shape(chunks, rank, lanes):
    return jax.ShapeDtypeStruct((chunks * rank + mark_rows, lanes), f32)


def tree_sum(values):
    values = list(values)
    while len(values) > 1:
        values = [values[at] + values[at + 1] for at in range(0, len(values), 2)]
    return values[0]


def after_cores_kernel(n_ia, n_ka, keep, got, own_core, own_depth, own_rows, *messages):
    half = n_ia * n_ka
    depth = keep[half + n_ka] + got[half + n_ka]
    flat, exponent = scaled(depth)
    own_depth[...] = flat * power_of(exponent)[:1]
    own_core[...] = keep[:n_ka] + got[:n_ka]
    own_rows[...] = keep[half : half + n_ka] + got[half : half + n_ka]
    for mask in range(1, n_ia):
        lines = slice(mask * n_ka, (mask + 1) * n_ka)
        core = (keep[lines] + got[lines]).reshape(-1, depth.shape[1])
        fill_message(messages[mask - 1], scaled(core), (flat, exponent))


def after_cores(n_ia, n_ka, keep, got):
    _, rank, lanes = keep.shape
    outs = [jax.ShapeDtypeStruct(shape, f32) for shape in ((n_ka, rank, lanes), (rank, lanes), (n_ka, rank, lanes))]
    outs += [message_shape(n_ka + 1, rank, lanes)] * (n_ia - 1)
    outs = vmem_call(functools.partial(after_cores_kernel, n_ia, n_ka), tuple(outs), keep, got, name="after_cores")
    return outs[0], outs[1], outs[2], outs[3:]


def after_rows_kernel(n_ia, n_ka, own_core, own_depth, own_rows, cols_sum, *refs):
    messages, refs = refs[: n_ia - 1], refs[n_ia - 1 :]
    depth_out, *outs, depth_here, sem = refs
    count, rank, lanes = own_core.shape
    depths = [own_depth[...]] + [message_part(message, count * rank, rank, 1) for message in messages]
    depth_here[...] = tree_sum(depths)
    copy = pltpu.make_async_copy(depth_here, depth_out, sem)
    copy.start()
    core = own_core[...].reshape(count * rank, lanes)
    for message in messages:
        core = core + message_part(message, 0, count * rank, 0)
    flat, exponent = scaled(core)
    for mask in range(n_ka):
        fill_message(outs[mask], (flat, exponent), scaled(own_rows[mask]), scaled(cols_sum[mask]))
    copy.wait()


def after_rows(n_ia, n_ka, own_core, own_depth, own_rows, cols_sum, messages):
    count, rank, lanes = own_core.shape
    outs = (jax.ShapeDtypeStruct((rank, lanes), f32),) + (message_shape(count + 2, rank, lanes),) * n_ka
    outs = vmem_call(
        functools.partial(after_rows_kernel, n_ia, n_ka),
        outs,
        own_core,
        own_depth,
        own_rows,
        cols_sum,
        *messages,
        name="after_rows",
        to_hbm=0,
    )
    return outs[0], outs[1:]


def after_depths_kernel(n_ka, rank, *refs):
    messages, (out, rows_out, rows_here, sem) = refs[:n_ka], refs[n_ka:]
    rows_here[...] = tree_sum(message_part(message, n_ka * rank, rank, 1) for message in messages)
    copy = pltpu.make_async_copy(rows_here, rows_out, sem)
    copy.start()
    cores = []
    for mask, message in enumerate(messages):
        part = message_part(message, 0, n_ka * rank, 0)
        cores.append(jnp.concatenate([part[(at ^ mask) * rank : ((at ^ mask) + 1) * rank] for at in range(n_ka)]))
    cols = tree_sum(message_part(message, (n_ka + 1) * rank, rank, 2) for message in messages)
    fill_message(out, scaled(tree_sum(cores)), scaled(cols))
    copy.wait()


def after_depths(n_ka, rank, messages):
    lanes = messages[0].shape[1]
    outs = (message_shape(n_ka + 1, rank, lanes), jax.ShapeDtypeStruct((rank, lanes), f32))
    return vmem_call(functools.partial(after_depths_kernel, n_ka, rank), outs, *messages, name="after_depths", to_hbm=1)


def unpack_kernel(sizes, rank, first_message, *refs):
    n_ia, n_ka = sizes["ia"], sizes["ka"]
    messages = refs[:n_ia]
    core_out, *cols, whole, sems = refs[n_ia if first_message == 0 else n_ia + 1 :]
    pairs = rank // 2
    own = masks_of(True, sizes)[2]
    copies = []
    if cols:
        cols_out, cols_here = cols
        cols_here[...] = tree_sum(message_part(message, n_ka * rank, rank, 1) for message in messages)
        copies.append(pltpu.make_async_copy(cols_here, cols_out, sems.at[2 * n_ia]))
        copies[-1].start()
    for at in range(n_ia):
        first = pl.multiple_of(((own // n_ka) ^ (first_message + at)) * n_ka, n_ka)
        for mask in range(n_ka):
            piece = message_part(messages[at], mask * rank, rank, 0)
            line = lax.rem(own, n_ka) ^ mask
            whole[at, 0, line] = piece[:, :rank]
            whole[at, 1, line] = piece[:, rank:]
        for h in range(2):
            lines = pl.ds(h * pairs + first, n_ka)
            copies.append(pltpu.make_async_copy(whole.at[at, h], core_out.at[lines], sems.at[2 * at + h]))
            copies[-1].start()
    for copy in copies:
        copy.wait()


def unpack(sizes, rank, messages, core=None):
    lanes = messages[0].shape[1]
    near = core is None
    out_shape = [jax.ShapeDtypeStruct((rank, rank, rank), f32)]
    out_specs = [pl.BlockSpec(memory_space=pltpu.HBM)]
    scratch = []
    if near:
        out_shape.append(jax.ShapeDtypeStruct((rank, lanes), f32))
        out_specs.append(pl.BlockSpec(memory_space=pltpu.HBM))
        scratch.append(pltpu.VMEM((rank, lanes), f32))
    return pl.pallas_call(
        functools.partial(unpack_kernel, sizes, rank, 0 if near else sizes["ia"]),
        out_shape=tuple(out_shape),
        in_specs=[pl.BlockSpec(memory_space=pltpu.VMEM)] * len(messages)
        + ([] if near else [pl.BlockSpec(memory_space=pltpu.HBM)]),
        out_specs=tuple(out_specs),
        scratch_shapes=[
            *scratch,
            pltpu.VMEM((len(messages), 2, sizes["ka"], rank, rank), f32),
            pltpu.SemaphoreType.DMA((2 * len(messages) + 1,)),
        ],
        input_output_aliases={} if near else {len(messages): 0},
        compiler_params=pltpu.CompilerParams(vmem_limit_bytes=24 * 2**20),
        cost_estimate=pl.CostEstimate(flops=10**6, bytes_accessed=4 * 2**20, transcendentals=0),
        name="unpack_near" if near else "unpack_far",
    )(*messages, *([] if near else [core]))


def power_of_two(n):
    return n & (n - 1) == 0


def swap(value, axis, size, mask):
    return lax.ppermute(value, axis, [(at, at ^ mask) for at in range(size)])


def on_device(sizes, observed, weights, coords, counts, factor_rows, factor_cols, factor_depth, core_tensor):
    n_ia, n_ja, n_ka = sizes["ia"], sizes["ja"], sizes["ka"]
    devices = n_ia * n_ja * n_ka
    rank = core_tensor.shape[0]
    _, _, slots, rows, slab, cols = observed.shape
    data = pltpu.with_memory_space_constraint(observed.reshape(observed.shape[2:]), pltpu.HBM)
    weight = pltpu.with_memory_space_constraint(weights.reshape(weights.shape[2:]), pltpu.HBM)
    core_here = pltpu.with_memory_space_constraint(core_tensor, pltpu.HBM)
    depth_here = pltpu.with_memory_space_constraint(factor_depth, pltpu.HBM)
    row_chunks = factor_rows.shape[1] * n_ja * n_ka // rows
    col_chunks = factor_cols.shape[1] * n_ka // cols
    depth_blocks = factor_depth.shape[1] // n_ka // slab
    ia, ja, ka = lax.axis_index("ia"), lax.axis_index("ja"), lax.axis_index("ka")
    by_swaps = (
        n_ja == 2
        and power_of_two(n_ia)
        and power_of_two(n_ka)
        and rank // 2 == devices
        and factor_rows.shape[1] == rows
        and factor_cols.shape[1] == cols
        and rows == cols == 2 * rank == depth_blocks * slab
    )

    if by_swaps:
        own = jnp.stack([factor_rows, swap(factor_rows, "ja", n_ja, 1), factor_cols])
        pieces = [own] + [swap(own, "ka", n_ka, mask) for mask in range(1, n_ka)]
        row_spots = [(mask, line) for line in range(n_ja) for mask in range(n_ka)]
        col_spots = [(mask, n_ja) for mask in range(n_ka)]
    else:
        row_table = lax.all_gather(factor_rows, ("ja", "ka"), axis=1, tiled=True)
        row_table = row_table.reshape(rank, row_chunks, rows).transpose(1, 0, 2)
        col_table = lax.all_gather(factor_cols, "ka", axis=1, tiled=True)
        col_table = col_table.reshape(rank, col_chunks, cols).transpose(1, 0, 2)
        pieces = [row_table, col_table]
        row_spots = [(0, line) for line in range(row_chunks)]
        own = row_table
        col_spots = [(1, line) for line in range(col_chunks)]

    cube, cube_turned, core_pairs, own_depth, coords, spread = first_cubes(
        own,
        depth_here,
        core_here,
        pltpu.with_memory_space_constraint(coords.transpose(0, 3, 1, 2), pltpu.HBM),
        data,
        weight,
        depth_blocks,
    )
    *sums, cols_sum, _ = terms(
        by_swaps,
        sizes,
        row_spots,
        col_spots,
        counts,
        coords,
        data,
        weight,
        cube,
        cube_turned,
        pieces,
        core_pairs,
        own_depth,
        spread,
    )

    if not by_swaps:
        core_sum, rows_sum, depth_sum = sums
        rows_whole = rows_sum.transpose(1, 0, 2).reshape(rank, row_chunks * rows)
        cols_whole = cols_sum.transpose(1, 0, 2).reshape(rank, col_chunks * cols)
        core_whole = core_sum.reshape(rank // 2, rank, 2, rank).transpose(2, 0, 1, 3).reshape(rank, rank, rank)
        return (
            lax.psum_scatter(rows_whole, ("ja", "ka"), scatter_dimension=1, tiled=True),
            lax.psum_scatter(lax.psum(cols_whole, "ia"), "ka", scatter_dimension=1, tiled=True),
            lax.psum(depth_sum, ("ia", "ja")),
            lax.psum(core_whole, ("ia", "ja", "ka")),
        )

    keep, send = sums
    got = swap(send, "ja", n_ja, 1)
    own_core, own_depth, own_rows, messages = after_cores(n_ia, n_ka, keep, got)
    messages = [swap(message.astype(wire), "ia", n_ia, at + 1).astype(f32) for at, message in enumerate(messages)]
    depth_total, messages = after_rows(n_ia, n_ka, own_core, own_depth, own_rows, cols_sum, messages)
    messages = [messages[0]] + [
        swap(messages[mask].astype(wire), "ka", n_ka, mask).astype(f32) for mask in range(1, n_ka)
    ]
    message, rows_total = after_depths(n_ka, rank, messages)
    sent = message.astype(wire)
    sent = [sent] + [swap(sent, "ia", n_ia, mask) for mask in range(1, n_ia)]
    other = [swap(each, "ja", n_ja, 1) for each in sent]
    core_near, cols_total = unpack(sizes, rank, [each.astype(f32) for each in sent])
    (core_total,) = unpack(sizes, rank, [each.astype(f32) for each in other], core_near)
    return (rows_total, cols_total, depth_total, core_total)


def solution(mesh):
    in_specs = (
        P("ia", "ja", "ka", None, None, None),
        P("ia", "ja", "ka", None, None, None),
        P("ia", "ja", "ka", None),
        P("ia", "ja", "ka"),
        P(None, ("ia", "ja", "ka")),
        P(None, ("ja", "ka")),
        P(),
        P(),
    )
    out_specs = (P(None, ("ia", "ja", "ka")), P(None, ("ja", "ka")), P(None, "ka"), P())
    return jax.shard_map(
        functools.partial(on_device, dict(mesh.shape)),
        mesh=mesh,
        in_specs=in_specs,
        out_specs=out_specs,
        check_vma=False,
    )
```

```python
import functools

import jax
import jax.numpy as jnp
from jax import lax
from jax.experimental import pallas as pl
from jax.experimental.pallas import tpu as pltpu
from jax.sharding import PartitionSpec as P

resid_scale = 1.0 / 64.0
f32 = jnp.float32
bf16 = jnp.bfloat16
wire = jnp.float16


def dot(a, b, contract=((1,), (0,))):
    return lax.dot_general(a, b, (contract, ((), ())), preferred_element_type=f32)


def spread_out(source, target):
    rows, slab, _ = source.shape
    for i in range(rows):
        target[i * (slab + 1) : i * (slab + 1) + slab, :] = source[i].astype(f32)


def cube_kernel(
    slab,
    after,
    factor_depth,
    core,
    coords,
    data,
    weight,
    cube_out,
    cube_turned_out,
    core_out,
    depth_out,
    coords_out,
    spread,
    depth_here,
    core_here,
    fetched,
    cube_wide,
    sems,
):
    pairs, _, rank = core_out.shape
    half = slab // 2
    depth_blocks = cube_out.shape[0]
    width = depth_here.shape[1]
    start = pl.multiple_of(lax.axis_index("ka") * width, width)
    copies = [
        pltpu.make_async_copy(factor_depth.at[:, pl.ds(start, width)], depth_here, sems.at[0]),
        pltpu.make_async_copy(core, core_here, sems.at[1]),
        pltpu.make_async_copy(coords, coords_out, sems.at[2]),
        pltpu.make_async_copy(data.at[0], fetched.at[0], sems.at[3]),
        pltpu.make_async_copy(weight.at[0], fetched.at[1], sems.at[4]),
    ]
    for copy in copies:
        copy.start()
    copies[0].wait()
    depth = depth_here[...].astype(f32).T.astype(bf16)
    depth_out[...] = depth
    order = [depth[t * slab + h * half : t * slab + (h + 1) * half] for h in range(2) for t in range(depth_blocks)]
    ordered = jnp.concatenate(order, axis=0)
    count = depth_blocks * half
    copies[1].wait()
    for pair in range(pairs):
        core_out[pair] = jnp.concatenate([core_here[pair], core_here[pairs + pair]], axis=0)

    def one_pair(pair, carry):
        piece = dot(ordered, core_out[pair], ((1,), (1,)))
        for which in range(2):
            here = piece[:, which * rank : (which + 1) * rank]
            wide = jnp.concatenate([here[:count], here[count:]], axis=1)
            cube_wide[pl.ds(which * pairs + pair, count, stride=rank + 1), :] = wide
        return carry

    lax.fori_loop(0, pairs, one_pair, 0, unroll=8)
    for t in range(depth_blocks):
        for kp in range(half):
            at = (t * half + kp) * (rank + 1)
            block = cube_wide[at : at + rank, :]
            cube_out[t, kp * rank : (kp + 1) * rank, :] = block.astype(bf16)
        cube_turned_out[t] = cube_out[t].astype(f32).T.astype(bf16)
    for copy in copies[2:]:
        copy.wait()
    for at in range(2):
        spread_out(fetched.at[at], spread.at[at])


def first_cubes(after, factor_depth, core, coords, data, weight, depth_blocks):
    rank = core.shape[0]
    _, rows, slab, cols = data.shape
    half = slab // 2
    width = depth_blocks * slab
    return pl.pallas_call(
        functools.partial(cube_kernel, slab),
        out_shape=(
            jax.ShapeDtypeStruct((depth_blocks, half * rank, 2 * rank), bf16),
            jax.ShapeDtypeStruct((depth_blocks, 2 * rank, half * rank), bf16),
            jax.ShapeDtypeStruct((rank // 2, 2 * rank, rank), bf16),
            jax.ShapeDtypeStruct((width, rank), bf16),
            jax.ShapeDtypeStruct(coords.shape, coords.dtype),
            jax.ShapeDtypeStruct((2, rows * (slab + 1), cols), f32),
        ),
        in_specs=[pl.BlockSpec(memory_space=pl.ANY)] + [pl.BlockSpec(memory_space=pltpu.HBM)] * 5,
        out_specs=[pl.BlockSpec(memory_space=pltpu.VMEM)] * 4
        + [pl.BlockSpec(memory_space=pltpu.SMEM), pl.BlockSpec(memory_space=pltpu.VMEM)],
        scratch_shapes=[
            pltpu.VMEM((rank, width), bf16),
            pltpu.VMEM(core.shape, bf16),
            pltpu.VMEM((2, rows, slab, cols), bf16),
            pltpu.VMEM((depth_blocks * half * (rank + 1), 2 * rank), f32),
            pltpu.SemaphoreType.DMA((5,)),
        ],
        compiler_params=pltpu.CompilerParams(vmem_limit_bytes=40 * 2**20),
        cost_estimate=pl.CostEstimate(flops=10**9, bytes_accessed=4 * 2**20, transcendentals=0),
        name="first_cubes",
    )(after, factor_depth, core, coords, data, weight)


def places_of(relative, sizes):
    if not relative:
        return (lambda chunk: chunk), (lambda chunk: chunk), (lambda at: at)
    n_ia, n_ka = sizes["ia"], sizes["ka"]
    ia, ja, ka = lax.axis_index("ia"), lax.axis_index("ja"), lax.axis_index("ka")

    def col_place(chunk):
        return lax.rem(chunk - ka + n_ka, n_ka)

    def row_place(chunk):
        return (lax.div(chunk, n_ka) ^ ja) * n_ka + col_place(lax.rem(chunk, n_ka))

    def core_pair(at):
        far = (ja ^ (at // (n_ia * n_ka))) * n_ia + (ia ^ (at // n_ka % n_ia))
        return far * n_ka + lax.rem(ka + at % n_ka, n_ka)

    return row_place, col_place, core_pair


def terms_kernel(relative, sizes, row_spots, col_spots, counts, coords, data, weight, cube, cube_turned, *refs):
    pieces = refs[: 1 + max(at for at, _ in row_spots + col_spots)]
    (
        core,
        depth_turned,
        _,
        *outs,
        cols_out,
        spread,
        rows_out,
        row_table,
        col_table,
        wide_col,
        backward,
        by_rank,
        second_all,
        depth_all,
        depth_sum,
        fetched,
        sems,
    ) = refs[len(pieces) :]
    slots, rows, slab, cols = data.shape
    pairs = core.shape[0]
    rank = 2 * pairs
    half = slab // 2
    depth_blocks = cube.shape[0]
    count = counts[0, 0, 0]
    row_place, col_place, core_pair = places_of(relative, sizes)
    row_base = lax.axis_index("ia") * row_table.shape[0]
    col_base = lax.axis_index("ja") * col_table.shape[0]
    depth_base = lax.axis_index("ka") * depth_blocks

    def fetches(slot):
        side = lax.rem(slot, 2)
        return [
            pltpu.make_async_copy(source.at[slot], fetched.at[side, which], sems.at[side, which])
            for which, source in enumerate((data, weight))
        ]

    def fetch(slot):
        @pl.when(slot < count)
        def _():
            for copy in fetches(slot):
                copy.start()

    def arrive(slot):
        for copy in fetches(slot):
            copy.wait()

    for s in range(slots):

        @pl.when(s >= count)
        def _():
            lines = slice(s * slab, (s + 1) * slab)
            second_all[:, lines, :] = jnp.zeros((pairs, slab, 2 * rank), bf16)
            depth_all[lines, :] = jnp.zeros((slab, rank), bf16)

    depth_sum[...] = jnp.zeros_like(depth_sum)
    rows_out[...] = jnp.zeros_like(rows_out)
    cols_out[...] = jnp.zeros_like(cols_out)
    wide_col[...] = jnp.zeros_like(wide_col)
    for spots, table in ((row_spots, row_table), (col_spots, col_table)):
        for at, (piece, line) in enumerate(spots):
            table[at] = pieces[piece][line]

    def one_slot(slot, carry):
        fetch(slot + 1)

        @pl.when(slot > 0)
        def _():
            arrive(slot)
            for which in range(2):
                spread_out(fetched.at[lax.rem(slot, 2), which], spread.at[which])

        row_at = row_place(coords[0, 0, 0, slot] - row_base)
        col_at = col_place(coords[0, 1, 0, slot] - col_base)
        depth_at = coords[0, 2, 0, slot] - depth_base
        row_factor = row_table[row_at]
        row_turned = row_factor.astype(f32).T.astype(bf16)
        col_factor = col_table[col_at]
        wide_col[:rank, :cols] = col_factor
        wide_col[rank:, cols:] = col_factor
        own_depth = depth_turned[pl.ds(pl.multiple_of(depth_at * slab, slab), slab), :]
        depth_all[pl.ds(pl.multiple_of(slot * slab, slab), slab), :] = own_depth

        step = 8
        groups = half // step
        wide_factor = wide_col[...]
        def second_of(g):
            lines = cube[depth_at, g * step * rank : (g + 1) * step * rank, :]
            block = dot(lines, wide_factor).astype(bf16)
            return jnp.concatenate([block[kp * rank : (kp + 1) * rank] for kp in range(step)], axis=1)

        def residual_of(g, model):
            parts = []
            for kp in range(step):
                for h in range(2):
                    lines = pl.ds(h * half + g * step + kp, rows, stride=slab + 1)
                    seen, scale = spread[0, lines, :], spread[1, lines, :]
                    at = (kp * 2 + h) * cols
                    gap = model[:, at : at + cols] - seen
                    parts.append((scale * gap * resid_scale).astype(bf16))
            return jnp.concatenate(parts, axis=1)

        def keep_back(g, back):
            back = back.astype(bf16)
            for kp in range(step):
                pair = back[:, kp * 2 * cols : (kp + 1) * 2 * cols]
                at = (g * step + kp) * rank
                backward[at : at + rank, :] = pair
                wider = pair.astype(f32)
                for h in range(2):
                    lines = pl.ds(h * half + g * step + kp, rank, stride=slab + 1)
                    by_rank[lines, :] = wider[:, h * cols : (h + 1) * cols]

        row_sum = jnp.zeros((rows, rank), f32)
        seconds = [second_of(g) for g in range(groups)]
        models = [None] * groups
        models[0] = dot(row_turned, seconds[0])
        for g in range(groups):
            if g + 1 < groups:
                models[g + 1] = dot(row_turned, seconds[g + 1])
            residual = residual_of(g, models[g])
            keep_back(g, dot(row_factor, residual))
            row_sum = row_sum + dot(residual, seconds[g], ((1,), (1,)))
        rows_out[row_at] += row_sum.T
        wide = dot(cube_turned[depth_at], backward[...])
        cols_out[col_at] += wide[:rank, :cols] + wide[rank:, cols:]
        lines = pl.ds(pl.multiple_of(slot * slab, slab), slab)
        for first in range(0, pairs, 8):
            ranked = []
            for pair in range(first, first + 8):
                spots = [at * (slab + 1) for at in (pair, pairs + pair)]
                ranked.append(jnp.concatenate([by_rank[at : at + slab, :].astype(bf16) for at in spots], axis=1))
            ranked = jnp.concatenate(ranked, axis=0)
            second_back = dot(ranked, wide_col[...], ((1,), (1,))).astype(bf16)
            second_all[first : first + 8, lines, :] = second_back.reshape(8, slab, 2 * rank)

        return carry

    lax.fori_loop(0, count, one_slot, 0)

    if relative:
        sides = [(outs[0], 0), (outs[1], 0)]
        core_spots = [sides[at // (pairs // 2)] + (at % (pairs // 2),) for at in range(pairs)]
        row_count = len(row_spots) // 2
        row_places = [sides[at // row_count] + (pairs // 2 + at % row_count,) for at in range(2 * row_count)]
    else:
        core_spots = [(outs[0], 0, at) for at in range(pairs)]
        row_places = [(outs[1], 0, at) for at in range(len(row_spots))]
    total = jnp.zeros((second_all.shape[1], rank), f32)
    for at in range(pairs):
        pair = core_pair(at)
        second = second_all[pair]
        total = total + dot(second, core[pair])
        piece = dot(second, depth_all[...], ((0,), (0,)))
        out, _, line = core_spots[at]
        out[line] = jnp.concatenate([piece[:rank], piece[rank:]], axis=1)
    for at, (out, _, line) in enumerate(row_places):
        out[line] = rows_out[at]
    for s in range(slots):

        @pl.when(s < count)
        def _():
            at = coords[0, 2, 0, s] - depth_base
            lines = pl.ds(pl.multiple_of(at * slab, slab), slab)
            depth_sum[lines, :] += total[s * slab : (s + 1) * slab]

    depth = depth_sum[...].T
    if relative:
        for out in outs:
            out[pairs // 2 + row_count] = depth
    else:
        outs[2][...] = depth


def terms(relative, sizes, row_spots, col_spots, counts, coords, data, weight, cube, cube_turned, pieces, core, depth, spread):
    slots, rows, slab, cols = data.shape
    rank = core.shape[2]
    half = slab // 2
    depth_blocks = cube.shape[0]

    width = depth_blocks * slab
    if relative:
        chunks = (rank // 2 + len(row_spots)) // 2 + 1
        outs = (jax.ShapeDtypeStruct((chunks, rank, rows), f32),) * 2
    else:
        outs = (
            jax.ShapeDtypeStruct((rank // 2, rank, 2 * rank), f32),
            jax.ShapeDtypeStruct((len(row_spots), rank, rows), f32),
            jax.ShapeDtypeStruct((rank, width), f32),
        )
    outs += (
        jax.ShapeDtypeStruct((len(col_spots), rank, cols), f32),
        jax.ShapeDtypeStruct(spread.shape, f32),
    )
    return pl.pallas_call(
        functools.partial(terms_kernel, relative, sizes, row_spots, col_spots),
        out_shape=outs,
        grid_spec=pltpu.PrefetchScalarGridSpec(
            num_scalar_prefetch=0,
            grid=(),
            in_specs=[pl.BlockSpec(memory_space=pltpu.SMEM)] * 2
            + [pl.BlockSpec(memory_space=pltpu.HBM)] * 2
            + [pl.BlockSpec(memory_space=pltpu.VMEM)] * (5 + len(pieces)),
            out_specs=[pl.BlockSpec(memory_space=pltpu.VMEM)] * len(outs),
            scratch_shapes=[
                pltpu.VMEM((len(row_spots), rank, rows), f32),
                pltpu.VMEM((len(row_spots), rank, rows), bf16),
                pltpu.VMEM((len(col_spots), rank, cols), bf16),
                pltpu.VMEM((2 * rank, 2 * cols), bf16),
                pltpu.VMEM((half * rank, 2 * cols), bf16),
                pltpu.VMEM((rank * (slab + 1), cols), f32),
                pltpu.VMEM((rank // 2, slots * slab, 2 * rank), bf16),
                pltpu.VMEM((slots * slab, rank), bf16),
                pltpu.VMEM((depth_blocks * slab, rank), f32),
                pltpu.VMEM((2, 2, rows, slab, cols), bf16),
                pltpu.SemaphoreType.DMA((2, 2)),
            ],
        ),
        input_output_aliases={8 + len(pieces): len(outs) - 1},
        compiler_params=pltpu.CompilerParams(vmem_limit_bytes=40 * 2**20),
        cost_estimate=pl.CostEstimate(flops=10**9, bytes_accessed=16 * 2**20, transcendentals=0),
        name="terms",
    )(counts, coords, data, weight, cube, cube_turned, *pieces, core, depth, spread)


mark_rows = 16
top_exponent = 14.0


def vmem_call(kernel, out_shape, *operands, name, to_hbm=None):
    spaces = [pltpu.HBM if at == to_hbm else pltpu.VMEM for at in range(len(out_shape))]
    scratch = []
    if to_hbm is not None:
        scratch = [pltpu.VMEM(out_shape[to_hbm].shape, out_shape[to_hbm].dtype), pltpu.SemaphoreType.DMA]
    return pl.pallas_call(
        kernel,
        out_shape=out_shape,
        in_specs=[pl.BlockSpec(memory_space=pltpu.VMEM)] * len(operands),
        out_specs=tuple(pl.BlockSpec(memory_space=space) for space in spaces),
        scratch_shapes=scratch,
        compiler_params=pltpu.CompilerParams(vmem_limit_bytes=24 * 2**20),
        name=name,
    )(*operands)


def power_of(exponent):
    whole = jnp.abs(exponent).astype(jnp.int32)
    value = jnp.ones_like(exponent)
    for bit in range(7):
        factor = jnp.where(exponent < 0, f32(2.0 ** -(2**bit)), f32(2.0 ** (2**bit)))
        value = value * jnp.where((whole >> bit) & 1 == 1, factor, f32(1.0))
    return value


def exponent_of(value):
    lanes = value.shape[-1]
    largest = jnp.max(jnp.max(jnp.abs(value.reshape(-1, 8, lanes)), axis=0), axis=0, keepdims=True)
    largest = jnp.max(largest, axis=1, keepdims=True)
    largest = jnp.broadcast_to(jnp.maximum(largest, f32(1e-30)), (8, lanes))
    return jnp.ceil(jnp.log(largest) * f32(1.4426950408889634)) - f32(top_exponent)


def rounded(value):
    stretched = value * f32(8193.0)
    return stretched - (stretched - value)


def scaled(value):
    exponent = exponent_of(value)
    return rounded(value * power_of(-exponent)[:1]), exponent


def fill_message(out, *parts):
    at = 0
    mark = None
    for which, (flat, exponent) in enumerate(parts):
        out[at : at + flat.shape[0], :] = flat
        at += flat.shape[0]
        exponent = jnp.broadcast_to(exponent[:1], (mark_rows, flat.shape[1]))
        line = lax.broadcasted_iota(jnp.int32, exponent.shape, 0)
        mark = exponent if mark is None else jnp.where(line >= which, exponent, mark)
    out[at : at + mark_rows, :] = mark


def message_part(message, start, rows, part):
    mark = message.shape[0] - mark_rows + part
    return message[start : start + rows, :] * power_of(message[mark : mark + 1, :])


def message_shape(chunks, rank, lanes):
    return jax.ShapeDtypeStruct((chunks * rank + mark_rows, lanes), f32)


def tree_order(count):
    if count == 1:
        return [0]
    return [2 * at for at in tree_order(count // 2)] + [2 * at + 1 for at in tree_order(count // 2)]


def tree_sum(values):
    values = list(values)
    while len(values) > 1:
        values = [values[at] + values[at + 1] for at in range(0, len(values), 2)]
    return values[0]


def after_cores_kernel(n_ia, n_ka, keep, got, own_core, own_depth, own_rows, *messages):
    half = n_ia * n_ka
    depth = keep[half + n_ka] + got[half + n_ka]
    flat, exponent = scaled(depth)
    own_depth[...] = flat * power_of(exponent)[:1]
    own_core[...] = keep[:n_ka] + got[:n_ka]
    own_rows[...] = keep[half : half + n_ka] + got[half : half + n_ka]
    for mask in range(1, n_ia):
        lines = slice(mask * n_ka, (mask + 1) * n_ka)
        core = (keep[lines] + got[lines]).reshape(-1, depth.shape[1])
        fill_message(messages[mask - 1], scaled(core), (flat, exponent))


def after_cores(n_ia, n_ka, keep, got):
    _, rank, lanes = keep.shape
    outs = [jax.ShapeDtypeStruct(shape, f32) for shape in ((n_ka, rank, lanes), (rank, lanes), (n_ka, rank, lanes))]
    outs += [message_shape(n_ka + 1, rank, lanes)] * (n_ia - 1)
    outs = vmem_call(functools.partial(after_cores_kernel, n_ia, n_ka), tuple(outs), keep, got, name="after_cores")
    return outs[0], outs[1], outs[2], outs[3:]


def after_rows_kernel(n_ia, n_ka, own_core, own_depth, own_rows, cols_sum, *refs):
    messages, refs = refs[: n_ia - 1], refs[n_ia - 1 :]
    depth_out, *outs, depth_here, sem = refs
    count, rank, lanes = own_core.shape
    depths = [own_depth[...]] + [message_part(message, count * rank, rank, 1) for message in messages]
    depth_here[...] = tree_sum(depths)
    copy = pltpu.make_async_copy(depth_here, depth_out, sem)
    copy.start()
    core = own_core[...].reshape(count * rank, lanes)
    for message in messages:
        core = core + message_part(message, 0, count * rank, 0)
    flat, exponent = scaled(core)
    for mask in range(n_ka):
        fill_message(outs[mask], (flat, exponent), scaled(own_rows[mask]), scaled(cols_sum[mask]))
    copy.wait()


def after_rows(n_ia, n_ka, own_core, own_depth, own_rows, cols_sum, messages):
    count, rank, lanes = own_core.shape
    outs = (jax.ShapeDtypeStruct((rank, lanes), f32),) + (message_shape(count + 2, rank, lanes),) * n_ka
    outs = vmem_call(
        functools.partial(after_rows_kernel, n_ia, n_ka),
        outs,
        own_core,
        own_depth,
        own_rows,
        cols_sum,
        *messages,
        name="after_rows",
        to_hbm=0,
    )
    return outs[0], outs[1:]


def after_depths_kernel(n_ka, rank, *refs):
    messages, (out, rows_out, rows_here, sem) = refs[:n_ka], refs[n_ka:]
    rows_here[...] = tree_sum(message_part(message, n_ka * rank, rank, 1) for message in messages)
    copy = pltpu.make_async_copy(rows_here, rows_out, sem)
    copy.start()
    cores = []
    for by in tree_order(n_ka):
        part = message_part(messages[by], 0, n_ka * rank, 0)
        order = [(at + by) % n_ka for at in range(n_ka)]
        cores.append(jnp.concatenate([part[at * rank : (at + 1) * rank] for at in order]))
    cols = tree_sum(message_part(message, (n_ka + 1) * rank, rank, 2) for message in messages)
    fill_message(out, scaled(tree_sum(cores)), scaled(cols))
    copy.wait()


def after_depths(n_ka, rank, messages):
    lanes = messages[0].shape[1]
    outs = (message_shape(n_ka + 1, rank, lanes), jax.ShapeDtypeStruct((rank, lanes), f32))
    return vmem_call(functools.partial(after_depths_kernel, n_ka, rank), outs, *messages, name="after_depths", to_hbm=1)


def unpack_kernel(sizes, rank, first_message, *refs):
    n_ia, n_ka = sizes["ia"], sizes["ka"]
    messages = refs[:n_ia]
    core_out, *cols, whole, sems = refs[n_ia if first_message == 0 else n_ia + 1 :]
    pairs = rank // 2
    ka = lax.axis_index("ka")
    own = lax.axis_index("ja") * n_ia + lax.axis_index("ia")
    copies = []
    if cols:
        cols_out, cols_here = cols
        cols_here[...] = tree_sum(message_part(message, n_ka * rank, rank, 1) for message in messages)
        copies.append(pltpu.make_async_copy(cols_here, cols_out, sems.at[2 * n_ia]))
        copies[-1].start()
    for at in range(n_ia):
        first = pl.multiple_of((own ^ (first_message + at)) * n_ka, n_ka)
        for mask in range(n_ka):
            piece = message_part(messages[at], mask * rank, rank, 0)
            line = lax.rem(ka + mask, n_ka)
            whole[at, 0, line] = piece[:, :rank]
            whole[at, 1, line] = piece[:, rank:]
        for h in range(2):
            lines = pl.ds(h * pairs + first, n_ka)
            copies.append(pltpu.make_async_copy(whole.at[at, h], core_out.at[lines], sems.at[2 * at + h]))
            copies[-1].start()
    for copy in copies:
        copy.wait()


def unpack(sizes, rank, messages, core=None):
    lanes = messages[0].shape[1]
    near = core is None
    out_shape = [jax.ShapeDtypeStruct((rank, rank, rank), f32)]
    out_specs = [pl.BlockSpec(memory_space=pltpu.HBM)]
    scratch = []
    if near:
        out_shape.append(jax.ShapeDtypeStruct((rank, lanes), f32))
        out_specs.append(pl.BlockSpec(memory_space=pltpu.HBM))
        scratch.append(pltpu.VMEM((rank, lanes), f32))
    return pl.pallas_call(
        functools.partial(unpack_kernel, sizes, rank, 0 if near else sizes["ia"]),
        out_shape=tuple(out_shape),
        in_specs=[pl.BlockSpec(memory_space=pltpu.VMEM)] * len(messages)
        + ([] if near else [pl.BlockSpec(memory_space=pltpu.HBM)]),
        out_specs=tuple(out_specs),
        scratch_shapes=[
            *scratch,
            pltpu.VMEM((len(messages), 2, sizes["ka"], rank, rank), f32),
            pltpu.SemaphoreType.DMA((2 * len(messages) + 1,)),
        ],
        input_output_aliases={} if near else {len(messages): 0},
        compiler_params=pltpu.CompilerParams(vmem_limit_bytes=24 * 2**20),
        cost_estimate=pl.CostEstimate(flops=10**6, bytes_accessed=4 * 2**20, transcendentals=0),
        name="unpack_near" if near else "unpack_far",
    )(*messages, *([] if near else [core]))


def power_of_two(n):
    return n & (n - 1) == 0


def swap(value, axis, size, mask):
    return lax.ppermute(value, axis, [(at, at ^ mask) for at in range(size)])


def shift(value, axis, size, by):
    return lax.ppermute(value, axis, [(at, (at + by) % size) for at in range(size)])


def on_device(sizes, observed, weights, coords, counts, factor_rows, factor_cols, factor_depth, core_tensor):
    n_ia, n_ja, n_ka = sizes["ia"], sizes["ja"], sizes["ka"]
    devices = n_ia * n_ja * n_ka
    rank = core_tensor.shape[0]
    _, _, slots, rows, slab, cols = observed.shape
    data = pltpu.with_memory_space_constraint(observed.reshape(observed.shape[2:]), pltpu.HBM)
    weight = pltpu.with_memory_space_constraint(weights.reshape(weights.shape[2:]), pltpu.HBM)
    core_here = pltpu.with_memory_space_constraint(core_tensor, pltpu.HBM)
    depth_here = pltpu.with_memory_space_constraint(factor_depth, pltpu.HBM)
    row_chunks = factor_rows.shape[1] * n_ja * n_ka // rows
    col_chunks = factor_cols.shape[1] * n_ka // cols
    depth_blocks = factor_depth.shape[1] // n_ka // slab
    ia, ja, ka = lax.axis_index("ia"), lax.axis_index("ja"), lax.axis_index("ka")
    by_swaps = (
        n_ja == 2
        and power_of_two(n_ia)
        and power_of_two(n_ka)
        and rank // 2 == devices
        and factor_rows.shape[1] == rows
        and factor_cols.shape[1] == cols
        and rows == cols == 2 * rank == depth_blocks * slab
    )

    if by_swaps:
        own = jnp.stack([factor_rows, swap(factor_rows, "ja", n_ja, 1), factor_cols])
        pieces = [own] + [shift(own, "ka", n_ka, n_ka - at) for at in range(1, n_ka)]
        row_spots = [(mask, line) for line in range(n_ja) for mask in range(n_ka)]
        col_spots = [(mask, n_ja) for mask in range(n_ka)]
    else:
        row_table = lax.all_gather(factor_rows, ("ja", "ka"), axis=1, tiled=True)
        row_table = row_table.reshape(rank, row_chunks, rows).transpose(1, 0, 2)
        col_table = lax.all_gather(factor_cols, "ka", axis=1, tiled=True)
        col_table = col_table.reshape(rank, col_chunks, cols).transpose(1, 0, 2)
        pieces = [row_table, col_table]
        row_spots = [(0, line) for line in range(row_chunks)]
        own = row_table
        col_spots = [(1, line) for line in range(col_chunks)]

    cube, cube_turned, core_pairs, own_depth, coords, spread = first_cubes(
        own,
        depth_here,
        core_here,
        pltpu.with_memory_space_constraint(coords.transpose(0, 3, 1, 2), pltpu.HBM),
        data,
        weight,
        depth_blocks,
    )
    *sums, cols_sum, _ = terms(
        by_swaps,
        sizes,
        row_spots,
        col_spots,
        counts,
        coords,
        data,
        weight,
        cube,
        cube_turned,
        pieces,
        core_pairs,
        own_depth,
        spread,
    )

    if not by_swaps:
        core_sum, rows_sum, depth_sum = sums
        rows_whole = rows_sum.transpose(1, 0, 2).reshape(rank, row_chunks * rows)
        cols_whole = cols_sum.transpose(1, 0, 2).reshape(rank, col_chunks * cols)
        core_whole = core_sum.reshape(rank // 2, rank, 2, rank).transpose(2, 0, 1, 3).reshape(rank, rank, rank)
        return (
            lax.psum_scatter(rows_whole, ("ja", "ka"), scatter_dimension=1, tiled=True),
            lax.psum_scatter(lax.psum(cols_whole, "ia"), "ka", scatter_dimension=1, tiled=True),
            lax.psum(depth_sum, ("ia", "ja")),
            lax.psum(core_whole, ("ia", "ja", "ka")),
        )

    keep, send = sums
    got = swap(send, "ja", n_ja, 1)
    own_core, own_depth, own_rows, messages = after_cores(n_ia, n_ka, keep, got)
    messages = [swap(message.astype(wire), "ia", n_ia, at + 1).astype(f32) for at, message in enumerate(messages)]
    depth_total, messages = after_rows(n_ia, n_ka, own_core, own_depth, own_rows, cols_sum, messages)
    got = {by: shift(messages[by].astype(wire), "ka", n_ka, by).astype(f32) for by in reversed(range(1, n_ka))}
    messages = [messages[0]] + [got[by] for by in range(1, n_ka)]
    message, rows_total = after_depths(n_ka, rank, messages)
    sent = message.astype(wire)
    sent = [sent] + [swap(sent, "ia", n_ia, mask) for mask in range(1, n_ia)]
    other = [swap(each, "ja", n_ja, 1) for each in sent]
    core_near, cols_total = unpack(sizes, rank, [each.astype(f32) for each in sent])
    (core_total,) = unpack(sizes, rank, [each.astype(f32) for each in other], core_near)
    return (rows_total, cols_total, depth_total, core_total)


def solution(mesh):
    in_specs = (
        P("ia", "ja", "ka", None, None, None),
        P("ia", "ja", "ka", None, None, None),
        P("ia", "ja", "ka", None),
        P("ia", "ja", "ka"),
        P(None, ("ia", "ja", "ka")),
        P(None, ("ja", "ka")),
        P(),
        P(),
    )
    out_specs = (P(None, ("ia", "ja", "ka")), P(None, ("ja", "ka")), P(None, "ka"), P())
    return jax.shard_map(
        functools.partial(on_device, dict(mesh.shape)),
        mesh=mesh,
        in_specs=in_specs,
        out_specs=out_specs,
        check_vma=False,
    )
```

```python
import functools

import jax
import jax.numpy as jnp
from jax import lax
from jax.experimental import pallas as pl
from jax.experimental.pallas import tpu as pltpu
from jax.sharding import PartitionSpec as P

resid_scale = 1.0 / 64.0
f32 = jnp.float32
bf16 = jnp.bfloat16
wire = jnp.float16


def dot(a, b, contract=((1,), (0,))):
    return lax.dot_general(a, b, (contract, ((), ())), preferred_element_type=f32)


def spread_out(source, target):
    rows, slab, _ = source.shape
    for i in range(rows):
        target[i * (slab + 1) : i * (slab + 1) + slab, :] = source[i].astype(f32)


def cube_kernel(
    slab,
    after,
    factor_depth,
    core,
    coords,
    data,
    weight,
    cube_out,
    cube_turned_out,
    core_out,
    depth_out,
    coords_out,
    spread,
    depth_here,
    core_here,
    fetched,
    cube_wide,
    sems,
):
    pairs, _, rank = core_out.shape
    half = slab // 2
    depth_blocks = cube_out.shape[0]
    width = depth_here.shape[1]
    start = pl.multiple_of(lax.axis_index("ka") * width, width)
    copies = [
        pltpu.make_async_copy(factor_depth.at[:, pl.ds(start, width)], depth_here, sems.at[0]),
        pltpu.make_async_copy(core, core_here, sems.at[1]),
        pltpu.make_async_copy(coords, coords_out, sems.at[2]),
        pltpu.make_async_copy(data.at[0], fetched.at[0], sems.at[3]),
        pltpu.make_async_copy(weight.at[0], fetched.at[1], sems.at[4]),
    ]
    for copy in copies:
        copy.start()
    copies[0].wait()
    depth = depth_here[...].astype(f32).T.astype(bf16)
    depth_out[...] = depth
    order = [depth[t * slab + h * half : t * slab + (h + 1) * half] for h in range(2) for t in range(depth_blocks)]
    ordered = jnp.concatenate(order, axis=0)
    count = depth_blocks * half
    copies[1].wait()
    for pair in range(pairs):
        core_out[pair] = jnp.concatenate([core_here[pair], core_here[pairs + pair]], axis=0)

    def one_pair(pair, carry):
        piece = dot(ordered, core_out[pair], ((1,), (1,)))
        for which in range(2):
            here = piece[:, which * rank : (which + 1) * rank]
            wide = jnp.concatenate([here[:count], here[count:]], axis=1)
            cube_wide[pl.ds(which * pairs + pair, count, stride=rank + 1), :] = wide
        return carry

    lax.fori_loop(0, pairs, one_pair, 0, unroll=8)
    for t in range(depth_blocks):
        for kp in range(half):
            at = (t * half + kp) * (rank + 1)
            block = cube_wide[at : at + rank, :]
            cube_out[t, kp * rank : (kp + 1) * rank, :] = block.astype(bf16)
        cube_turned_out[t] = cube_out[t].astype(f32).T.astype(bf16)
    for copy in copies[2:]:
        copy.wait()
    for at in range(2):
        spread_out(fetched.at[at], spread.at[at])


def first_cubes(after, factor_depth, core, coords, data, weight, depth_blocks):
    rank = core.shape[0]
    _, rows, slab, cols = data.shape
    half = slab // 2
    width = depth_blocks * slab
    return pl.pallas_call(
        functools.partial(cube_kernel, slab),
        out_shape=(
            jax.ShapeDtypeStruct((depth_blocks, half * rank, 2 * rank), bf16),
            jax.ShapeDtypeStruct((depth_blocks, 2 * rank, half * rank), bf16),
            jax.ShapeDtypeStruct((rank // 2, 2 * rank, rank), bf16),
            jax.ShapeDtypeStruct((width, rank), bf16),
            jax.ShapeDtypeStruct(coords.shape, coords.dtype),
            jax.ShapeDtypeStruct((2, rows * (slab + 1), cols), f32),
        ),
        in_specs=[pl.BlockSpec(memory_space=pl.ANY)] + [pl.BlockSpec(memory_space=pltpu.HBM)] * 5,
        out_specs=[pl.BlockSpec(memory_space=pltpu.VMEM)] * 4
        + [pl.BlockSpec(memory_space=pltpu.SMEM), pl.BlockSpec(memory_space=pltpu.VMEM)],
        scratch_shapes=[
            pltpu.VMEM((rank, width), bf16),
            pltpu.VMEM(core.shape, bf16),
            pltpu.VMEM((2, rows, slab, cols), bf16),
            pltpu.VMEM((depth_blocks * half * (rank + 1), 2 * rank), f32),
            pltpu.SemaphoreType.DMA((5,)),
        ],
        compiler_params=pltpu.CompilerParams(vmem_limit_bytes=40 * 2**20),
        cost_estimate=pl.CostEstimate(flops=10**9, bytes_accessed=4 * 2**20, transcendentals=0),
        name="first_cubes",
    )(after, factor_depth, core, coords, data, weight)


def masks_of(relative, sizes):
    ia, ja, ka = lax.axis_index("ia"), lax.axis_index("ja"), lax.axis_index("ka")
    if not relative:
        return 0, 0, 0
    return ja * sizes["ka"] + ka, ka, (ja * sizes["ia"] + ia) * sizes["ka"] + ka


def terms_kernel(relative, sizes, row_spots, col_spots, counts, coords, data, weight, cube, cube_turned, *refs):
    pieces = refs[: 1 + max(at for at, _ in row_spots + col_spots)]
    (
        core,
        depth_turned,
        _,
        *outs,
        cols_out,
        spread,
        rows_out,
        row_table,
        col_table,
        wide_col,
        backward,
        by_rank,
        second_all,
        depth_all,
        depth_sum,
        fetched,
        sems,
    ) = refs[len(pieces) :]
    slots, rows, slab, cols = data.shape
    pairs = core.shape[0]
    rank = 2 * pairs
    half = slab // 2
    depth_blocks = cube.shape[0]
    count = counts[0, 0, 0]
    row_mask, col_mask, core_mask = masks_of(relative, sizes)
    row_base = lax.axis_index("ia") * row_table.shape[0]
    col_base = lax.axis_index("ja") * col_table.shape[0]
    depth_base = lax.axis_index("ka") * depth_blocks

    def fetches(slot):
        side = lax.rem(slot, 2)
        return [
            pltpu.make_async_copy(source.at[slot], fetched.at[side, which], sems.at[side, which])
            for which, source in enumerate((data, weight))
        ]

    def fetch(slot):
        @pl.when(slot < count)
        def _():
            for copy in fetches(slot):
                copy.start()

    def arrive(slot):
        for copy in fetches(slot):
            copy.wait()

    for s in range(slots):

        @pl.when(s >= count)
        def _():
            lines = slice(s * slab, (s + 1) * slab)
            second_all[:, lines, :] = jnp.zeros((pairs, slab, 2 * rank), bf16)
            depth_all[lines, :] = jnp.zeros((slab, rank), bf16)

    depth_sum[...] = jnp.zeros_like(depth_sum)
    rows_out[...] = jnp.zeros_like(rows_out)
    cols_out[...] = jnp.zeros_like(cols_out)
    wide_col[...] = jnp.zeros_like(wide_col)
    for spots, table in ((row_spots, row_table), (col_spots, col_table)):
        for at, (piece, line) in enumerate(spots):
            table[at] = pieces[piece][line]

    def one_slot(slot, carry):
        fetch(slot + 1)

        @pl.when(slot > 0)
        def _():
            arrive(slot)
            for which in range(2):
                spread_out(fetched.at[lax.rem(slot, 2), which], spread.at[which])

        row_at = (coords[0, 0, 0, slot] - row_base) ^ row_mask
        col_at = (coords[0, 1, 0, slot] - col_base) ^ col_mask
        depth_at = coords[0, 2, 0, slot] - depth_base
        row_factor = row_table[row_at]
        row_turned = row_factor.astype(f32).T.astype(bf16)
        col_factor = col_table[col_at]
        wide_col[:rank, :cols] = col_factor
        wide_col[rank:, cols:] = col_factor
        own_depth = depth_turned[pl.ds(pl.multiple_of(depth_at * slab, slab), slab), :]
        depth_all[pl.ds(pl.multiple_of(slot * slab, slab), slab), :] = own_depth

        step = 8
        groups = half // step
        wide_factor = wide_col[...]
        def second_of(g):
            lines = cube[depth_at, g * step * rank : (g + 1) * step * rank, :]
            block = dot(lines, wide_factor).astype(bf16)
            return jnp.concatenate([block[kp * rank : (kp + 1) * rank] for kp in range(step)], axis=1)

        def residual_of(g, model):
            parts = []
            for kp in range(step):
                for h in range(2):
                    lines = pl.ds(h * half + g * step + kp, rows, stride=slab + 1)
                    seen, scale = spread[0, lines, :], spread[1, lines, :]
                    at = (kp * 2 + h) * cols
                    gap = model[:, at : at + cols] - seen
                    parts.append((scale * gap * resid_scale).astype(bf16))
            return jnp.concatenate(parts, axis=1)

        def keep_back(g, back):
            back = back.astype(bf16)
            for kp in range(step):
                pair = back[:, kp * 2 * cols : (kp + 1) * 2 * cols]
                at = (g * step + kp) * rank
                backward[at : at + rank, :] = pair
                wider = pair.astype(f32)
                for h in range(2):
                    lines = pl.ds(h * half + g * step + kp, rank, stride=slab + 1)
                    by_rank[lines, :] = wider[:, h * cols : (h + 1) * cols]

        row_sum = jnp.zeros((rows, rank), f32)
        seconds = [second_of(g) for g in range(groups)]
        models = [None] * groups
        models[0] = dot(row_turned, seconds[0])
        for g in range(groups):
            if g + 1 < groups:
                models[g + 1] = dot(row_turned, seconds[g + 1])
            residual = residual_of(g, models[g])
            keep_back(g, dot(row_factor, residual))
            row_sum = row_sum + dot(residual, seconds[g], ((1,), (1,)))
        rows_out[row_at] += row_sum.T
        wide = dot(cube_turned[depth_at], backward[...])
        cols_out[col_at] += wide[:rank, :cols] + wide[rank:, cols:]
        lines = pl.ds(pl.multiple_of(slot * slab, slab), slab)
        for first in range(0, pairs, 8):
            ranked = []
            for pair in range(first, first + 8):
                spots = [at * (slab + 1) for at in (pair, pairs + pair)]
                ranked.append(jnp.concatenate([by_rank[at : at + slab, :].astype(bf16) for at in spots], axis=1))
            ranked = jnp.concatenate(ranked, axis=0)
            second_back = dot(ranked, wide_col[...], ((1,), (1,))).astype(bf16)
            second_all[first : first + 8, lines, :] = second_back.reshape(8, slab, 2 * rank)

        return carry

    lax.fori_loop(0, count, one_slot, 0)

    if relative:
        sides = [(outs[0], 0), (outs[1], 0)]
        core_spots = [sides[at // (pairs // 2)] + (at % (pairs // 2),) for at in range(pairs)]
        row_count = len(row_spots) // 2
        row_places = [sides[at // row_count] + (pairs // 2 + at % row_count,) for at in range(2 * row_count)]
    else:
        core_spots = [(outs[0], 0, at) for at in range(pairs)]
        row_places = [(outs[1], 0, at) for at in range(len(row_spots))]
    total = jnp.zeros((second_all.shape[1], rank), f32)
    for at in range(pairs):
        pair = at ^ core_mask
        second = second_all[pair]
        total = total + dot(second, core[pair])
        piece = dot(second, depth_all[...], ((0,), (0,)))
        out, _, line = core_spots[at]
        out[line] = jnp.concatenate([piece[:rank], piece[rank:]], axis=1)
    for at, (out, _, line) in enumerate(row_places):
        out[line] = rows_out[at]
    for s in range(slots):

        @pl.when(s < count)
        def _():
            at = coords[0, 2, 0, s] - depth_base
            lines = pl.ds(pl.multiple_of(at * slab, slab), slab)
            depth_sum[lines, :] += total[s * slab : (s + 1) * slab]

    depth = depth_sum[...].T
    if relative:
        for out in outs:
            out[pairs // 2 + row_count] = depth
    else:
        outs[2][...] = depth


def terms(relative, sizes, row_spots, col_spots, counts, coords, data, weight, cube, cube_turned, pieces, core, depth, spread):
    slots, rows, slab, cols = data.shape
    rank = core.shape[2]
    half = slab // 2
    depth_blocks = cube.shape[0]

    width = depth_blocks * slab
    if relative:
        chunks = (rank // 2 + len(row_spots)) // 2 + 1
        outs = (jax.ShapeDtypeStruct((chunks, rank, rows), f32),) * 2
    else:
        outs = (
            jax.ShapeDtypeStruct((rank // 2, rank, 2 * rank), f32),
            jax.ShapeDtypeStruct((len(row_spots), rank, rows), f32),
            jax.ShapeDtypeStruct((rank, width), f32),
        )
    outs += (
        jax.ShapeDtypeStruct((len(col_spots), rank, cols), f32),
        jax.ShapeDtypeStruct(spread.shape, f32),
    )
    return pl.pallas_call(
        functools.partial(terms_kernel, relative, sizes, row_spots, col_spots),
        out_shape=outs,
        grid_spec=pltpu.PrefetchScalarGridSpec(
            num_scalar_prefetch=0,
            grid=(),
            in_specs=[pl.BlockSpec(memory_space=pltpu.SMEM)] * 2
            + [pl.BlockSpec(memory_space=pltpu.HBM)] * 2
            + [pl.BlockSpec(memory_space=pltpu.VMEM)] * (5 + len(pieces)),
            out_specs=[pl.BlockSpec(memory_space=pltpu.VMEM)] * len(outs),
            scratch_shapes=[
                pltpu.VMEM((len(row_spots), rank, rows), f32),
                pltpu.VMEM((len(row_spots), rank, rows), bf16),
                pltpu.VMEM((len(col_spots), rank, cols), bf16),
                pltpu.VMEM((2 * rank, 2 * cols), bf16),
                pltpu.VMEM((half * rank, 2 * cols), bf16),
                pltpu.VMEM((rank * (slab + 1), cols), f32),
                pltpu.VMEM((rank // 2, slots * slab, 2 * rank), bf16),
                pltpu.VMEM((slots * slab, rank), bf16),
                pltpu.VMEM((depth_blocks * slab, rank), f32),
                pltpu.VMEM((2, 2, rows, slab, cols), bf16),
                pltpu.SemaphoreType.DMA((2, 2)),
            ],
        ),
        input_output_aliases={8 + len(pieces): len(outs) - 1},
        compiler_params=pltpu.CompilerParams(vmem_limit_bytes=40 * 2**20),
        cost_estimate=pl.CostEstimate(flops=10**9, bytes_accessed=16 * 2**20, transcendentals=0),
        name="terms",
    )(counts, coords, data, weight, cube, cube_turned, *pieces, core, depth, spread)


mark_rows = 16
top_exponent = 14.0


def vmem_call(kernel, out_shape, *operands, name):
    return pl.pallas_call(
        kernel,
        out_shape=out_shape,
        in_specs=[pl.BlockSpec(memory_space=pltpu.VMEM)] * len(operands),
        out_specs=tuple(pl.BlockSpec(memory_space=pltpu.VMEM) for _ in out_shape),
        compiler_params=pltpu.CompilerParams(vmem_limit_bytes=24 * 2**20),
        name=name,
    )(*operands)


def power_of(exponent):
    whole = jnp.abs(exponent).astype(jnp.int32)
    value = jnp.ones_like(exponent)
    for bit in range(7):
        factor = jnp.where(exponent < 0, f32(2.0 ** -(2**bit)), f32(2.0 ** (2**bit)))
        value = value * jnp.where((whole >> bit) & 1 == 1, factor, f32(1.0))
    return value


def exponent_of(value):
    lanes = value.shape[-1]
    largest = jnp.max(jnp.max(jnp.abs(value.reshape(-1, 8, lanes)), axis=0), axis=0, keepdims=True)
    largest = jnp.max(largest, axis=1, keepdims=True)
    largest = jnp.broadcast_to(jnp.maximum(largest, f32(1e-30)), (8, lanes))
    return jnp.ceil(jnp.log(largest) * f32(1.4426950408889634)) - f32(top_exponent)


def rounded(value):
    stretched = value * f32(8193.0)
    return stretched - (stretched - value)


def scaled(value):
    exponent = exponent_of(value)
    return rounded(value * power_of(-exponent)[:1]), exponent


def fill_message(out, *parts):
    at = 0
    mark = None
    for which, (flat, exponent) in enumerate(parts):
        out[at : at + flat.shape[0], :] = flat
        at += flat.shape[0]
        exponent = jnp.broadcast_to(exponent[:1], (mark_rows, flat.shape[1]))
        line = lax.broadcasted_iota(jnp.int32, exponent.shape, 0)
        mark = exponent if mark is None else jnp.where(line >= which, exponent, mark)
    out[at : at + mark_rows, :] = mark


def message_part(message, start, rows, part):
    mark = message.shape[0] - mark_rows + part
    return message[start : start + rows, :] * power_of(message[mark : mark + 1, :])


def message_shape(chunks, rank, lanes):
    return jax.ShapeDtypeStruct((chunks * rank + mark_rows, lanes), f32)


def tree_sum(values):
    values = list(values)
    while len(values) > 1:
        values = [values[at] + values[at + 1] for at in range(0, len(values), 2)]
    return values[0]


def after_cores_kernel(n_ia, n_ka, keep, got, own_core, own_depth, own_rows, *messages):
    half = n_ia * n_ka
    depth = keep[half + n_ka] + got[half + n_ka]
    flat, exponent = scaled(depth)
    own_depth[...] = flat * power_of(exponent)[:1]
    own_core[...] = keep[:n_ka] + got[:n_ka]
    own_rows[...] = keep[half : half + n_ka] + got[half : half + n_ka]
    for mask in range(1, n_ia):
        lines = slice(mask * n_ka, (mask + 1) * n_ka)
        core = (keep[lines] + got[lines]).reshape(-1, depth.shape[1])
        fill_message(messages[mask - 1], scaled(core), (flat, exponent))


def after_cores(n_ia, n_ka, keep, got):
    _, rank, lanes = keep.shape
    outs = [jax.ShapeDtypeStruct(shape, f32) for shape in ((n_ka, rank, lanes), (rank, lanes), (n_ka, rank, lanes))]
    outs += [message_shape(n_ka + 1, rank, lanes)] * (n_ia - 1)
    outs = vmem_call(functools.partial(after_cores_kernel, n_ia, n_ka), tuple(outs), keep, got, name="after_cores")
    return outs[0], outs[1], outs[2], outs[3:]


def after_rows_kernel(n_ia, n_ka, own_core, own_depth, own_rows, cols_sum, *refs):
    messages, refs = refs[: n_ia - 1], refs[n_ia - 1 :]
    depth_out, *outs = refs
    count, rank, lanes = own_core.shape
    depths = [own_depth[...]] + [message_part(message, count * rank, rank, 1) for message in messages]
    depth_out[...] = tree_sum(depths)
    core = own_core[...].reshape(count * rank, lanes)
    for message in messages:
        core = core + message_part(message, 0, count * rank, 0)
    flat, exponent = scaled(core)
    for mask in range(n_ka):
        fill_message(outs[mask], (flat, exponent), scaled(own_rows[mask]), scaled(cols_sum[mask]))


def after_rows(n_ia, n_ka, own_core, own_depth, own_rows, cols_sum, messages):
    count, rank, lanes = own_core.shape
    outs = (jax.ShapeDtypeStruct((rank, lanes), f32),) + (message_shape(count + 2, rank, lanes),) * n_ka
    outs = vmem_call(
        functools.partial(after_rows_kernel, n_ia, n_ka),
        outs,
        own_core,
        own_depth,
        own_rows,
        cols_sum,
        *messages,
        name="after_rows",
    )
    return outs[0], outs[1:]


def after_depths_kernel(n_ka, rank, *refs):
    messages, (out, rows_out) = refs[:n_ka], refs[n_ka:]
    rows_out[...] = tree_sum(message_part(message, n_ka * rank, rank, 1) for message in messages)
    cores = []
    for mask, message in enumerate(messages):
        part = message_part(message, 0, n_ka * rank, 0)
        cores.append(jnp.concatenate([part[(at ^ mask) * rank : ((at ^ mask) + 1) * rank] for at in range(n_ka)]))
    cols = tree_sum(message_part(message, (n_ka + 1) * rank, rank, 2) for message in messages)
    fill_message(out, scaled(tree_sum(cores)), scaled(cols))


def after_depths(n_ka, rank, messages):
    lanes = messages[0].shape[1]
    outs = (message_shape(n_ka + 1, rank, lanes), jax.ShapeDtypeStruct((rank, lanes), f32))
    return vmem_call(functools.partial(after_depths_kernel, n_ka, rank), outs, *messages, name="after_depths")


def unpack_kernel(sizes, rank, first_message, *refs):
    n_ia, n_ka = sizes["ia"], sizes["ka"]
    messages = refs[:n_ia]
    near = first_message == 0
    pairs = rank // 2
    ia, ja, ka = lax.axis_index("ia"), lax.axis_index("ja"), lax.axis_index("ka")
    copies = []
    if near:
        rows_total, depth_total, core_out, rows_out, depth_out, cols_out, cols_here, whole, sems = refs[n_ia:]
        cols_here[...] = tree_sum(message_part(message, n_ka * rank, rank, 1) for message in messages)
        for source, out in ((rows_total, rows_out), (depth_total, depth_out), (cols_here, cols_out)):
            copies.append(pltpu.make_async_copy(source, out, sems.at[2 * n_ia + len(copies)]))
            copies[-1].start()
    else:
        core_out, whole, sems = refs[n_ia + 1 :]
    for at in range(n_ia):
        first = pl.multiple_of(((ja * n_ia + ia) ^ (first_message + at)) * n_ka, n_ka)
        for mask in range(n_ka):
            piece = message_part(messages[at], mask * rank, rank, 0)
            whole[at, 0, ka ^ mask] = piece[:, :rank]
            whole[at, 1, ka ^ mask] = piece[:, rank:]
        for h in range(2):
            lines = pl.ds(h * pairs + first, n_ka)
            copies.append(pltpu.make_async_copy(whole.at[at, h], core_out.at[lines], sems.at[2 * at + h]))
            copies[-1].start()
    for copy in copies:
        copy.wait()


def unpack(sizes, rank, messages, core=None, *totals):
    lanes = messages[0].shape[1]
    near = core is None
    given = list(totals) if near else [core]
    scratch = [pltpu.VMEM((rank, lanes), f32)] if near else []
    out_shape = [jax.ShapeDtypeStruct((rank, rank, rank), f32)]
    if near:
        out_shape += [jax.ShapeDtypeStruct(total.shape, f32) for total in totals]
        out_shape += [jax.ShapeDtypeStruct((rank, lanes), f32)]
    return pl.pallas_call(
        functools.partial(unpack_kernel, sizes, rank, 0 if near else sizes["ia"]),
        out_shape=tuple(out_shape),
        in_specs=[pl.BlockSpec(memory_space=pltpu.VMEM)] * len(messages)
        + [pl.BlockSpec(memory_space=pltpu.VMEM if near else pltpu.HBM)] * len(given),
        out_specs=tuple(pl.BlockSpec(memory_space=pltpu.HBM) for _ in out_shape),
        scratch_shapes=[
            *scratch,
            pltpu.VMEM((len(messages), 2, sizes["ka"], rank, rank), f32),
            pltpu.SemaphoreType.DMA((2 * len(messages) + 3,)),
        ],
        input_output_aliases={} if near else {len(messages): 0},
        compiler_params=pltpu.CompilerParams(vmem_limit_bytes=24 * 2**20),
        cost_estimate=pl.CostEstimate(flops=10**6, bytes_accessed=4 * 2**20, transcendentals=0),
        name="unpack_near" if near else "unpack_far",
    )(*messages, *given)


def power_of_two(n):
    return n & (n - 1) == 0


def swap(value, axis, size, mask):
    return lax.ppermute(value, axis, [(at, at ^ mask) for at in range(size)])


def on_device(sizes, observed, weights, coords, counts, factor_rows, factor_cols, factor_depth, core_tensor):
    n_ia, n_ja, n_ka = sizes["ia"], sizes["ja"], sizes["ka"]
    devices = n_ia * n_ja * n_ka
    rank = core_tensor.shape[0]
    _, _, slots, rows, slab, cols = observed.shape
    data = pltpu.with_memory_space_constraint(observed.reshape(observed.shape[2:]), pltpu.HBM)
    weight = pltpu.with_memory_space_constraint(weights.reshape(weights.shape[2:]), pltpu.HBM)
    core_here = pltpu.with_memory_space_constraint(core_tensor, pltpu.HBM)
    depth_here = pltpu.with_memory_space_constraint(factor_depth, pltpu.HBM)
    row_chunks = factor_rows.shape[1] * n_ja * n_ka // rows
    col_chunks = factor_cols.shape[1] * n_ka // cols
    depth_blocks = factor_depth.shape[1] // n_ka // slab
    ia, ja, ka = lax.axis_index("ia"), lax.axis_index("ja"), lax.axis_index("ka")
    by_swaps = (
        n_ja == 2
        and power_of_two(n_ia)
        and power_of_two(n_ka)
        and rank // 2 == devices
        and factor_rows.shape[1] == rows
        and factor_cols.shape[1] == cols
        and rows == cols == 2 * rank == depth_blocks * slab
    )

    if by_swaps:
        own = jnp.stack([factor_rows, swap(factor_rows, "ja", n_ja, 1), factor_cols])
        pieces = [own] + [swap(own, "ka", n_ka, mask) for mask in range(1, n_ka)]
        row_spots = [(mask, line) for line in range(n_ja) for mask in range(n_ka)]
        col_spots = [(mask, n_ja) for mask in range(n_ka)]
    else:
        row_table = lax.all_gather(factor_rows, ("ja", "ka"), axis=1, tiled=True)
        row_table = row_table.reshape(rank, row_chunks, rows).transpose(1, 0, 2)
        col_table = lax.all_gather(factor_cols, "ka", axis=1, tiled=True)
        col_table = col_table.reshape(rank, col_chunks, cols).transpose(1, 0, 2)
        pieces = [row_table, col_table]
        row_spots = [(0, line) for line in range(row_chunks)]
        own = row_table
        col_spots = [(1, line) for line in range(col_chunks)]

    cube, cube_turned, core_pairs, own_depth, coords, spread = first_cubes(
        own,
        depth_here,
        core_here,
        pltpu.with_memory_space_constraint(coords.transpose(0, 3, 1, 2), pltpu.HBM),
        data,
        weight,
        depth_blocks,
    )
    *sums, cols_sum, _ = terms(
        by_swaps,
        sizes,
        row_spots,
        col_spots,
        counts,
        coords,
        data,
        weight,
        cube,
        cube_turned,
        pieces,
        core_pairs,
        own_depth,
        spread,
    )

    if not by_swaps:
        core_sum, rows_sum, depth_sum = sums
        rows_whole = rows_sum.transpose(1, 0, 2).reshape(rank, row_chunks * rows)
        cols_whole = cols_sum.transpose(1, 0, 2).reshape(rank, col_chunks * cols)
        core_whole = core_sum.reshape(rank // 2, rank, 2, rank).transpose(2, 0, 1, 3).reshape(rank, rank, rank)
        return (
            lax.psum_scatter(rows_whole, ("ja", "ka"), scatter_dimension=1, tiled=True),
            lax.psum_scatter(lax.psum(cols_whole, "ia"), "ka", scatter_dimension=1, tiled=True),
            lax.psum(depth_sum, ("ia", "ja")),
            lax.psum(core_whole, ("ia", "ja", "ka")),
        )

    keep, send = sums
    got = swap(send, "ja", n_ja, 1)
    own_core, own_depth, own_rows, messages = after_cores(n_ia, n_ka, keep, got)
    messages = [swap(message.astype(wire), "ia", n_ia, at + 1).astype(f32) for at, message in enumerate(messages)]
    depth_total, messages = after_rows(n_ia, n_ka, own_core, own_depth, own_rows, cols_sum, messages)
    messages = [messages[0]] + [
        swap(messages[mask].astype(wire), "ka", n_ka, mask).astype(f32) for mask in range(1, n_ka)
    ]
    message, rows_total = after_depths(n_ka, rank, messages)
    sent = message.astype(wire)
    sent = [sent] + [swap(sent, "ia", n_ia, mask) for mask in range(1, n_ia)]
    other = [swap(each, "ja", n_ja, 1) for each in sent]
    core_near, rows_total, depth_total, cols_total = unpack(
        sizes, rank, [each.astype(f32) for each in sent], None, rows_total, depth_total
    )
    (core_total,) = unpack(sizes, rank, [each.astype(f32) for each in other], core_near)
    return (rows_total, cols_total, depth_total, core_total)


def solution(mesh):
    in_specs = (
        P("ia", "ja", "ka", None, None, None),
        P("ia", "ja", "ka", None, None, None),
        P("ia", "ja", "ka", None),
        P("ia", "ja", "ka"),
        P(None, ("ia", "ja", "ka")),
        P(None, ("ja", "ka")),
        P(),
        P(),
    )
    out_specs = (P(None, ("ia", "ja", "ka")), P(None, ("ja", "ka")), P(None, "ka"), P())
    return jax.shard_map(
        functools.partial(on_device, dict(mesh.shape)),
        mesh=mesh,
        in_specs=in_specs,
        out_specs=out_specs,
        check_vma=False,
    )
```

```python
import functools

import jax
import jax.numpy as jnp
from jax import lax
from jax.experimental import pallas as pl
from jax.experimental.pallas import tpu as pltpu
from jax.sharding import PartitionSpec as P

resid_scale = 1.0 / 64.0
f32 = jnp.float32
bf16 = jnp.bfloat16
wire = jnp.float16


def dot(a, b, contract=((1,), (0,))):
    return lax.dot_general(a, b, (contract, ((), ())), preferred_element_type=f32)


def spread_out(source, target):
    rows, slab, _ = source.shape
    for i in range(rows):
        target[i * (slab + 1) : i * (slab + 1) + slab, :] = source[i].astype(f32)


def cube_kernel(
    slab,
    after,
    factor_depth,
    core,
    coords,
    data,
    weight,
    cube_out,
    cube_turned_out,
    core_out,
    depth_out,
    coords_out,
    spread,
    depth_here,
    core_here,
    fetched,
    cube_wide,
    sems,
):
    pairs, _, rank = core_out.shape
    half = slab // 2
    depth_blocks = cube_out.shape[0]
    width = depth_here.shape[1]
    start = pl.multiple_of(lax.axis_index("ka") * width, width)
    copies = [
        pltpu.make_async_copy(factor_depth.at[:, pl.ds(start, width)], depth_here, sems.at[0]),
        pltpu.make_async_copy(core, core_here, sems.at[1]),
        pltpu.make_async_copy(coords, coords_out, sems.at[2]),
        pltpu.make_async_copy(data.at[0], fetched.at[0], sems.at[3]),
        pltpu.make_async_copy(weight.at[0], fetched.at[1], sems.at[4]),
    ]
    for copy in copies:
        copy.start()
    copies[0].wait()
    depth = depth_here[...].astype(f32).T.astype(bf16)
    depth_out[...] = depth
    order = [depth[t * slab + h * half : t * slab + (h + 1) * half] for h in range(2) for t in range(depth_blocks)]
    ordered = jnp.concatenate(order, axis=0)
    count = depth_blocks * half
    copies[1].wait()
    for pair in range(pairs):
        core_out[pair] = jnp.concatenate([core_here[pair], core_here[pairs + pair]], axis=0)

    def one_pair(pair, carry):
        piece = dot(ordered, core_out[pair], ((1,), (1,)))
        for which in range(2):
            here = piece[:, which * rank : (which + 1) * rank]
            wide = jnp.concatenate([here[:count], here[count:]], axis=1)
            cube_wide[pl.ds(which * pairs + pair, count, stride=rank + 1), :] = wide
        return carry

    lax.fori_loop(0, pairs, one_pair, 0, unroll=8)
    for t in range(depth_blocks):
        for kp in range(half):
            at = (t * half + kp) * (rank + 1)
            block = cube_wide[at : at + rank, :]
            cube_out[t, kp * rank : (kp + 1) * rank, :] = block.astype(bf16)
        cube_turned_out[t] = cube_out[t].astype(f32).T.astype(bf16)
    for copy in copies[2:]:
        copy.wait()
    for at in range(2):
        spread_out(fetched.at[at], spread.at[at])


def first_cubes(after, factor_depth, core, coords, data, weight, depth_blocks):
    rank = core.shape[0]
    _, rows, slab, cols = data.shape
    half = slab // 2
    width = depth_blocks * slab
    return pl.pallas_call(
        functools.partial(cube_kernel, slab),
        out_shape=(
            jax.ShapeDtypeStruct((depth_blocks, half * rank, 2 * rank), bf16),
            jax.ShapeDtypeStruct((depth_blocks, 2 * rank, half * rank), bf16),
            jax.ShapeDtypeStruct((rank // 2, 2 * rank, rank), bf16),
            jax.ShapeDtypeStruct((width, rank), bf16),
            jax.ShapeDtypeStruct(coords.shape, coords.dtype),
            jax.ShapeDtypeStruct((2, rows * (slab + 1), cols), f32),
        ),
        in_specs=[pl.BlockSpec(memory_space=pl.ANY)] + [pl.BlockSpec(memory_space=pltpu.HBM)] * 5,
        out_specs=[pl.BlockSpec(memory_space=pltpu.VMEM)] * 4
        + [pl.BlockSpec(memory_space=pltpu.SMEM), pl.BlockSpec(memory_space=pltpu.VMEM)],
        scratch_shapes=[
            pltpu.VMEM((rank, width), bf16),
            pltpu.VMEM(core.shape, bf16),
            pltpu.VMEM((2, rows, slab, cols), bf16),
            pltpu.VMEM((depth_blocks * half * (rank + 1), 2 * rank), f32),
            pltpu.SemaphoreType.DMA((5,)),
        ],
        compiler_params=pltpu.CompilerParams(vmem_limit_bytes=40 * 2**20),
        cost_estimate=pl.CostEstimate(flops=10**9, bytes_accessed=4 * 2**20, transcendentals=0),
        name="first_cubes",
    )(after, factor_depth, core, coords, data, weight)


def masks_of(relative, sizes):
    ia, ja, ka = lax.axis_index("ia"), lax.axis_index("ja"), lax.axis_index("ka")
    if not relative:
        return 0, 0, 0
    return ja * sizes["ka"] + ka, ka, (ja * sizes["ia"] + ia) * sizes["ka"] + ka


def core_chunk(second, depth):
    rank = depth.shape[1]
    piece = dot(second, depth, ((0,), (0,)))
    return jnp.concatenate([piece[:rank], piece[rank:]], axis=1)


def keep_kernel(sizes, second_all, depth_all, out):
    core_mask = masks_of(True, sizes)[2]
    for at in range(out.shape[0]):
        out[at] = core_chunk(second_all[at ^ core_mask], depth_all[...])


def keep_terms(sizes, second_all, depth_all):
    pairs, _, lanes = second_all.shape
    return pl.pallas_call(
        functools.partial(keep_kernel, sizes),
        out_shape=jax.ShapeDtypeStruct((pairs // 2, depth_all.shape[1], lanes), f32),
        in_specs=[pl.BlockSpec(memory_space=pltpu.VMEM)] * 2,
        out_specs=pl.BlockSpec(memory_space=pltpu.VMEM),
        compiler_params=pltpu.CompilerParams(vmem_limit_bytes=24 * 2**20),
        cost_estimate=pl.CostEstimate(flops=10**9, bytes_accessed=4 * 2**20, transcendentals=0),
        name="keep_terms",
    )(second_all, depth_all)


def terms_kernel(relative, sizes, row_spots, col_spots, counts, coords, data, weight, cube, cube_turned, *refs):
    pieces = refs[: 1 + max(at for at, _ in row_spots + col_spots)]
    (
        core,
        depth_turned,
        _,
        *outs,
        cols_out,
        second_all,
        depth_all,
        spread,
        rows_out,
        row_table,
        col_table,
        wide_col,
        backward,
        by_rank,
        depth_sum,
        fetched,
        sems,
    ) = refs[len(pieces) :]
    slots, rows, slab, cols = data.shape
    pairs = core.shape[0]
    rank = 2 * pairs
    half = slab // 2
    depth_blocks = cube.shape[0]
    count = counts[0, 0, 0]
    row_mask, col_mask, core_mask = masks_of(relative, sizes)
    row_base = lax.axis_index("ia") * row_table.shape[0]
    col_base = lax.axis_index("ja") * col_table.shape[0]
    depth_base = lax.axis_index("ka") * depth_blocks

    def fetches(slot):
        side = lax.rem(slot, 2)
        return [
            pltpu.make_async_copy(source.at[slot], fetched.at[side, which], sems.at[side, which])
            for which, source in enumerate((data, weight))
        ]

    def fetch(slot):
        @pl.when(slot < count)
        def _():
            for copy in fetches(slot):
                copy.start()

    def arrive(slot):
        for copy in fetches(slot):
            copy.wait()

    for s in range(slots):

        @pl.when(s >= count)
        def _():
            lines = slice(s * slab, (s + 1) * slab)
            second_all[:, lines, :] = jnp.zeros((pairs, slab, 2 * rank), bf16)
            depth_all[lines, :] = jnp.zeros((slab, rank), bf16)

    depth_sum[...] = jnp.zeros_like(depth_sum)
    rows_out[...] = jnp.zeros_like(rows_out)
    cols_out[...] = jnp.zeros_like(cols_out)
    wide_col[...] = jnp.zeros_like(wide_col)
    for spots, table in ((row_spots, row_table), (col_spots, col_table)):
        for at, (piece, line) in enumerate(spots):
            table[at] = pieces[piece][line]

    def one_slot(slot, carry):
        fetch(slot + 1)

        @pl.when(slot > 0)
        def _():
            arrive(slot)
            for which in range(2):
                spread_out(fetched.at[lax.rem(slot, 2), which], spread.at[which])

        row_at = (coords[0, 0, 0, slot] - row_base) ^ row_mask
        col_at = (coords[0, 1, 0, slot] - col_base) ^ col_mask
        depth_at = coords[0, 2, 0, slot] - depth_base
        row_factor = row_table[row_at]
        row_turned = row_factor.astype(f32).T.astype(bf16)
        col_factor = col_table[col_at]
        wide_col[:rank, :cols] = col_factor
        wide_col[rank:, cols:] = col_factor
        own_depth = depth_turned[pl.ds(pl.multiple_of(depth_at * slab, slab), slab), :]
        depth_all[pl.ds(pl.multiple_of(slot * slab, slab), slab), :] = own_depth

        step = 8
        groups = half // step
        wide_factor = wide_col[...]
        def second_of(g):
            lines = cube[depth_at, g * step * rank : (g + 1) * step * rank, :]
            block = dot(lines, wide_factor).astype(bf16)
            return jnp.concatenate([block[kp * rank : (kp + 1) * rank] for kp in range(step)], axis=1)

        def residual_of(g, model):
            parts = []
            for kp in range(step):
                for h in range(2):
                    lines = pl.ds(h * half + g * step + kp, rows, stride=slab + 1)
                    seen, scale = spread[0, lines, :], spread[1, lines, :]
                    at = (kp * 2 + h) * cols
                    gap = model[:, at : at + cols] - seen
                    parts.append((scale * gap * resid_scale).astype(bf16))
            return jnp.concatenate(parts, axis=1)

        def keep_back(g, back):
            back = back.astype(bf16)
            for kp in range(step):
                pair = back[:, kp * 2 * cols : (kp + 1) * 2 * cols]
                at = (g * step + kp) * rank
                backward[at : at + rank, :] = pair
                wider = pair.astype(f32)
                for h in range(2):
                    lines = pl.ds(h * half + g * step + kp, rank, stride=slab + 1)
                    by_rank[lines, :] = wider[:, h * cols : (h + 1) * cols]

        row_sum = jnp.zeros((rows, rank), f32)
        seconds = [second_of(g) for g in range(groups)]
        models = [None] * groups
        models[0] = dot(row_turned, seconds[0])
        for g in range(groups):
            if g + 1 < groups:
                models[g + 1] = dot(row_turned, seconds[g + 1])
            residual = residual_of(g, models[g])
            keep_back(g, dot(row_factor, residual))
            row_sum = row_sum + dot(residual, seconds[g], ((1,), (1,)))
        rows_out[row_at] += row_sum.T
        wide = dot(cube_turned[depth_at], backward[...])
        cols_out[col_at] += wide[:rank, :cols] + wide[rank:, cols:]
        lines = pl.ds(pl.multiple_of(slot * slab, slab), slab)
        for first in range(0, pairs, 8):
            ranked = []
            for pair in range(first, first + 8):
                spots = [at * (slab + 1) for at in (pair, pairs + pair)]
                ranked.append(jnp.concatenate([by_rank[at : at + slab, :].astype(bf16) for at in spots], axis=1))
            ranked = jnp.concatenate(ranked, axis=0)
            second_back = dot(ranked, wide_col[...], ((1,), (1,))).astype(bf16)
            second_all[first : first + 8, lines, :] = second_back.reshape(8, slab, 2 * rank)

        return carry

    lax.fori_loop(0, count, one_slot, 0)

    if relative:
        start, row_count = pairs // 2, len(row_spots) // 2
        core_spots = [None] * start + [(outs[1], at) for at in range(start)]
        row_places = [(outs[0], at) for at in range(row_count)] + [(outs[1], start + at) for at in range(row_count)]
    else:
        core_spots = [(outs[0], at) for at in range(pairs)]
        row_places = [(outs[1], at) for at in range(len(row_spots))]
    total = jnp.zeros((second_all.shape[1], rank), f32)
    for pair in range(pairs):
        total = total + dot(second_all[pair], core[pair])
    for at, spot in enumerate(core_spots):
        if spot is not None:
            out, line = spot
            out[line] = core_chunk(second_all[at ^ core_mask], depth_all[...])
    for at, (out, line) in enumerate(row_places):
        out[line] = rows_out[at]
    for s in range(slots):

        @pl.when(s < count)
        def _():
            at = coords[0, 2, 0, s] - depth_base
            lines = pl.ds(pl.multiple_of(at * slab, slab), slab)
            depth_sum[lines, :] += total[s * slab : (s + 1) * slab]

    depth = depth_sum[...].T
    if relative:
        outs[0][row_count] = depth
        outs[1][start + row_count] = depth
    else:
        outs[2][...] = depth


def terms(relative, sizes, row_spots, col_spots, counts, coords, data, weight, cube, cube_turned, pieces, core, depth, spread):
    slots, rows, slab, cols = data.shape
    rank = core.shape[2]
    half = slab // 2
    depth_blocks = cube.shape[0]

    width = depth_blocks * slab
    if relative:
        chunks = len(row_spots) // 2 + 1
        outs = tuple(jax.ShapeDtypeStruct((at, rank, rows), f32) for at in (chunks, rank // 4 + chunks))
    else:
        outs = (
            jax.ShapeDtypeStruct((rank // 2, rank, 2 * rank), f32),
            jax.ShapeDtypeStruct((len(row_spots), rank, rows), f32),
            jax.ShapeDtypeStruct((rank, width), f32),
        )
    outs += (
        jax.ShapeDtypeStruct((len(col_spots), rank, cols), f32),
        jax.ShapeDtypeStruct((rank // 2, slots * slab, 2 * rank), bf16),
        jax.ShapeDtypeStruct((slots * slab, rank), bf16),
        jax.ShapeDtypeStruct(spread.shape, f32),
    )
    return pl.pallas_call(
        functools.partial(terms_kernel, relative, sizes, row_spots, col_spots),
        out_shape=outs,
        grid_spec=pltpu.PrefetchScalarGridSpec(
            num_scalar_prefetch=0,
            grid=(),
            in_specs=[pl.BlockSpec(memory_space=pltpu.SMEM)] * 2
            + [pl.BlockSpec(memory_space=pltpu.HBM)] * 2
            + [pl.BlockSpec(memory_space=pltpu.VMEM)] * (5 + len(pieces)),
            out_specs=[pl.BlockSpec(memory_space=pltpu.VMEM)] * len(outs),
            scratch_shapes=[
                pltpu.VMEM((len(row_spots), rank, rows), f32),
                pltpu.VMEM((len(row_spots), rank, rows), bf16),
                pltpu.VMEM((len(col_spots), rank, cols), bf16),
                pltpu.VMEM((2 * rank, 2 * cols), bf16),
                pltpu.VMEM((half * rank, 2 * cols), bf16),
                pltpu.VMEM((rank * (slab + 1), cols), f32),
                pltpu.VMEM((depth_blocks * slab, rank), f32),
                pltpu.VMEM((2, 2, rows, slab, cols), bf16),
                pltpu.SemaphoreType.DMA((2, 2)),
            ],
        ),
        input_output_aliases={8 + len(pieces): len(outs) - 1},
        compiler_params=pltpu.CompilerParams(vmem_limit_bytes=40 * 2**20),
        cost_estimate=pl.CostEstimate(flops=10**9, bytes_accessed=16 * 2**20, transcendentals=0),
        name="terms",
    )(counts, coords, data, weight, cube, cube_turned, *pieces, core, depth, spread)


mark_rows = 16
top_exponent = 14.0


def vmem_call(kernel, out_shape, *operands, name):
    return pl.pallas_call(
        kernel,
        out_shape=out_shape,
        in_specs=[pl.BlockSpec(memory_space=pltpu.VMEM)] * len(operands),
        out_specs=tuple(pl.BlockSpec(memory_space=pltpu.VMEM) for _ in out_shape),
        compiler_params=pltpu.CompilerParams(vmem_limit_bytes=24 * 2**20),
        name=name,
    )(*operands)


def power_of(exponent):
    whole = jnp.abs(exponent).astype(jnp.int32)
    value = jnp.ones_like(exponent)
    for bit in range(7):
        factor = jnp.where(exponent < 0, f32(2.0 ** -(2**bit)), f32(2.0 ** (2**bit)))
        value = value * jnp.where((whole >> bit) & 1 == 1, factor, f32(1.0))
    return value


def exponent_of(value):
    lanes = value.shape[-1]
    largest = jnp.max(jnp.max(jnp.abs(value.reshape(-1, 8, lanes)), axis=0), axis=0, keepdims=True)
    largest = jnp.max(largest, axis=1, keepdims=True)
    largest = jnp.broadcast_to(jnp.maximum(largest, f32(1e-30)), (8, lanes))
    return jnp.ceil(jnp.log(largest) * f32(1.4426950408889634)) - f32(top_exponent)


def rounded(value):
    stretched = value * f32(8193.0)
    return stretched - (stretched - value)


def scaled(value):
    exponent = exponent_of(value)
    return rounded(value * power_of(-exponent)[:1]), exponent


def fill_message(out, *parts):
    at = 0
    mark = None
    for which, (flat, exponent) in enumerate(parts):
        out[at : at + flat.shape[0], :] = flat
        at += flat.shape[0]
        exponent = jnp.broadcast_to(exponent[:1], (mark_rows, flat.shape[1]))
        line = lax.broadcasted_iota(jnp.int32, exponent.shape, 0)
        mark = exponent if mark is None else jnp.where(line >= which, exponent, mark)
    out[at : at + mark_rows, :] = mark


def message_part(message, start, rows, part):
    mark = message.shape[0] - mark_rows + part
    return message[start : start + rows, :] * power_of(message[mark : mark + 1, :])


def message_shape(chunks, rank, lanes):
    return jax.ShapeDtypeStruct((chunks * rank + mark_rows, lanes), f32)


def tree_sum(values):
    values = list(values)
    while len(values) > 1:
        values = [values[at] + values[at + 1] for at in range(0, len(values), 2)]
    return values[0]


def after_cores_kernel(n_ia, n_ka, core_keep, keep, got, own_core, own_depth, own_rows, *messages):
    half = n_ia * n_ka
    depth = keep[n_ka] + got[half + n_ka]
    flat, exponent = scaled(depth)
    own_depth[...] = flat * power_of(exponent)[:1]
    own_core[...] = core_keep[:n_ka] + got[:n_ka]
    own_rows[...] = keep[:n_ka] + got[half : half + n_ka]
    for mask in range(1, n_ia):
        lines = slice(mask * n_ka, (mask + 1) * n_ka)
        core = (core_keep[lines] + got[lines]).reshape(-1, depth.shape[1])
        fill_message(messages[mask - 1], scaled(core), (flat, exponent))


def after_cores(n_ia, n_ka, core_keep, keep, got):
    _, rank, lanes = keep.shape
    outs = [jax.ShapeDtypeStruct(shape, f32) for shape in ((n_ka, rank, lanes), (rank, lanes), (n_ka, rank, lanes))]
    outs += [message_shape(n_ka + 1, rank, lanes)] * (n_ia - 1)
    outs = vmem_call(functools.partial(after_cores_kernel, n_ia, n_ka), tuple(outs), core_keep, keep, got, name="after_cores")
    return outs[0], outs[1], outs[2], outs[3:]


def after_rows_kernel(n_ia, n_ka, own_core, own_depth, own_rows, cols_sum, *refs):
    messages, refs = refs[: n_ia - 1], refs[n_ia - 1 :]
    depth_out, *outs = refs
    count, rank, lanes = own_core.shape
    depths = [own_depth[...]] + [message_part(message, count * rank, rank, 1) for message in messages]
    depth_out[...] = tree_sum(depths)
    core = own_core[...].reshape(count * rank, lanes)
    for message in messages:
        core = core + message_part(message, 0, count * rank, 0)
    flat, exponent = scaled(core)
    for mask in range(n_ka):
        fill_message(outs[mask], (flat, exponent), scaled(own_rows[mask]), scaled(cols_sum[mask]))


def after_rows(n_ia, n_ka, own_core, own_depth, own_rows, cols_sum, messages):
    count, rank, lanes = own_core.shape
    outs = (jax.ShapeDtypeStruct((rank, lanes), f32),) + (message_shape(count + 2, rank, lanes),) * n_ka
    outs = vmem_call(
        functools.partial(after_rows_kernel, n_ia, n_ka),
        outs,
        own_core,
        own_depth,
        own_rows,
        cols_sum,
        *messages,
        name="after_rows",
    )
    return outs[0], outs[1:]


def after_depths_kernel(n_ka, rank, *refs):
    messages, (out, rows_out) = refs[:n_ka], refs[n_ka:]
    rows_out[...] = tree_sum(message_part(message, n_ka * rank, rank, 1) for message in messages)
    cores = []
    for mask, message in enumerate(messages):
        part = message_part(message, 0, n_ka * rank, 0)
        cores.append(jnp.concatenate([part[(at ^ mask) * rank : ((at ^ mask) + 1) * rank] for at in range(n_ka)]))
    cols = tree_sum(message_part(message, (n_ka + 1) * rank, rank, 2) for message in messages)
    fill_message(out, scaled(tree_sum(cores)), scaled(cols))


def after_depths(n_ka, rank, messages):
    lanes = messages[0].shape[1]
    outs = (message_shape(n_ka + 1, rank, lanes), jax.ShapeDtypeStruct((rank, lanes), f32))
    return vmem_call(functools.partial(after_depths_kernel, n_ka, rank), outs, *messages, name="after_depths")


def unpack_kernel(sizes, rank, first_message, *refs):
    n_ia, n_ka = sizes["ia"], sizes["ka"]
    messages = refs[:n_ia]
    near = first_message == 0
    pairs = rank // 2
    ia, ja, ka = lax.axis_index("ia"), lax.axis_index("ja"), lax.axis_index("ka")
    copies = []
    if near:
        rows_total, depth_total, core_out, rows_out, depth_out, cols_out, cols_here, whole, sems = refs[n_ia:]
        cols_here[...] = tree_sum(message_part(message, n_ka * rank, rank, 1) for message in messages)
        for source, out in ((rows_total, rows_out), (depth_total, depth_out), (cols_here, cols_out)):
            copies.append(pltpu.make_async_copy(source, out, sems.at[2 * n_ia + len(copies)]))
            copies[-1].start()
    else:
        core_out, whole, sems = refs[n_ia + 1 :]
    for at in range(n_ia):
        first = pl.multiple_of(((ja * n_ia + ia) ^ (first_message + at)) * n_ka, n_ka)
        for mask in range(n_ka):
            piece = message_part(messages[at], mask * rank, rank, 0)
            whole[at, 0, ka ^ mask] = piece[:, :rank]
            whole[at, 1, ka ^ mask] = piece[:, rank:]
        for h in range(2):
            lines = pl.ds(h * pairs + first, n_ka)
            copies.append(pltpu.make_async_copy(whole.at[at, h], core_out.at[lines], sems.at[2 * at + h]))
            copies[-1].start()
    for copy in copies:
        copy.wait()


def unpack(sizes, rank, messages, core=None, *totals):
    lanes = messages[0].shape[1]
    near = core is None
    given = list(totals) if near else [core]
    scratch = [pltpu.VMEM((rank, lanes), f32)] if near else []
    out_shape = [jax.ShapeDtypeStruct((rank, rank, rank), f32)]
    if near:
        out_shape += [jax.ShapeDtypeStruct(total.shape, f32) for total in totals]
        out_shape += [jax.ShapeDtypeStruct((rank, lanes), f32)]
    return pl.pallas_call(
        functools.partial(unpack_kernel, sizes, rank, 0 if near else sizes["ia"]),
        out_shape=tuple(out_shape),
        in_specs=[pl.BlockSpec(memory_space=pltpu.VMEM)] * len(messages)
        + [pl.BlockSpec(memory_space=pltpu.VMEM if near else pltpu.HBM)] * len(given),
        out_specs=tuple(pl.BlockSpec(memory_space=pltpu.HBM) for _ in out_shape),
        scratch_shapes=[
            *scratch,
            pltpu.VMEM((len(messages), 2, sizes["ka"], rank, rank), f32),
            pltpu.SemaphoreType.DMA((2 * len(messages) + 3,)),
        ],
        input_output_aliases={} if near else {len(messages): 0},
        compiler_params=pltpu.CompilerParams(vmem_limit_bytes=24 * 2**20),
        cost_estimate=pl.CostEstimate(flops=10**6, bytes_accessed=4 * 2**20, transcendentals=0),
        name="unpack_near" if near else "unpack_far",
    )(*messages, *given)


def power_of_two(n):
    return n & (n - 1) == 0


def swap(value, axis, size, mask):
    return lax.ppermute(value, axis, [(at, at ^ mask) for at in range(size)])


def on_device(sizes, observed, weights, coords, counts, factor_rows, factor_cols, factor_depth, core_tensor):
    n_ia, n_ja, n_ka = sizes["ia"], sizes["ja"], sizes["ka"]
    devices = n_ia * n_ja * n_ka
    rank = core_tensor.shape[0]
    _, _, slots, rows, slab, cols = observed.shape
    data = pltpu.with_memory_space_constraint(observed.reshape(observed.shape[2:]), pltpu.HBM)
    weight = pltpu.with_memory_space_constraint(weights.reshape(weights.shape[2:]), pltpu.HBM)
    core_here = pltpu.with_memory_space_constraint(core_tensor, pltpu.HBM)
    depth_here = pltpu.with_memory_space_constraint(factor_depth, pltpu.HBM)
    row_chunks = factor_rows.shape[1] * n_ja * n_ka // rows
    col_chunks = factor_cols.shape[1] * n_ka // cols
    depth_blocks = factor_depth.shape[1] // n_ka // slab
    ia, ja, ka = lax.axis_index("ia"), lax.axis_index("ja"), lax.axis_index("ka")
    by_swaps = (
        n_ja == 2
        and power_of_two(n_ia)
        and power_of_two(n_ka)
        and rank // 2 == devices
        and factor_rows.shape[1] == rows
        and factor_cols.shape[1] == cols
        and rows == cols == 2 * rank == depth_blocks * slab
    )

    if by_swaps:
        own = jnp.stack([factor_rows, swap(factor_rows, "ja", n_ja, 1), factor_cols])
        pieces = [own] + [swap(own, "ka", n_ka, mask) for mask in range(1, n_ka)]
        row_spots = [(mask, line) for line in range(n_ja) for mask in range(n_ka)]
        col_spots = [(mask, n_ja) for mask in range(n_ka)]
    else:
        row_table = lax.all_gather(factor_rows, ("ja", "ka"), axis=1, tiled=True)
        row_table = row_table.reshape(rank, row_chunks, rows).transpose(1, 0, 2)
        col_table = lax.all_gather(factor_cols, "ka", axis=1, tiled=True)
        col_table = col_table.reshape(rank, col_chunks, cols).transpose(1, 0, 2)
        pieces = [row_table, col_table]
        row_spots = [(0, line) for line in range(row_chunks)]
        own = row_table
        col_spots = [(1, line) for line in range(col_chunks)]

    cube, cube_turned, core_pairs, own_depth, coords, spread = first_cubes(
        own,
        depth_here,
        core_here,
        pltpu.with_memory_space_constraint(coords.transpose(0, 3, 1, 2), pltpu.HBM),
        data,
        weight,
        depth_blocks,
    )
    *sums, cols_sum, second_all, depth_all, _ = terms(
        by_swaps,
        sizes,
        row_spots,
        col_spots,
        counts,
        coords,
        data,
        weight,
        cube,
        cube_turned,
        pieces,
        core_pairs,
        own_depth,
        spread,
    )

    if not by_swaps:
        core_sum, rows_sum, depth_sum = sums
        rows_whole = rows_sum.transpose(1, 0, 2).reshape(rank, row_chunks * rows)
        cols_whole = cols_sum.transpose(1, 0, 2).reshape(rank, col_chunks * cols)
        core_whole = core_sum.reshape(rank // 2, rank, 2, rank).transpose(2, 0, 1, 3).reshape(rank, rank, rank)
        return (
            lax.psum_scatter(rows_whole, ("ja", "ka"), scatter_dimension=1, tiled=True),
            lax.psum_scatter(lax.psum(cols_whole, "ia"), "ka", scatter_dimension=1, tiled=True),
            lax.psum(depth_sum, ("ia", "ja")),
            lax.psum(core_whole, ("ia", "ja", "ka")),
        )

    keep, send = sums
    got = swap(send, "ja", n_ja, 1)
    core_keep = keep_terms(sizes, second_all, depth_all)
    own_core, own_depth, own_rows, messages = after_cores(n_ia, n_ka, core_keep, keep, got)
    messages = [swap(message.astype(wire), "ia", n_ia, at + 1).astype(f32) for at, message in enumerate(messages)]
    depth_total, messages = after_rows(n_ia, n_ka, own_core, own_depth, own_rows, cols_sum, messages)
    messages = [messages[0]] + [
        swap(messages[mask].astype(wire), "ka", n_ka, mask).astype(f32) for mask in range(1, n_ka)
    ]
    message, rows_total = after_depths(n_ka, rank, messages)
    sent = message.astype(wire)
    sent = [sent] + [swap(sent, "ia", n_ia, mask) for mask in range(1, n_ia)]
    other = [swap(each, "ja", n_ja, 1) for each in sent]
    core_near, rows_total, depth_total, cols_total = unpack(
        sizes, rank, [each.astype(f32) for each in sent], None, rows_total, depth_total
    )
    (core_total,) = unpack(sizes, rank, [each.astype(f32) for each in other], core_near)
    return (rows_total, cols_total, depth_total, core_total)


def solution(mesh):
    in_specs = (
        P("ia", "ja", "ka", None, None, None),
        P("ia", "ja", "ka", None, None, None),
        P("ia", "ja", "ka", None),
        P("ia", "ja", "ka"),
        P(None, ("ia", "ja", "ka")),
        P(None, ("ja", "ka")),
        P(),
        P(),
    )
    out_specs = (P(None, ("ia", "ja", "ka")), P(None, ("ja", "ka")), P(None, "ka"), P())
    return jax.shard_map(
        functools.partial(on_device, dict(mesh.shape)),
        mesh=mesh,
        in_specs=in_specs,
        out_specs=out_specs,
        check_vma=False,
    )
```
